128 devices in a mesh: dp: 8 (over x, core), seq: 16 (over z, y).
Axes of the slice: x: 4, y: 4, z: 4, core: 2. Of those that a mesh axis runs over, the one named last changes fastest.
Arguments:
- tokens: bfloat16 [16, 4096, 1024], P('dp', 'seq'), may hold values from -8 to 8
- lengths: int32 [16], P('dp'), may hold values from 1 to 4096, as said below
- cotangent: bfloat16 [16, 4096, 1024], P('dp', 'seq'), may hold values from -6 to 6
- norm_gain: bfloat16 [1024], replicated, may hold values from 0.5 to 1.5
- in_weight: bfloat16 [1024, 3072], replicated, may hold values from -0.1875 to 0.1875
- gate_down: bfloat16 [1024, 16], replicated, may hold values from -0.1875 to 0.1875
- gate_up: bfloat16 [512, 16], replicated, may hold values from -1.5 to 1.5
- gate_bias: bfloat16 [512], replicated, may hold values from 0.5 to 6
- head_gain: bfloat16 [256], replicated, may hold values from 0.5 to 1.5
- out_weight: bfloat16 [1024, 1024], replicated, may hold values from -0.1875 to 0.1875
- mlp_gain: bfloat16 [1024], replicated, may hold values from 0.5 to 1.5
- up_weight: bfloat16 [1024, 5632], replicated, may hold values from -0.1875 to 0.1875
- down_weight: bfloat16 [2816, 1024], replicated, may hold values from -0.109375 to 0.109375
Outputs:
- output: bfloat16 [16, 4096, 1024], P('dp', 'seq')
- input_grad: bfloat16 [16, 4096, 1024], P('dp', 'seq')
- grad_norm_gain: float32 [1024], P('seq')
- grad_in_weight: float32 [1024, 3072], P('seq')
- grad_gate_down: float32 [1024, 16], P('seq')
- grad_gate_up: float32 [512, 16], P('seq')
- grad_gate_bias: float32 [512], P('seq')
- grad_head_gain: float32 [256], P('seq')
- grad_out_weight: float32 [1024, 1024], P('seq')
- grad_mlp_gain: float32 [1024], P('seq')
- grad_up_weight: float32 [1024, 5632], P('seq')
- grad_down_weight: float32 [2816, 1024], P('seq')
The draws below stay inside these ranges and needn't reach their ends.
Inputs may be any that keep to these rules, and one draw needn't show every extreme that they name: Row r is live in its first lengths[r] of 4096 slots; of the 2 rows on each index of dp, one is live in all 4096.
All inputs are finite; a program needn't handle non-finite values.
Results may differ from the reference program's by a relative error of at most 0.012.
The reference program's roundings to bfloat16 on the way count: a program that leaves them out, or rounds other values in their place, can miss the bound.
Values sent between devices are 32-bit elements; how exact they have to be, the bound alone decides.
No kernel may reach another device: no remote copies, remote signals or barrier semaphores. Data moves between devices by JAX's collectives and lax.ppermute only.
A program may use at most 320 MiB of HBM per device.

```python
import jax
import jax.numpy as jnp
from jax import lax

D = 1024
FF = 2816
HEADS = 4
KHEAD = 128
VHEAD = 256
RANK = 16
BLOCK = 64
ROWS_DP = 2
KD = 512
VALUE = 1024
BUCKET = 4096
ROWS = 16


def draw_lengths(key, part):
    key = jax.random.fold_in(key, 7)
    first_key, second_key, pick_key = jax.random.split(key, 3)
    first_draw = jax.random.randint(first_key, (ROWS,), 1, BUCKET + 1)
    second_draw = jax.random.randint(second_key, (ROWS,), 1, BUCKET + 1)
    chosen = jax.random.randint(pick_key, (ROWS // ROWS_DP,), 0, ROWS_DP)
    row_slot = jnp.arange(ROWS, dtype=jnp.int32) % ROWS_DP
    full_row = row_slot == jnp.repeat(chosen, ROWS_DP)
    return jnp.where(full_row, BUCKET, jnp.minimum(first_draw, second_draw)).astype(jnp.int32)


def spiked(drawn, rng, source, target, shards_of, factor):
    owner, partner = [(jnp.arange(drawn.shape[position]) // (drawn.shape[position] // shards_of)).reshape([-1 if axis == position else 1 for axis in range(drawn.ndim)]) for position in (source, target)]
    chosen = jax.random.permutation(rng, shards_of)[partner]
    strong = (owner == chosen) | (owner == (partner + shards_of // 2) % shards_of)
    return jnp.where(strong, factor * drawn, drawn)


def block_levels(rng, dims, cuts, low, largest):
    def one(position, parts):
        draws = jax.random.uniform(jax.random.fold_in(jax.random.fold_in(rng, 6), position), (parts,), jnp.float32, low / len(cuts), largest / len(cuts))
        return jnp.repeat(jnp.exp(draws), dims[position] // parts).reshape((-1,) + (1,) * (len(dims) - position - 1))

    loudness = one(*cuts[0])
    for cut in cuts[1:]:
        loudness = loudness * one(*cut)
    return loudness


def gaussian(own_key, extent, width, limit, cuts=(), kind=jnp.bfloat16):
    values = width * jax.random.normal(own_key, extent, jnp.float32)
    if cuts:
        values = values * block_levels(own_key, extent, cuts, -0.22, 0.18)
    return jnp.clip(values, -limit, limit).astype(kind)


def noise_with(stream_key, dims, scale, bound, cuts, heavy, kind=jnp.bfloat16):
    entries = scale * jax.random.normal(stream_key, dims, jnp.float32)
    if cuts:
        entries = entries * block_levels(stream_key, dims, cuts, -0.22, 0.18)
    return jnp.clip(spiked(entries, jax.random.fold_in(stream_key, 3), *heavy), -bound, bound).astype(kind)


def setup_inputs(seed: int = 0) -> dict:
    seeds = jax.random.split(jax.random.key(seed), 14)
    return {
        "tokens": noise_with(seeds[0], (ROWS, BUCKET, D), 1.0, 8.0, ((0, 8), (1, 16)), (1, 2, 16, 2.0)),
        "lengths": draw_lengths(jax.random.fold_in(seeds[13], 71), 0),
        "cotangent": gaussian(seeds[2], (ROWS, BUCKET, D), 1.0, 6.0, ((0, 8), (1, 16))),
        "norm_gain": jnp.clip(1.0 + 0.1 * jax.random.normal(seeds[3], (D,), jnp.float32), 0.5, 1.5).astype(jnp.bfloat16),
        "in_weight": gaussian(seeds[4], (D, 2 * KD + 2 * VALUE), D ** -0.5, 0.1875),
        "gate_down": gaussian(seeds[5], (D, RANK), D ** -0.5, 0.1875),
        "gate_up": gaussian(seeds[6], (KD, RANK), RANK ** -0.5, 1.5),
        "gate_bias": jnp.clip(jax.random.uniform(seeds[7], (KD,), jnp.float32, 0.5, 6.0), 0.5, 6.0).astype(jnp.bfloat16),
        "head_gain": jnp.clip(1.0 + 0.1 * jax.random.normal(seeds[8], (VHEAD,), jnp.float32), 0.5, 1.5).astype(jnp.bfloat16),
        "out_weight": gaussian(seeds[9], (VALUE, D), VALUE ** -0.5, 0.1875),
        "mlp_gain": jnp.clip(1.0 + 0.1 * jax.random.normal(seeds[10], (D,), jnp.float32), 0.5, 1.5).astype(jnp.bfloat16),
        "up_weight": gaussian(seeds[11], (D, 2 * FF), D ** -0.5, 0.1875),
        "down_weight": gaussian(seeds[12], (FF, D), FF ** -0.5, 0.109375),
    }


@jax.custom_vjp
def low(v):
    return lax.optimization_barrier(v.astype(jnp.bfloat16)).astype(jnp.float32)

@jax.custom_vjp
def low_back(v):
    return v

def low_keep(v):
    return (low(v), None)

def low_pass(kept, grad):
    return (grad,)

def back_keep(v):
    return (v, None)

def back_low(kept, grad):
    return (low(grad),)
low.defvjp(low_keep, low_pass)
low_back.defvjp(back_keep, back_low)
EPSILON = 1e-06

def exact_product(subscripts, left_side, right_side):
    return jnp.einsum(subscripts, left_side, right_side, precision=lax.Precision.HIGHEST)

def rms_scale(values_in, gain_vector):
    return values_in * lax.rsqrt(lax.optimization_barrier(jnp.mean(values_in * values_in, -1, keepdims=True)) + EPSILON) * gain_vector

def block_step(state, pieces):
    queries, key_rows, value_rows, log_gate = pieces
    log_decay = jnp.cumsum(log_gate, axis=1)
    closing = log_decay[:, -1]
    causal_mask = jnp.tril(jnp.ones((BLOCK, BLOCK), jnp.float32))
    query_scaled = queries * jnp.exp(log_decay)
    key_scaled = key_rows * jnp.exp(-log_decay)
    key_closing = key_rows * jnp.exp(closing[:, None] - log_decay)
    scores = exact_product('rihd,rjhd->rhij', query_scaled, key_scaled) * causal_mask
    result = exact_product('rhij,rjhe->rihe', scores, value_rows) + exact_product('rihd,rhde->rihe', query_scaled, state)
    updated = jnp.exp(closing)[..., None] * state + exact_product('rjhd,rjhe->rhde', key_closing, value_rows)
    return (updated, result)

def forward(inputs, norm_gain, in_weight, gate_down, gate_up, gate_bias, head_gain, out_weight, mlp_gain, up_weight, down_weight, live_mask):
    row_count = inputs.shape[0]
    live_col = live_mask[..., None]
    normed = low(rms_scale(inputs, norm_gain))
    projected = low_back(exact_product('rtd,dc->rtc', normed, in_weight))
    low_rank = low_back(exact_product('rtd,dn->rtn', normed, gate_down))
    gate_logit = exact_product('rtn,kn->rtk', low_rank, gate_up) + gate_bias
    log_gate = jax.nn.log_sigmoid(gate_logit) / 16.0 * live_col
    queries = projected[..., :KD] * KHEAD ** (-0.5)
    key_rows = projected[..., KD:2 * KD] * live_col
    value_rows = projected[..., 2 * KD:2 * KD + VALUE] * live_col
    out_gate = projected[..., 2 * KD + VALUE:]

    def blocks(source_array, width_each):
        return source_array.reshape(row_count, BUCKET // BLOCK, BLOCK, HEADS, width_each).transpose(1, 0, 2, 3, 4)
    initial = jnp.zeros((row_count, HEADS, KHEAD, VHEAD), jnp.float32)
    unused, pieces = lax.scan(jax.checkpoint(block_step), initial, (blocks(queries, KHEAD), blocks(key_rows, KHEAD), blocks(value_rows, VHEAD), blocks(log_gate, KHEAD)))
    heads_out = pieces.transpose(1, 0, 2, 3, 4).reshape(row_count, BUCKET, HEADS, VHEAD)
    head_norm = rms_scale(heads_out, head_gain).reshape(row_count, BUCKET, VALUE)
    mixed_heads = low(head_norm * jax.nn.silu(out_gate))
    attended = low_back(exact_product('rtv,vd->rtd', mixed_heads, out_weight))
    middle = inputs + attended
    mlp_in = low(rms_scale(middle, mlp_gain))
    gate_act = low_back(exact_product('rtd,df->rtf', mlp_in, up_weight))
    hidden = low(jax.nn.silu(gate_act[..., :FF]) * gate_act[..., FF:])
    return middle + exact_product('rtf,fd->rtd', hidden, down_weight)

def reference(tokens, lengths, cotangent, norm_gain, in_weight, gate_down, gate_up, gate_bias, head_gain, out_weight, mlp_gain, up_weight, down_weight):
    weights = tuple((weight.astype(jnp.float32) for weight in (norm_gain, in_weight, gate_down, gate_up, gate_bias, head_gain, out_weight, mlp_gain, up_weight, down_weight)))
    positions = jnp.arange(BUCKET, dtype=jnp.int32)
    live_mask = (positions[None, :] < lengths[:, None]).astype(jnp.float32)
    groups = ROWS // ROWS_DP

    def one_group(totals, group_items):
        group_tokens, group_live, group_cot = group_items

        def run_block(inputs, *parameters):
            return forward(inputs, *parameters, group_live)
        result, pullback = jax.vjp(run_block, group_tokens.astype(jnp.float32), *weights)
        gradients = pullback(group_cot.astype(jnp.float32))
        summed = tuple((total_sum + gradient for total_sum, gradient in zip(totals, gradients[1:])))
        return (summed, (result.astype(jnp.bfloat16), gradients[0].astype(jnp.bfloat16)))
    zeros = tuple((jnp.zeros_like(weight) for weight in weights))
    totals, (outputs, input_grads) = lax.scan(one_group, zeros, (tokens.reshape(groups, ROWS_DP, BUCKET, D), live_mask.reshape(groups, ROWS_DP, BUCKET), cotangent.reshape(groups, ROWS_DP, BUCKET, D)))
    return (outputs.reshape(ROWS, BUCKET, D), input_grads.reshape(ROWS, BUCKET, D), totals[0], totals[1], totals[2], totals[3], totals[4], totals[5], totals[6], totals[7], totals[8], totals[9])
```

```python
import functools

import jax
import jax.numpy as jnp
import numpy as np
from jax import lax
from jax.experimental import pallas as pl
from jax.experimental.pallas import tpu as pltpu
from jax.sharding import PartitionSpec as P

F32 = jnp.float32
BF16 = jnp.bfloat16
D = 1024
FF = 2816
HEADS = 4
KHEAD = 128
VHEAD = 256
KD = 512
VALUE = 1024
ROWS = 2
SEG = 256
BLK = 128
N = ROWS * SEG
SEQ = 16
TILE = 256
EPSILON = 1e-06
VMEM_LIMIT = 56 * 1024 * 1024


def params(**kw):
    return pltpu.CompilerParams(vmem_limit_bytes=VMEM_LIMIT, **kw)


def cost(flops, nbytes):
    return pl.CostEstimate(flops=int(flops), bytes_accessed=int(nbytes), transcendentals=0)


def dot(a, b, ca=1, cb=0):
    return lax.dot_general(a, b, (((ca,), (cb,)), ((), ())), preferred_element_type=F32)


def split(a):
    high = a.astype(BF16)
    return high, (a - high.astype(F32)).astype(BF16)


def dot3(a, b, ca=1, cb=0):
    ah, al = split(a)
    bh, bl = split(b)
    return dot(ah, bh, ca, cb) + (dot(ah, bl, ca, cb) + dot(al, bh, ca, cb))


def dot_ones(ones, b, ca=1, cb=0):
    high = b.astype(BF16)
    rest = b - high.astype(F32)
    mid = rest.astype(BF16)
    low = (rest - mid.astype(F32)).astype(BF16)
    return dot(ones, high, ca, cb) + (dot(ones, mid, ca, cb) + dot(ones, low, ca, cb))


def sigmoid(u):
    return 1.0 / (1.0 + jnp.exp(-u))


def inverse_rms(u):
    return lax.rsqrt(jnp.mean(u * u, -1, keepdims=True) + EPSILON)


def live(limit_ref, row, first, count, width):
    where = lax.broadcasted_iota(jnp.int32, (count, width), 0) + first
    return (where < limit_ref[row]).astype(F32)


def lower(shape):
    return lax.broadcasted_iota(jnp.int32, shape, 0) >= lax.broadcasted_iota(jnp.int32, shape, 1)


def proj_kernel(
    limit_ref, tok_ref, gain_ref, w_ref, gd_ref, gu_ref, gb_ref,
    proj_ref, normed_ref, ld_ref, cl_ref, logit_ref, low_ref, upd_ref, out_ref,
    kc_ref,
):
    n = pl.program_id(0)

    @pl.when(n == 0)
    def _():
        inputs = tok_ref[...].astype(F32)
        normed = (inputs * inverse_rms(inputs) * gain_ref[...].astype(F32)).astype(BF16)
        normed_ref[...] = normed
        low = dot(normed, gd_ref[...])
        low_ref[...] = low
        low_high, low_low = split(low)
        logit = dot(low_high, gu_ref[...], 1, 1) + dot(low_low, gu_ref[...], 1, 1)
        logit = logit + gb_ref[...].astype(F32)
        logit_ref[...] = logit
        ones = lower((BLK, BLK)).astype(BF16)
        for row in range(ROWS):
            for part in range(SEG // BLK):
                at = row * SEG + part * BLK
                u = logit[at : at + BLK]
                log_gate = (jnp.minimum(u, 0.0) - jnp.log1p(jnp.exp(-jnp.abs(u)))) * (1.0 / 16.0)
                log_gate = log_gate * live(limit_ref, row, part * BLK, BLK, KD)
                decay = dot_ones(ones, log_gate)
                ld_ref[at : at + BLK] = decay
                m = row * (SEG // BLK) + part
                cl_ref[m : m + 1] = decay[BLK - 1 : BLK]
        cl_ref[4:8] = jnp.zeros((4, KD), F32)

    acc = dot(normed_ref[...], w_ref[...])

    @pl.when(n == 0)
    def _():
        for row in range(ROWS):
            for part in range(SEG // BLK):
                at = row * SEG + part * BLK
                m = row * (SEG // BLK) + part
                key = acc[at : at + BLK] * live(limit_ref, row, part * BLK, BLK, KD)
                proj_ref[at : at + BLK] = key
                kc_ref[at : at + BLK] = key * jnp.exp(cl_ref[m : m + 1] - ld_ref[at : at + BLK])

    for step in (1, 2):

        @pl.when(n == step)
        def _():
            for row in range(ROWS):
                values = []
                for part in range(SEG // BLK):
                    at = row * SEG + part * BLK
                    value = acc[at : at + BLK] * live(limit_ref, row, part * BLK, BLK, KD)
                    proj_ref[at : at + BLK] = value
                    values.append(value)
                for sub in range(2):
                    head = (step - 1) * 2 + sub
                    chan = slice(head * KHEAD, (head + 1) * KHEAD)
                    total = None
                    for part in range(SEG // BLK):
                        at = row * SEG + part * BLK
                        m = row * (SEG // BLK) + part
                        update = dot3(
                            values[part][:, sub * VHEAD : (sub + 1) * VHEAD],
                            kc_ref[at : at + BLK, chan], 0, 0,
                        )
                        upd_ref[row, part, head] = update
                        if total is None:
                            total = update
                        else:
                            total = jnp.exp(cl_ref[m : m + 1, chan]) * total + update
                    base = row * (SEG // BLK)
                    gone = cl_ref[base : base + 1, chan] + cl_ref[base + 1 : base + 2, chan]
                    for half in range(2):
                        piece = (row * HEADS + head) * 2 + half
                        out_ref[piece, 0:128] = total[half * 128 : (half + 1) * 128]
                        out_ref[piece, 128:136] = jnp.broadcast_to(gone, (8, KHEAD))

    @pl.when(n == 3)
    def _():
        proj_ref[...] = acc * KHEAD ** (-0.5)

    @pl.when(n > 3)
    def _():
        proj_ref[...] = acc


def project(limit, tokens, gain, w, gd, gu, gb):
    full = lambda shape: pl.BlockSpec(shape, lambda n, s: (0,) * len(shape))
    column = lambda n, s: (0, jnp.where(n < 3, n + 1, jnp.where(n == 3, 0, n)))
    return pl.pallas_call(
        proj_kernel,
        grid_spec=pltpu.PrefetchScalarGridSpec(
            num_scalar_prefetch=1,
            grid=(6,),
            in_specs=[
                full((N, D)), full((1, D)), pl.BlockSpec((D, KD), column),
                full((D, 16)), full((KD, 16)), full((1, KD)),
            ],
            out_specs=[
                pl.BlockSpec((N, KD), column), full((N, D)), full((N, KD)), full((8, KD)),
                full((N, KD)), full((N, 16)), full((ROWS, 2, HEADS, VHEAD, KHEAD)),
                full((SEQ, 136, KHEAD)),
            ],
            scratch_shapes=[pltpu.VMEM((N, KD), F32)],
        ),
        out_shape=[
            jax.ShapeDtypeStruct((N, 3072), F32), jax.ShapeDtypeStruct((N, D), BF16),
            jax.ShapeDtypeStruct((N, KD), F32), jax.ShapeDtypeStruct((8, KD), F32),
            jax.ShapeDtypeStruct((N, KD), F32), jax.ShapeDtypeStruct((N, 16), F32),
            jax.ShapeDtypeStruct((ROWS, 2, HEADS, VHEAD, KHEAD), F32),
            jax.ShapeDtypeStruct((SEQ, 136, KHEAD), F32),
        ],
        compiler_params=params(),
        cost_estimate=cost(2 * N * D * 3072, 24e6),
        name="project",
    )(limit, tokens, gain, w, gd, gu, gb)


def prefix_kernel(backward, part_ref, decay_ref, out_ref):
    run = jnp.zeros((128, KHEAD), F32)
    order = range(SEQ - 1, -1, -1) if backward else range(SEQ)
    for seg in order:
        out_ref[seg] = run
        run = jnp.exp(decay_ref[seg, 0:1]) * run + part_ref[seg, 0:128]


def prefix(parts, decays, backward):
    return pl.pallas_call(
        functools.partial(prefix_kernel, backward),
        grid=(1,),
        in_specs=[
            pl.BlockSpec((SEQ, 128, KHEAD), lambda n: (0, 0, 0)),
            pl.BlockSpec((SEQ, 8, KHEAD), lambda n: (0, 16, 0)),
        ],
        out_specs=pl.BlockSpec((SEQ, 128, KHEAD), lambda n: (0, 0, 0)),
        out_shape=jax.ShapeDtypeStruct((SEQ, 128, KHEAD), F32),
        compiler_params=params(),
        cost_estimate=cost(1e6, 2.2e6),
        name="prefix",
    )(parts, decays)


def attend_kernel(
    q_ref, k_ref, v_ref, og_ref, ld_ref, cl_ref, inc_ref, upd_ref, tok_ref, ow_ref, hg_ref, mg_ref,
    heads_ref, mixed_ref, middle_ref, mlp_ref, mlpt_ref,
):
    m = pl.program_id(0)
    rows = pl.ds(pl.multiple_of(m * BLK, BLK), BLK)
    mask = lower((BLK, BLK))
    second = lax.rem(m, 2) == 1
    previous = cl_ref[pl.ds(m - lax.rem(m, 2), 1), :]
    gain = hg_ref[...].astype(F32)
    for head in range(HEADS):
        chan = slice(head * KHEAD, (head + 1) * KHEAD)
        vals = slice(head * VHEAD, (head + 1) * VHEAD)
        start = inc_ref[0, head]
        start = jnp.where(second, jnp.exp(previous[:, chan]) * start + upd_ref[0, 0, head], start)
        decay = ld_ref[:, chan]
        centre = decay[BLK // 2 - 1 : BLK // 2]
        query = q_ref[:, chan]
        scores = dot3(query * jnp.exp(decay - centre), k_ref[:, chan] * jnp.exp(centre - decay), 1, 1)
        scores = jnp.where(mask, scores, 0.0)
        out = dot3(scores, v_ref[:, vals]) + dot3(query * jnp.exp(decay), start, 1, 1)
        heads_ref[:, vals] = out
        gate = og_ref[:, vals]
        mixed = out * inverse_rms(out) * gain * (gate * sigmoid(gate))
        mixed_ref[rows, vals] = mixed.astype(BF16)

    @pl.when(m == 3)
    def _():
        for at in range(0, N, 256):
            middle = tok_ref[at : at + 256].astype(F32) + dot(mixed_ref[at : at + 256], ow_ref[...])
            middle_ref[at : at + 256] = middle
            mlp_in = (middle * inverse_rms(middle) * mg_ref[...].astype(F32)).astype(BF16)
            mlp_ref[at : at + 256] = mlp_in
            mlpt_ref[:, at : at + 256] = mlp_in.T


def attend(proj, ld, cl, incoming, upd, tokens, ow, hg, mg):
    full = lambda shape: pl.BlockSpec(shape, lambda m: (0,) * len(shape))
    return pl.pallas_call(
        attend_kernel,
        grid=(4,),
        in_specs=[
            pl.BlockSpec((BLK, KD), lambda m: (m, 0)), pl.BlockSpec((BLK, KD), lambda m: (m, 1)),
            pl.BlockSpec((BLK, VALUE), lambda m: (m, 1)), pl.BlockSpec((BLK, VALUE), lambda m: (m, 2)),
            pl.BlockSpec((BLK, KD), lambda m: (m, 0)), full((8, KD)),
            pl.BlockSpec((1, HEADS, VHEAD, KHEAD), lambda m: (m // 2, 0, 0, 0)),
            pl.BlockSpec((1, 1, HEADS, VHEAD, KHEAD), lambda m: (m // 2, 0, 0, 0, 0)),
            full((N, D)), full((VALUE, D)), full((1, VHEAD)), full((1, D)),
        ],
        out_specs=[
            pl.BlockSpec((BLK, VALUE), lambda m: (m, 0)), full((N, VALUE)), full((N, D)),
            full((N, D)), full((D, N)),
        ],
        out_shape=[
            jax.ShapeDtypeStruct((N, VALUE), F32), jax.ShapeDtypeStruct((N, VALUE), BF16),
            jax.ShapeDtypeStruct((N, D), F32), jax.ShapeDtypeStruct((N, D), BF16),
            jax.ShapeDtypeStruct((D, N), BF16),
        ],
        compiler_params=params(),
        cost_estimate=cost(4e9, 22e6),
        name="attend",
    )(proj, proj, proj, proj, ld, cl, incoming, upd, tokens, ow, hg, mg)


def mlp_kernel(
    first, last, tiles, core_ref, mlp_ref, mlpt_ref, cot_ref, wg_ref, wu_ref, wd_ref, *rest
):
    rest = list(rest)
    if not first:
        acc_in, dacc_in = rest[:2]
        rest = rest[4:]
    if last:
        middle_ref = rest.pop(0)
    out_ref, dmlp_ref, upk_ref, ups_ref, dnk_ref, dns_ref = rest[:6]
    acc_ref, dacc_ref = rest[6:]
    t = pl.program_id(0)
    core = core_ref[0]

    @pl.when(t == 0)
    def _():
        if first:
            acc_ref[...] = jnp.zeros((N, D), F32)
            dacc_ref[...] = jnp.zeros((N, D), F32)
        else:
            acc_ref[...] = acc_in[...]
            dacc_ref[...] = dacc_in[...]

    mlp_in = mlp_ref[...]
    gate = dot(mlp_in, wg_ref[...])
    up = dot(mlp_in, wu_ref[...])
    d_hidden = dot(cot_ref[...], wd_ref[...], 1, 1)
    sig = sigmoid(gate)
    act = gate * sig
    hidden = (act * up).astype(BF16)
    d_gate = (d_hidden * up * (sig * (1.0 + gate * (1.0 - sig)))).astype(BF16)
    d_up = (d_hidden * act).astype(BF16)
    acc_ref[...] += dot(hidden, wd_ref[...])
    dacc_ref[...] += dot(d_gate, wg_ref[...], 1, 1) + dot(d_up, wu_ref[...], 1, 1)
    own = jnp.where(core == 0, d_gate, d_up)
    other = jnp.where(core == 0, d_up, d_gate)
    upk_ref[...] = dot(mlpt_ref[...], own)
    ups_ref[...] = dot(mlpt_ref[...], other)
    hidden_t = hidden.T
    half = D // 2
    dnk_ref[...] = dot(hidden_t, cot_ref[:, pl.ds(pl.multiple_of(core * half, half), half)])
    dns_ref[...] = dot(hidden_t, cot_ref[:, pl.ds(pl.multiple_of((1 - core) * half, half), half)])

    @pl.when(t == tiles - 1)
    def _():
        if last:
            out_ref[...] = (middle_ref[...] + acc_ref[...]).astype(BF16)
        else:
            out_ref[...] = acc_ref[...]
        dmlp_ref[...] = dacc_ref[...]


def mlp(core, mlp_in, mlp_t, cot, upw, dnw, start, tiles, carried, middle):
    first, last = carried is None, middle is not None
    full = lambda shape: pl.BlockSpec(shape, lambda t, c: (0,) * len(shape))
    total = FF // TILE
    operands = [mlp_in, mlp_t, cot, upw, upw, dnw]
    in_specs = [
        full((N, D)), full((D, N)), full((N, D)),
        pl.BlockSpec((D, TILE), lambda t, c: (0, start + t)),
        pl.BlockSpec((D, TILE), lambda t, c: (0, total + start + t)),
        pl.BlockSpec((TILE, D), lambda t, c: (start + t, 0)),
    ]
    aliases = {}
    if not first:
        operands += list(carried)
        in_specs += [full((N, D)), full((N, D))] + [pl.BlockSpec(memory_space=pl.ANY)] * 2
        aliases = {9: 4, 10: 5}
    if last:
        operands += [middle]
        in_specs += [full((N, D))]
    width = tiles * TILE
    return pl.pallas_call(
        functools.partial(mlp_kernel, first, last, tiles),
        grid_spec=pltpu.PrefetchScalarGridSpec(
            num_scalar_prefetch=1,
            grid=(tiles,),
            in_specs=in_specs,
            out_specs=[
                full((N, D)), full((N, D)),
                pl.BlockSpec((D, TILE), lambda t, c: (0, t)), pl.BlockSpec((D, TILE), lambda t, c: (0, t)),
                pl.BlockSpec((TILE, D // 2), lambda t, c: (start + t, 0)),
                pl.BlockSpec((TILE, D // 2), lambda t, c: (start + t, 0)),
            ],
            scratch_shapes=[pltpu.VMEM((N, D), F32), pltpu.VMEM((N, D), F32)],
        ),
        out_shape=[
            jax.ShapeDtypeStruct((N, D), BF16 if last else F32), jax.ShapeDtypeStruct((N, D), F32),
            jax.ShapeDtypeStruct((D, width), F32), jax.ShapeDtypeStruct((D, width), F32),
            jax.ShapeDtypeStruct((FF, D // 2), F32), jax.ShapeDtypeStruct((FF, D // 2), F32),
        ],
        input_output_aliases=aliases,
        compiler_params=params(),
        cost_estimate=cost(2 * 9 * N * D * width, 20e6),
        name="mlp",
    )(core, *operands)


def back_kernel(
    middle_ref, dmlp_ref, cot_ref, mg_ref, ow_ref, hg_ref, heads_ref, og_ref, q_ref, ld_ref, cl_ref,
    dmid_ref, datt_ref, mgg_ref, hgg_ref, dheads_ref, dog_ref, adj_ref, out_ref,
    dmix_ref,
):
    m = pl.program_id(0)

    @pl.when(m == 0)
    def _():
        total = jnp.zeros((1, D), F32)
        for at in range(0, N, 128):
            here = slice(at, at + 128)
            middle = middle_ref[here]
            scale = inverse_rms(middle)
            unit = middle * scale
            grad = dmlp_ref[here]
            total = total + jnp.sum(grad * unit, 0, keepdims=True)
            scaled = grad * mg_ref[...].astype(F32)
            d_middle = scale * (scaled - unit * jnp.mean(scaled * unit, -1, keepdims=True))
            d_middle = d_middle + cot_ref[here].astype(F32)
            dmid_ref[here] = d_middle
            datt_ref[here] = d_middle.astype(BF16)
        mgg_ref[...] = total
        hgg_ref[...] = jnp.zeros((1, VHEAD), F32)
        dmix_ref[...] = dot(datt_ref[...], ow_ref[...], 1, 1)

    block = m + 1 - 2 * lax.rem(m, 2)
    rows = pl.ds(pl.multiple_of(block * BLK, BLK), BLK)
    first = lax.rem(m, 2) == 0
    closing = cl_ref[pl.ds(block, 1), :]
    gain = hg_ref[...].astype(F32)
    for head in range(HEADS):
        chan = slice(head * KHEAD, (head + 1) * KHEAD)
        vals = slice(head * VHEAD, (head + 1) * VHEAD)
        out = heads_ref[:, vals]
        scale = inverse_rms(out)
        unit = out * scale
        gate = og_ref[:, vals]
        sig = sigmoid(gate)
        act = gate * sig
        d_mixed = dmix_ref[rows, vals]
        dog_ref[:, vals] = (d_mixed * (unit * gain) * (sig * (1.0 + gate * (1.0 - sig)))).astype(BF16)
        d_norm = d_mixed * act
        hgg_ref[...] += jnp.sum(d_norm * unit, 0, keepdims=True)
        scaled = d_norm * gain
        d_out = scale * (scaled - unit * jnp.mean(scaled * unit, -1, keepdims=True))
        dheads_ref[:, vals] = d_out
        adjoint = dot3(d_out, q_ref[:, chan] * jnp.exp(ld_ref[:, chan]), 0, 0)

        @pl.when(first)
        def _():
            adj_ref[0, head] = adjoint

        @pl.when(jnp.logical_not(first))
        def _():
            total = jnp.exp(closing[:, chan]) * adj_ref[0, head] + adjoint
            for half in range(2):
                out_ref[head * 2 + half] = total[half * 128 : (half + 1) * 128]


def back(middle, dmlp, cot, mg, ow, hg, heads, proj, ld, cl):
    full = lambda shape: pl.BlockSpec(shape, lambda m: (0,) * len(shape))
    block = lambda m: m + 1 - 2 * lax.rem(m, 2)
    return pl.pallas_call(
        back_kernel,
        grid=(4,),
        in_specs=[
            full((N, D)), full((N, D)), full((N, D)), full((1, D)), full((VALUE, D)), full((1, VHEAD)),
            pl.BlockSpec((BLK, VALUE), lambda m: (block(m), 0)),
            pl.BlockSpec((BLK, VALUE), lambda m: (block(m), 2)),
            pl.BlockSpec((BLK, KD), lambda m: (block(m), 0)),
            pl.BlockSpec((BLK, KD), lambda m: (block(m), 0)),
            full((8, KD)),
        ],
        out_specs=[
            full((N, D)), full((N, D)), full((1, D)), full((1, VHEAD)),
            pl.BlockSpec((BLK, VALUE), lambda m: (block(m), 0)),
            pl.BlockSpec((BLK, VALUE), lambda m: (block(m), 0)),
            pl.BlockSpec((1, HEADS, VHEAD, KHEAD), lambda m: (m // 2, 0, 0, 0)),
            pl.BlockSpec((8, 128, KHEAD), lambda m: (m // 2, 0, 0)),
        ],
        out_shape=[
            jax.ShapeDtypeStruct((N, D), F32), jax.ShapeDtypeStruct((N, D), BF16),
            jax.ShapeDtypeStruct((1, D), F32), jax.ShapeDtypeStruct((1, VHEAD), F32),
            jax.ShapeDtypeStruct((N, VALUE), F32), jax.ShapeDtypeStruct((N, VALUE), BF16),
            jax.ShapeDtypeStruct((ROWS, HEADS, VHEAD, KHEAD), F32),
            jax.ShapeDtypeStruct((SEQ, 128, KHEAD), F32),
        ],
        scratch_shapes=[pltpu.VMEM((N, VALUE), F32)],
        compiler_params=params(),
        cost_estimate=cost(2e9, 24e6),
        name="back",
    )(middle, dmlp, cot, mg, ow, hg, heads, proj, proj, ld, cl)


def inner_kernel(
    limit_ref, q_ref, k_ref, v_ref, dout_ref, ld_ref, cl_ref, inc_ref, ret_ref, upd_ref, adj_ref,
    logit_ref, low_ref, gu_ref,
    dproj_ref, dlow_ref, gb_ref, gup_ref,
    dlg_ref,
):
    m = pl.program_id(0)
    row = m // 2
    part = lax.rem(m, 2)
    second = part == 1

    @pl.when(m == 0)
    def _():
        gb_ref[...] = jnp.zeros((1, KD), F32)
        gup_ref[...] = jnp.zeros((KD, 16), F32)

    mask = lower((BLK, BLK))
    upper = lax.broadcasted_iota(jnp.int32, (BLK, BLK), 0) <= lax.broadcasted_iota(jnp.int32, (BLK, BLK), 1)
    upper = upper.astype(BF16)
    closing = cl_ref[pl.ds(m, 1), :]
    previous = cl_ref[pl.ds(row * 2, 1), :]
    following = cl_ref[pl.ds(row * 2 + 1, 1), :]
    alive = live(limit_ref, row, part * BLK, BLK, VHEAD)
    alive_key = alive[:, :KHEAD]
    for head in range(HEADS):
        chan = slice(head * KHEAD, (head + 1) * KHEAD)
        vals = slice(head * VHEAD, (head + 1) * VHEAD)
        start = inc_ref[0, head]
        start = jnp.where(second, jnp.exp(previous[:, chan]) * start + upd_ref[0, 0, head], start)
        update = jnp.where(second, upd_ref[0, 1, head], upd_ref[0, 0, head])
        end_state = jnp.exp(closing[:, chan]) * start + update
        end_grad = ret_ref[0, head]
        end_grad = jnp.where(second, end_grad, jnp.exp(following[:, chan]) * end_grad + adj_ref[0, head])
        decay = ld_ref[:, chan]
        centre = decay[BLK // 2 - 1 : BLK // 2]
        query = q_ref[:, chan]
        key = k_ref[:, chan]
        value = v_ref[:, vals]
        d_out = dout_ref[:, vals]
        up_factor = jnp.exp(decay - centre)
        down_factor = jnp.exp(centre - decay)
        query_mid = query * up_factor
        key_mid = key * down_factor
        close_factor = jnp.exp(closing[:, chan] - decay)
        scores = jnp.where(mask, dot3(query_mid, key_mid, 1, 1), 0.0)
        d_scores = jnp.where(mask, dot3(d_out, value, 1, 1), 0.0)
        d_query = up_factor * dot3(d_scores, key_mid) + jnp.exp(decay) * dot3(d_out, start)
        d_key = down_factor * dot3(d_scores, query_mid, 0, 0) + close_factor * dot3(value, end_grad)
        d_value = dot3(scores, d_out, 0, 0) + dot3(key * close_factor, end_grad, 1, 1)
        d_decay = query * d_query - key * d_key
        dlg_ref[:, chan] = dot_ones(upper, d_decay) + jnp.sum(end_grad * end_state, 0, keepdims=True)
        dproj_ref[:, chan] = (d_query * KHEAD ** (-0.5)).astype(BF16)
        dproj_ref[:, KD + head * KHEAD : KD + (head + 1) * KHEAD] = (d_key * alive_key).astype(BF16)
        dproj_ref[:, 2 * KD + head * VHEAD : 2 * KD + (head + 1) * VHEAD] = (d_value * alive).astype(BF16)
    alive_gate = live(limit_ref, row, part * BLK, BLK, KD)
    d_logit = dlg_ref[...] * alive_gate * (1.0 / (1.0 + jnp.exp(logit_ref[...]))) * (1.0 / 16.0)
    gb_ref[...] += jnp.sum(d_logit, 0, keepdims=True)
    gup_ref[...] += dot3(d_logit, low_ref[...], 0, 0)
    high, rest = split(d_logit)
    dlow_ref[...] = (dot(high, gu_ref[...]) + dot(rest, gu_ref[...])).astype(BF16)


def inner(limit, proj, dout, ld, cl, incoming, returned, upd, adj, logit, low, gu):
    full = lambda shape: pl.BlockSpec(shape, lambda m, s: (0,) * len(shape))
    by_row = pl.BlockSpec((1, HEADS, VHEAD, KHEAD), lambda m, s: (m // 2, 0, 0, 0))
    return pl.pallas_call(
        inner_kernel,
        grid_spec=pltpu.PrefetchScalarGridSpec(
            num_scalar_prefetch=1,
            grid=(4,),
            in_specs=[
                pl.BlockSpec((BLK, KD), lambda m, s: (m, 0)), pl.BlockSpec((BLK, KD), lambda m, s: (m, 1)),
                pl.BlockSpec((BLK, VALUE), lambda m, s: (m, 1)), pl.BlockSpec((BLK, VALUE), lambda m, s: (m, 0)),
                pl.BlockSpec((BLK, KD), lambda m, s: (m, 0)), full((8, KD)),
                by_row, by_row,
                pl.BlockSpec((1, 2, HEADS, VHEAD, KHEAD), lambda m, s: (m // 2, 0, 0, 0, 0)),
                by_row,
                pl.BlockSpec((BLK, KD), lambda m, s: (m, 0)), pl.BlockSpec((BLK, 16), lambda m, s: (m, 0)),
                full((KD, 16)),
            ],
            out_specs=[
                pl.BlockSpec((BLK, 2048), lambda m, s: (m, 0)), pl.BlockSpec((BLK, 16), lambda m, s: (m, 0)),
                full((1, KD)), full((KD, 16)),
            ],
            scratch_shapes=[pltpu.VMEM((BLK, KD), F32)],
        ),
        out_shape=[
            jax.ShapeDtypeStruct((N, 2048), BF16), jax.ShapeDtypeStruct((N, 16), BF16),
            jax.ShapeDtypeStruct((1, KD), F32), jax.ShapeDtypeStruct((KD, 16), F32),
        ],
        compiler_params=params(),
        cost_estimate=cost(5e9, 20e6),
        name="inner",
    )(limit, proj, proj, proj, dout, ld, cl, incoming, returned, upd, adj, logit, low, gu)


def outer_kernel(tiles, width, core_ref, x_ref, y_ref, keep_ref, send_ref, xt_ref):
    t = pl.program_id(0)

    @pl.when(t == 0)
    def _():
        xt_ref[...] = x_ref[...].T

    value = dot(xt_ref[...], y_ref[...])

    @pl.when(t < tiles // 2)
    def _():
        send_ref[...] = value

    @pl.when(t >= tiles // 2)
    def _():
        keep_ref[...] = value


def outer(core, x, y, width):
    features = x.shape[1]
    tiles = y.shape[1] // width
    half = tiles // 2

    def source(t, c):
        return (0, jnp.where(t < half, (1 - c[0]) * half + t, c[0] * half + t - half))

    return pl.pallas_call(
        functools.partial(outer_kernel, tiles, width),
        grid_spec=pltpu.PrefetchScalarGridSpec(
            num_scalar_prefetch=1,
            grid=(tiles,),
            in_specs=[
                pl.BlockSpec((N, features), lambda t, c: (0, 0)), pl.BlockSpec((N, width), source),
            ],
            out_specs=[
                pl.BlockSpec((features, width), lambda t, c: (0, jnp.maximum(t - half, 0))),
                pl.BlockSpec((features, width), lambda t, c: (0, jnp.minimum(t, half - 1))),
            ],
            scratch_shapes=[pltpu.VMEM((features, N), BF16)],
        ),
        out_shape=[jax.ShapeDtypeStruct((features, width * half), F32)] * 2,
        compiler_params=params(),
        cost_estimate=cost(2 * N * features * y.shape[1], 4 * features * y.shape[1]),
        name="outer",
    )(core, x, y)


def input_kernel(
    y_ref, og_ref, w_ref, dlow_ref, gd_ref, tok_ref, gain_ref, dmid_ref, normed_ref,
    grad_ref, ngg_ref, gdg_ref, acc_ref,
):
    t = pl.program_id(0)

    @pl.when(t == 0)
    def _():
        acc_ref[...] = dot(dlow_ref[...], gd_ref[...], 1, 1)
        gdg_ref[...] = dot(normed_ref[...], dlow_ref[...], 0, 0)

    @pl.when(t < 4)
    def _():
        acc_ref[...] += dot(y_ref[...], w_ref[...], 1, 1)

    @pl.when(t >= 4)
    def _():
        acc_ref[...] += dot(og_ref[...], w_ref[...], 1, 1)

    @pl.when(t == 5)
    def _():
        total = jnp.zeros((1, D), F32)
        for at in range(0, N, 128):
            here = slice(at, at + 128)
            inputs = tok_ref[here].astype(F32)
            scale = inverse_rms(inputs)
            unit = inputs * scale
            grad = acc_ref[here]
            total = total + jnp.sum(grad * unit, 0, keepdims=True)
            scaled = grad * gain_ref[...].astype(F32)
            d_inputs = scale * (scaled - unit * jnp.mean(scaled * unit, -1, keepdims=True))
            grad_ref[here] = (dmid_ref[here] + d_inputs).astype(BF16)
        ngg_ref[...] = total


def input_back(y, og, w, dlow, gd, tokens, gain, dmid, normed):
    full = lambda shape: pl.BlockSpec(shape, lambda t: (0,) * len(shape))
    return pl.pallas_call(
        input_kernel,
        grid=(6,),
        in_specs=[
            pl.BlockSpec((N, 512), lambda t: (0, jnp.minimum(t, 3))),
            pl.BlockSpec((N, 512), lambda t: (0, jnp.maximum(t - 4, 0))),
            pl.BlockSpec((D, 512), lambda t: (0, t)),
            full((N, 16)), full((D, 16)), full((N, D)), full((1, D)), full((N, D)), full((N, D)),
        ],
        out_specs=[full((N, D)), full((1, D)), full((D, 16))],
        out_shape=[
            jax.ShapeDtypeStruct((N, D), BF16), jax.ShapeDtypeStruct((1, D), F32),
            jax.ShapeDtypeStruct((D, 16), F32),
        ],
        scratch_shapes=[pltpu.VMEM((N, D), F32)],
        compiler_params=params(),
        cost_estimate=cost(2 * N * D * 3072, 16e6),
        name="input_back",
    )(y, og, w, dlow, gd, tokens, gain, dmid, normed)


SWAP = [(i, i ^ 1) for i in range(8)]
FLIP = {0: 1, 1: 3}
ORDERS = (((0, 1, 2, 3), (1, 0, 3, 2)), ((2, 3, 0, 1), (3, 2, 1, 0)))


def bit_of(seq, which):
    at = seq // 4 if which < 2 else seq % 4
    return at // 2 if which % 2 else int(at in (1, 2))


def chunk_of(order, bits):
    value = dict(zip(order, bits))
    along = [[0, 1, 3, 2][2 * value[2 * a + 1] + value[2 * a]] for a in range(2)]
    return along[0] * 4 + along[1]


def partner(seq, which):
    z, y = seq // 4, seq % 4
    return (z ^ FLIP[which]) * 4 + y if which < 2 else z * 4 + (y ^ FLIP[which - 2])


def tables():
    table = np.zeros((128, 64), np.int32)
    for device in range(128):
        core, seq = (device // 16) % 2, device % 16
        for v in range(2):
            order = ORDERS[v][core]
            chunks = [chunk_of(order, [(i >> 3) & 1, (i >> 2) & 1, (i >> 1) & 1, i & 1]) for i in range(16)]
            mine = [bit_of(seq, which) for which in order]
            table[device, v * 16 : v * 16 + 8] = chunks[mine[0] * 8 : mine[0] * 8 + 8]
            table[device, v * 16 + 8 : v * 16 + 16] = chunks[(1 - mine[0]) * 8 : (1 - mine[0]) * 8 + 8]
            table[device, 32 + v * 4 : 36 + v * 4] = mine
        table[device, 40] = core
    return table


TABLE = tables()
STEPS = [
    [
        [(d, (d // 16) * 16 + partner(d % 16, ORDERS[v][(d // 16) % 2][step])) for d in range(128)]
        for step in range(4)
    ]
    for v in range(2)
]
ACROSS = [
    [(i, ((i // 2) ^ FLIP[(i % 2 + step) % 2]) * 2 + i % 2) for i in range(8)] for step in range(2)
]


def exchange(value):
    return lax.all_to_all(value, "seq", 0, 0, tiled=True)


def swap(value):
    return lax.ppermute(value, "dp", SWAP)


def first_kernel(shapes, table_ref, *refs):
    del table_ref
    count = sum(4 if paired else 2 for _, _, paired in shapes)
    ins, (send_ref, keep_ref) = list(refs[:count]), refs[count:]
    for out_ref, skip in ((keep_ref, 0), (send_ref, 1)):
        at, used = 0, 0
        for rows, slabs, paired in shapes:
            value = ins[used + skip][0]
            if paired:
                value = value + ins[used + 2 + skip][0]
            for slab in range(slabs):
                out_ref[0, at : at + rows] = value[:, slab * 128 : (slab + 1) * 128]
                at += rows
            used += 4 if paired else 2


def first_halving(v, table, pieces):
    operands, specs, shapes, total = [], [], [], 0
    for array, other, block, width in pieces:
        rows = array.shape[1]
        for source in (array, other):
            if source is None:
                continue
            for skip in (0, 8):
                operands.append(source)
                specs.append(
                    pl.BlockSpec(
                        (1, rows, width), lambda i, t, b=block, k=v * 16 + skip: (t[k + i], 0, b)
                    )
                )
        shapes.append((rows, width // 128, other is not None))
        total += rows * (width // 128)
    out = pl.BlockSpec((1, total, 128), lambda i, t: (i, 0, 0))
    return pl.pallas_call(
        functools.partial(first_kernel, shapes),
        grid_spec=pltpu.PrefetchScalarGridSpec(
            num_scalar_prefetch=1, grid=(8,), in_specs=specs, out_specs=[out, out]
        ),
        out_shape=[jax.ShapeDtypeStruct((8, total, 128), F32)] * 2,
        compiler_params=params(),
        cost_estimate=cost(0, 6 * 8 * total * 512),
        name="halve_first",
    )(table, *operands)


def next_kernel(table_ref, ks_ref, kk_ref, rs_ref, rk_ref, send_ref, keep_ref):
    del table_ref
    send_ref[...] = ks_ref[...] + rs_ref[...]
    keep_ref[...] = kk_ref[...] + rk_ref[...]


def next_halving(v, step, table, keep, got):
    half, total = keep.shape[0] // 2, keep.shape[1]
    slot = 32 + v * 4 + step
    mine = pl.BlockSpec((1, total, 128), lambda i, t: (t[slot] * half + i, 0, 0))
    theirs = pl.BlockSpec((1, total, 128), lambda i, t: ((1 - t[slot]) * half + i, 0, 0))
    out = pl.BlockSpec((1, total, 128), lambda i, t: (i, 0, 0))
    return pl.pallas_call(
        next_kernel,
        grid_spec=pltpu.PrefetchScalarGridSpec(
            num_scalar_prefetch=1, grid=(half,), in_specs=[theirs, mine, theirs, mine], out_specs=[out, out]
        ),
        out_shape=[jax.ShapeDtypeStruct((half, total, 128), F32)] * 2,
        compiler_params=params(),
        cost_estimate=cost(0, 6 * half * total * 512),
        name="halve_next",
    )(table, keep, keep, got, got)


def hop(v, step, value):
    return lax.ppermute(value, ("dp", "seq"), STEPS[v][step])


def scatter(v, table, pieces):
    send, keep = first_halving(v, table, pieces)
    got = hop(v, 0, send)
    for step in range(1, 4):
        send, keep = next_halving(v, step, table, keep, got)
        got = hop(v, step, send)
    return (keep + got)[0]


def across(value):
    value = value + lax.ppermute(value, "dp", ACROSS[0])
    return value + lax.ppermute(value, "dp", ACROSS[1])


def unpack_kernel(core_ref, a_ref, a_other, b_ref, b_other, up_ref, down_ref, out_ref, in_ref, small_ref):
    core = core_ref[0]

    def place(own_ref, other_ref, at, rows, slabs, target, first, second):
        for slab in range(slabs):
            own = own_ref[at : at + rows]
            other = other_ref[at : at + rows]
            low = jnp.where(core == 0, own, other)
            high = jnp.where(core == 0, other, own)
            target[:, first + slab * 128 : first + (slab + 1) * 128] = low
            target[:, second + slab * 128 : second + (slab + 1) * 128] = high
            at += rows
        return at

    at = place(a_ref, a_other, 0, 64, 8, up_ref, 0, FF)
    at = place(a_ref, a_other, at, 64, 8, up_ref, 1024, FF + 1024)
    for v in range(2):
        at = place(a_ref, a_other, at, 64, 3, up_ref, 2048 + v * 384, FF + 2048 + v * 384)
        at = place(a_ref, a_other, at, 176, 2, down_ref, v * 256, 512 + v * 256)
    at = place(a_ref, a_other, at, 64, 4, out_ref, 0, 512)
    at = place(a_ref, a_other, at, 64, 4, in_ref, 2048, 2560)
    at = place(b_ref, b_other, 0, 64, 4, in_ref, 0, 1024)
    at = place(b_ref, b_other, at, 64, 4, in_ref, 512, 1536)
    small_ref[...] = b_ref[at : at + 16] + b_other[at : at + 16]


def unpack(core, a, a_other, b, b_other):
    return pl.pallas_call(
        unpack_kernel,
        in_specs=[pl.BlockSpec(memory_space=pltpu.SMEM)] + [pl.BlockSpec(memory_space=pltpu.VMEM)] * 4,
        out_specs=[pl.BlockSpec(memory_space=pltpu.VMEM)] * 5,
        out_shape=[
            jax.ShapeDtypeStruct((64, 2 * FF), F32), jax.ShapeDtypeStruct((176, D), F32),
            jax.ShapeDtypeStruct((64, D), F32), jax.ShapeDtypeStruct((64, 3072), F32),
            jax.ShapeDtypeStruct((16, 128), F32),
        ],
        compiler_params=params(),
        cost_estimate=cost(0, 7e6),
        name="unpack",
    )(core, a, a_other, b, b_other)


def chunks(value):
    return value.reshape(SEQ, value.shape[0] // SEQ, value.shape[1])


def shards(
    tokens, lengths, cotangent, norm_gain, in_weight, gate_down, gate_up, gate_bias, head_gain,
    out_weight, mlp_gain, up_weight, down_weight,
):
    place = lax.axis_index("seq")
    device = lax.axis_index("dp") * SEQ + place
    table = lax.dynamic_slice(jnp.asarray(TABLE), (device, 0), (1, 64)).reshape(64)
    core_arg = table[40:41]
    limit = lengths - (place * SEG).astype(jnp.int32)
    tok = tokens.reshape(N, D)
    cot = cotangent.reshape(N, D)
    line = lambda vector: vector.reshape(1, -1)

    proj, normed, ld, cl, logit, low, upd, pieces = project(
        limit, tok, line(norm_gain), in_weight, gate_down, gate_up, line(gate_bias)
    )
    gathered = exchange(pieces)
    incoming = exchange(prefix(gathered, gathered, False)).reshape(ROWS, HEADS, VHEAD, KHEAD)
    heads, mixed, middle, mlp_in, mlp_t = attend(
        proj, ld, cl, incoming, upd, tok, out_weight, line(head_gain), line(mlp_gain)
    )
    weights = (core_arg, mlp_in, mlp_t, cot, up_weight, down_weight)
    acc, dmlp, keep_a, send_a, dn_keep, dn_send = mlp(*weights, 0, 4, None, None)
    acc, dmlp, keep_b, send_b, dn_keep, dn_send = mlp(*weights, 4, 4, (acc, dmlp, dn_keep, dn_send), None)
    output, dmlp, keep_c, send_c, dn_keep, dn_send = mlp(
        *weights, 8, 3, (acc, dmlp, dn_keep, dn_send), middle
    )
    one = scatter(0, table, [(chunks(keep_a), chunks(swap(send_a)), 0, 1024)])
    two = scatter(1, table, [(chunks(keep_b), chunks(swap(send_b)), 0, 1024)])
    got_c, got_dn = chunks(swap(send_c)), chunks(swap(dn_send))
    three = [
        scatter(v, table, [(chunks(keep_c), got_c, v, 384), (chunks(dn_keep), got_dn, v, 256)])
        for v in range(2)
    ]
    dmid, datt, g_mlp_gain, g_head_gain, dheads, dog, adj, pieces_back = back(
        middle, dmlp, cot, line(mlp_gain), out_weight, line(head_gain), heads, proj, ld, cl
    )
    keep_o, send_o = outer(core_arg, mixed, datt, 256)
    keep_g, send_g = outer(core_arg, normed, dog, 512)
    four = [
        scatter(0, table, [(chunks(keep_o), chunks(swap(send_o)), 0, 512)]),
        scatter(1, table, [(chunks(keep_g), chunks(swap(send_g)), 0, 512)]),
    ]
    returned = exchange(prefix(exchange(pieces_back), gathered, True)).reshape(ROWS, HEADS, VHEAD, KHEAD)
    dproj, dlow, g_gate_bias, g_gate_up = inner(
        limit, proj, dheads, ld, cl, incoming, returned, upd, adj, logit, low, gate_up
    )
    keep_p, send_p = outer(core_arg, normed, dproj, 512)
    got_p = chunks(swap(send_p))
    input_grad, g_norm_gain, g_gate_down = input_back(
        dproj, dog, in_weight, dlow, gate_down, tok, line(norm_gain), dmid, normed
    )
    pack = jnp.concatenate(
        [
            g_norm_gain.reshape(SEQ, 64), g_gate_down.reshape(SEQ, 1024), g_gate_up.reshape(SEQ, 512),
            g_gate_bias.reshape(SEQ, 32), g_head_gain.reshape(SEQ, 16), g_mlp_gain.reshape(SEQ, 64),
            jnp.zeros((SEQ, 336), F32),
        ],
        1,
    ).reshape(SEQ, 16, 128)
    five = [
        scatter(0, table, [(chunks(keep_p), got_p, 0, 512)]),
        scatter(1, table, [(chunks(keep_p), got_p, 1, 512), (pack, None, 0, 128)]),
    ]
    early = across(jnp.concatenate([one, two, *three, *four], 0))
    late = across(jnp.concatenate(five, 0))
    grad_up, grad_down, grad_out, grad_in, small = unpack(core_arg, early, swap(early), late, swap(late))
    small = small.reshape(2048)
    return (
        output.reshape(ROWS, SEG, D),
        input_grad.reshape(ROWS, SEG, D),
        small[:64],
        grad_in,
        small[64:1088].reshape(64, 16),
        small[1088:1600].reshape(32, 16),
        small[1600:1632],
        small[1632:1648],
        grad_out,
        small[1648:1712],
        grad_up,
        grad_down,
    )


def solution(mesh):
    rows = P("dp", "seq", None)
    return jax.shard_map(
        shards,
        mesh=mesh,
        in_specs=(rows, P("dp"), rows) + (P(),) * 10,
        out_specs=(
            rows, rows, P("seq"), P("seq", None), P("seq", None), P("seq", None), P("seq"), P("seq"),
            P("seq", None), P("seq"), P("seq", None), P("seq", None),
        ),
        check_vma=False,
    )
```

```python
import functools

import jax
import jax.numpy as jnp
import numpy as np
from jax import lax
from jax.experimental import pallas as pl
from jax.experimental.pallas import tpu as pltpu
from jax.sharding import PartitionSpec as P

F32 = jnp.float32
BF16 = jnp.bfloat16
D = 1024
FF = 2816
HEADS = 4
KHEAD = 128
VHEAD = 256
KD = 512
VALUE = 1024
ROWS = 2
SEG = 256
BLK = 128
N = ROWS * SEG
SEQ = 16
TILE = 256
EPSILON = 1e-06
VMEM_LIMIT = 62 * 1024 * 1024


def params(**kw):
    return pltpu.CompilerParams(vmem_limit_bytes=VMEM_LIMIT, **kw)


def cost(us):
    return pl.CostEstimate(flops=0, bytes_accessed=int(us * 3e6), transcendentals=0)


def dot(a, b, ca=1, cb=0):
    return lax.dot_general(a, b, (((ca,), (cb,)), ((), ())), preferred_element_type=F32)


def split(a):
    high = a.astype(BF16)
    return high, (a - high.astype(F32)).astype(BF16)


def dot3(a, b, ca=1, cb=0):
    ah, al = split(a)
    bh, bl = split(b)
    return dot(ah, bh, ca, cb) + (dot(ah, bl, ca, cb) + dot(al, bh, ca, cb))


def dot_ones(ones, b, ca=1, cb=0):
    high = b.astype(BF16)
    rest = b - high.astype(F32)
    mid = rest.astype(BF16)
    low = (rest - mid.astype(F32)).astype(BF16)
    return dot(ones, high, ca, cb) + (dot(ones, mid, ca, cb) + dot(ones, low, ca, cb))


def sigmoid(u):
    return 1.0 / (1.0 + jnp.exp(-u))


def inverse_rms(u):
    return lax.rsqrt(jnp.mean(u * u, -1, keepdims=True) + EPSILON)


def live(lengths_ref, table_ref, row, first, count, width):
    where = lax.broadcasted_iota(jnp.int32, (count, width), 0) + (first + table_ref[46] * SEG)
    return (where < lengths_ref[row]).astype(F32)


def lower(shape):
    return lax.broadcasted_iota(jnp.int32, shape, 0) >= lax.broadcasted_iota(jnp.int32, shape, 1)


def proj_kernel(
    limit_ref, core_ref, tok_ref, cot_ref, gain_ref, w_ref, gd_ref, gu_ref, gb_ref,
    proj_ref, normed_ref, normt_ref, cots_ref, ld_ref, cl_ref, logit_ref, low_ref, upd_ref, out_ref,
    kc_ref,
):
    n = pl.program_id(0)

    @pl.when(n == 0)
    def _():
        inputs = tok_ref[...].astype(F32)
        normed = (inputs * inverse_rms(inputs) * gain_ref[...].astype(F32)).astype(BF16)
        normed_ref[...] = normed
        low = dot(normed, gd_ref[...], 1, 1)
        low_ref[...] = low
        low_high, low_low = split(low)
        logit = dot(low_high, gu_ref[...]) + dot(low_low, gu_ref[...])
        logit = logit + gb_ref[...].astype(F32)
        logit_ref[...] = logit
        ones = lower((BLK, BLK)).astype(BF16)
        for row in range(ROWS):
            for part in range(SEG // BLK):
                at = row * SEG + part * BLK
                u = logit[at : at + BLK]
                log_gate = (jnp.minimum(u, 0.0) - jnp.log1p(jnp.exp(-jnp.abs(u)))) * (1.0 / 16.0)
                log_gate = log_gate * live(limit_ref, core_ref, row, part * BLK, BLK, KD)
                decay = dot_ones(ones, log_gate)
                ld_ref[at : at + BLK] = decay
                m = row * (SEG // BLK) + part
                cl_ref[m : m + 1] = decay[BLK - 1 : BLK]
        cl_ref[4:8] = jnp.zeros((4, KD), F32)

    acc = dot(normed_ref[...], w_ref[...])

    @pl.when(n == 0)
    def _():
        for row in range(ROWS):
            for part in range(SEG // BLK):
                at = row * SEG + part * BLK
                m = row * (SEG // BLK) + part
                key = acc[at : at + BLK] * live(limit_ref, core_ref, row, part * BLK, BLK, KD)
                proj_ref[at : at + BLK] = key
                kc_ref[at : at + BLK] = key * jnp.exp(cl_ref[m : m + 1] - ld_ref[at : at + BLK])

    for step in (1, 2):

        @pl.when(n == step)
        def _():
            for row in range(ROWS):
                values = []
                for part in range(SEG // BLK):
                    at = row * SEG + part * BLK
                    value = acc[at : at + BLK] * live(limit_ref, core_ref, row, part * BLK, BLK, KD)
                    proj_ref[at : at + BLK] = value
                    values.append(value)
                for sub in range(2):
                    head = (step - 1) * 2 + sub
                    chan = slice(head * KHEAD, (head + 1) * KHEAD)
                    total = None
                    for part in range(SEG // BLK):
                        at = row * SEG + part * BLK
                        m = row * (SEG // BLK) + part
                        update = dot3(
                            values[part][:, sub * VHEAD : (sub + 1) * VHEAD],
                            kc_ref[at : at + BLK, chan], 0, 0,
                        )
                        upd_ref[row, part, head] = update
                        if total is None:
                            total = update
                        else:
                            total = jnp.exp(cl_ref[m : m + 1, chan]) * total + update
                    base = row * (SEG // BLK)
                    gone = cl_ref[base : base + 1, chan] + cl_ref[base + 1 : base + 2, chan]
                    for half in range(2):
                        piece = (row * HEADS + head) * 2 + half
                        out_ref[piece, 0:128] = total[half * 128 : (half + 1) * 128]
                        out_ref[piece, 128:136] = jnp.broadcast_to(gone, (8, KHEAD))

    @pl.when(n == 3)
    def _():
        proj_ref[...] = acc * KHEAD ** (-0.5)

    @pl.when(n > 3)
    def _():
        proj_ref[...] = acc

    @pl.when(n == 4)
    def _():
        normt_ref[...] = normed_ref[...].T.astype(F32)

    @pl.when(n == 5)
    def _():
        cots_ref[...] = cot_ref[:, pl.ds(pl.multiple_of((1 - core_ref[40]) * 512, 512), 512)].astype(F32)


def project(limit, core, tokens, cot, gain, w, gd, gu, gb):
    full = lambda shape: pl.BlockSpec(shape, lambda n, s, c: (0,) * len(shape))
    column = lambda n, s, c: (0, jnp.where(n < 3, n + 1, jnp.where(n == 3, 0, n)))
    return pl.pallas_call(
        proj_kernel,
        grid_spec=pltpu.PrefetchScalarGridSpec(
            num_scalar_prefetch=2,
            grid=(6,),
            in_specs=[
                full((N, D)), full((N, D)), full((1, D)), pl.BlockSpec((D, KD), column),
                full((16, D)), full((16, KD)), full((1, KD)),
            ],
            out_specs=[
                pl.BlockSpec((N, KD), column), full((N, D)), full((D, N)), full((N, KD)),
                full((N, KD)), full((8, KD)),
                full((N, KD)), full((N, 16)), full((ROWS, 2, HEADS, VHEAD, KHEAD)),
                full((SEQ, 136, KHEAD)),
            ],
            scratch_shapes=[pltpu.VMEM((N, KD), F32)],
        ),
        out_shape=[
            jax.ShapeDtypeStruct((N, 3072), F32), jax.ShapeDtypeStruct((N, D), BF16),
            jax.ShapeDtypeStruct((D, N), F32), jax.ShapeDtypeStruct((N, KD), F32),
            jax.ShapeDtypeStruct((N, KD), F32), jax.ShapeDtypeStruct((8, KD), F32),
            jax.ShapeDtypeStruct((N, KD), F32), jax.ShapeDtypeStruct((N, 16), F32),
            jax.ShapeDtypeStruct((ROWS, 2, HEADS, VHEAD, KHEAD), F32),
            jax.ShapeDtypeStruct((SEQ, 136, KHEAD), F32),
        ],
        compiler_params=params(),
        cost_estimate=cost(17),
        name="project",
    )(limit, core, tokens, cot, gain, w, gd, gu, gb)


def prefix_kernel(backward, part_ref, decay_ref, out_ref):
    run = jnp.zeros((128, KHEAD), F32)
    order = range(SEQ - 1, -1, -1) if backward else range(SEQ)
    for seg in order:
        out_ref[seg] = run
        run = jnp.exp(decay_ref[seg, 0:1]) * run + part_ref[seg, 0:128]


def prefix(parts, decays, backward):
    return pl.pallas_call(
        functools.partial(prefix_kernel, backward),
        grid=(1,),
        in_specs=[
            pl.BlockSpec((SEQ, 128, KHEAD), lambda n: (0, 0, 0)),
            pl.BlockSpec((SEQ, 8, KHEAD), lambda n: (0, 16, 0)),
        ],
        out_specs=pl.BlockSpec((SEQ, 128, KHEAD), lambda n: (0, 0, 0)),
        out_shape=jax.ShapeDtypeStruct((SEQ, 128, KHEAD), F32),
        compiler_params=params(),
        cost_estimate=cost(0.1),
        name="prefix",
    )(parts, decays)


def attend_kernel(
    q_ref, k_ref, v_ref, og_ref, ld_ref, cl_ref, inc_ref, upd_ref, tok_ref, ow_ref, hg_ref, mg_ref,
    heads_ref, middle_ref, mlp_ref, both_ref,
    mixed_ref,
):
    m = pl.program_id(0)
    rows = pl.ds(pl.multiple_of(m * BLK, BLK), BLK)
    mask = lower((BLK, BLK))
    second = lax.rem(m, 2) == 1
    previous = cl_ref[pl.ds(m - lax.rem(m, 2), 1), :]
    gain = hg_ref[...].astype(F32)
    for head in range(HEADS):
        chan = slice(head * KHEAD, (head + 1) * KHEAD)
        vals = slice(head * VHEAD, (head + 1) * VHEAD)
        start = inc_ref[0, head]
        start = jnp.where(second, jnp.exp(previous[:, chan]) * start + upd_ref[0, 0, head], start)
        decay = ld_ref[:, chan]
        centre = decay[BLK // 2 - 1 : BLK // 2]
        query = q_ref[:, chan]
        scores = dot3(query * jnp.exp(decay - centre), k_ref[:, chan] * jnp.exp(centre - decay), 1, 1)
        scores = jnp.where(mask, scores, 0.0)
        out = dot3(scores, v_ref[:, vals]) + dot3(query * jnp.exp(decay), start, 1, 1)
        heads_ref[:, vals] = out
        gate = og_ref[:, vals]
        mixed = out * inverse_rms(out) * gain * (gate * sigmoid(gate))
        mixed_ref[rows, vals] = mixed.astype(BF16)

    @pl.when(m == 3)
    def _():
        for at in range(0, N, 256):
            middle = tok_ref[at : at + 256].astype(F32) + dot(mixed_ref[at : at + 256], ow_ref[...])
            middle_ref[at : at + 256] = middle
            mlp_in = (middle * inverse_rms(middle) * mg_ref[...].astype(F32)).astype(BF16)
            mlp_ref[at : at + 256] = mlp_in
            both_ref[:D, at : at + 256] = mlp_in.T.astype(F32)
            both_ref[D:, at : at + 256] = mixed_ref[at : at + 256].T.astype(F32)


def attend(proj, ld, cl, incoming, upd, tokens, ow, hg, mg):
    full = lambda shape: pl.BlockSpec(shape, lambda m: (0,) * len(shape))
    return pl.pallas_call(
        attend_kernel,
        grid=(4,),
        in_specs=[
            pl.BlockSpec((BLK, KD), lambda m: (m, 0)), pl.BlockSpec((BLK, KD), lambda m: (m, 1)),
            pl.BlockSpec((BLK, VALUE), lambda m: (m, 1)), pl.BlockSpec((BLK, VALUE), lambda m: (m, 2)),
            pl.BlockSpec((BLK, KD), lambda m: (m, 0)), full((8, KD)),
            pl.BlockSpec((1, HEADS, VHEAD, KHEAD), lambda m: (m // 2, 0, 0, 0)),
            pl.BlockSpec((1, 1, HEADS, VHEAD, KHEAD), lambda m: (m // 2, 0, 0, 0, 0)),
            full((N, D)), full((VALUE, D)), full((1, VHEAD)), full((1, D)),
        ],
        out_specs=[
            pl.BlockSpec((BLK, VALUE), lambda m: (m, 0)), full((N, D)), full((N, D)), full((D + VALUE, N)),
        ],
        out_shape=[
            jax.ShapeDtypeStruct((N, VALUE), F32), jax.ShapeDtypeStruct((N, D), F32),
            jax.ShapeDtypeStruct((N, D), BF16), jax.ShapeDtypeStruct((D + VALUE, N), F32),
        ],
        scratch_shapes=[pltpu.VMEM((N, VALUE), BF16)],
        compiler_params=params(),
        cost_estimate=cost(13),
        name="attend",
    )(proj, proj, proj, proj, ld, cl, incoming, upd, tokens, ow, hg, mg)


TILES = FF // TILE


def mlp_kernel(
    core_ref, mlp_ref, cot_ref, wg_ref, wu_ref, wd_ref, middle_ref,
    out_ref, dmlp_ref, own_ref, send_ref, hidt_ref, acc_ref,
):
    t = pl.program_id(0)

    @pl.when(t == 0)
    def _():
        acc_ref[...] = middle_ref[...]
        dmlp_ref[...] = jnp.zeros((N, D), F32)

    mlp_in = mlp_ref[...]
    gate = dot(mlp_in, wg_ref[...])
    up = dot(mlp_in, wu_ref[...])
    d_hidden = dot(cot_ref[...], wd_ref[...], 1, 1)
    sig = sigmoid(gate)
    act = gate * sig
    hidden = (act * up).astype(BF16)
    d_gate = (d_hidden * up * (sig * (1.0 + gate * (1.0 - sig)))).astype(BF16)
    d_up = (d_hidden * act).astype(BF16)
    acc_ref[...] += dot(hidden, wd_ref[...])
    dmlp_ref[...] += dot(d_gate, wg_ref[...], 1, 1) + dot(d_up, wu_ref[...], 1, 1)
    first = core_ref[40] == 0
    own_ref[...] = jnp.where(first, d_gate, d_up)
    send_ref[...] = jnp.where(first, d_up, d_gate).astype(F32)
    hidt_ref[...] = hidden.T.astype(F32)

    @pl.when(t == TILES - 1)
    def _():
        out_ref[...] = acc_ref[...].astype(BF16)


def mlp(core, mlp_in, cot, upw, dnw, middle):
    full = lambda shape: pl.BlockSpec(shape, lambda t, c: (0,) * len(shape))
    column = lambda rows: pl.BlockSpec((rows, TILE), lambda t, c: (0, t))
    return pl.pallas_call(
        mlp_kernel,
        grid_spec=pltpu.PrefetchScalarGridSpec(
            num_scalar_prefetch=1,
            grid=(TILES,),
            in_specs=[
                full((N, D)), full((N, D)), column(D),
                pl.BlockSpec((D, TILE), lambda t, c: (0, TILES + t)),
                pl.BlockSpec((TILE, D), lambda t, c: (t, 0)), full((N, D)),
            ],
            out_specs=[
                full((N, D)), full((N, D)), column(N), column(N),
                pl.BlockSpec((TILE, N), lambda t, c: (t, 0)),
            ],
            scratch_shapes=[pltpu.VMEM((N, D), F32)],
        ),
        out_shape=[
            jax.ShapeDtypeStruct((N, D), BF16), jax.ShapeDtypeStruct((N, D), F32),
            jax.ShapeDtypeStruct((N, FF), BF16), jax.ShapeDtypeStruct((N, FF), F32),
            jax.ShapeDtypeStruct((FF, N), F32),
        ],
        compiler_params=params(),
        cost_estimate=cost(30),
        name="mlp",
    )(core, mlp_in, cot, upw, upw, dnw, middle)


def down_grad_kernel(
    table_ref, hid_ref, hid_other, cot_ref, cot_other, keep_ref, send_ref, cotb_ref, hidb_ref
):
    @pl.when(pl.program_id(0) == 0)
    def _():
        cotb_ref[:N] = cot_ref[...]
        cotb_ref[N:] = cot_other[...].astype(BF16)

    hidb_ref[:, :N] = hid_ref[...].reshape(TILE, N).astype(BF16)
    hidb_ref[:, N:] = hid_other[...].reshape(TILE, N).astype(BF16)
    down = dot(hidb_ref[...], cotb_ref[...]).reshape(SEQ, 16, 512)
    for slab in range(4):
        slot = table_ref[41 + slab]

        @pl.when(slot < 2)
        def _():
            keep_ref[slot] = down[:, :, slab * 128 : (slab + 1) * 128]

        @pl.when(slot >= 2)
        def _():
            send_ref[slot - 2] = down[:, :, slab * 128 : (slab + 1) * 128]


def down_grad(table, hid, hid_other, cot, cot_other):
    tall = pl.BlockSpec((SEQ, 16, N), lambda t, c: (0, t, 0))
    out = pl.BlockSpec((2, SEQ, 16, 128), lambda t, c: (0, 0, t, 0))
    return pl.pallas_call(
        down_grad_kernel,
        grid_spec=pltpu.PrefetchScalarGridSpec(
            num_scalar_prefetch=1,
            grid=(TILES,),
            in_specs=[
                tall, tall, pl.BlockSpec((N, 512), lambda t, c: (0, c[40])),
                pl.BlockSpec((N, 512), lambda t, c: (0, 0)),
            ],
            out_specs=[out, out],
            scratch_shapes=[pltpu.VMEM((2 * N, 512), BF16), pltpu.VMEM((TILE, 2 * N), BF16)],
        ),
        out_shape=[jax.ShapeDtypeStruct((2, SEQ, 176, 128), F32)] * 2,
        compiler_params=params(),
        cost_estimate=cost(0.1),
        name="down_grad",
    )(table, chunks(hid), chunks(hid_other), cot, cot_other)


def up_grad_kernel(mlpt_ref, mlpt_other, act_ref, act_other, out_ref, left_ref, right_ref):
    @pl.when(pl.program_id(0) == 0)
    def _():
        left_ref[:, :N] = mlpt_ref[...].astype(BF16)
        left_ref[:, N:] = mlpt_other[...].astype(BF16)

    right_ref[:N] = act_ref[...]
    right_ref[N:] = act_other[...].astype(BF16)
    up = dot(left_ref[...], right_ref[...]).reshape(SEQ, 64, TILE)
    for slab in range(2):
        out_ref[:, slab * 64 : slab * 64 + 64] = up[:, :, slab * 128 : (slab + 1) * 128]


def up_grad(mlpt, mlpt_other, act, act_other):
    full = lambda shape: pl.BlockSpec(shape, lambda t: (0,) * len(shape))
    wide = pl.BlockSpec((N, TILE), lambda t: (0, t))
    return pl.pallas_call(
        up_grad_kernel,
        grid=(TILES,),
        in_specs=[full((D, N)), full((D, N)), wide, wide],
        out_specs=pl.BlockSpec((SEQ, 128, 128), lambda t: (0, t, 0)),
        scratch_shapes=[pltpu.VMEM((D, 2 * N), BF16), pltpu.VMEM((2 * N, TILE), BF16)],
        out_shape=jax.ShapeDtypeStruct((SEQ, TILES * 128, 128), F32),
        compiler_params=params(),
        cost_estimate=cost(40),
        name="up_grad",
    )(mlpt, mlpt_other, act, act_other)


def back_kernel(
    core_ref, middle_ref, dmlp_ref, cot_ref, mg_ref, ow_ref, hg_ref, heads_ref, og_ref, q_ref, ld_ref, cl_ref,
    dmid_ref, datt_ref, mgg_ref, hgg_ref, dheads_ref, dog_ref, sends_ref, adj_ref, out_ref,
    dmix_ref,
):
    away = pl.ds(pl.multiple_of((1 - core_ref[40]) * 512, 512), 512)
    m = pl.program_id(0)

    @pl.when(m == 0)
    def _():
        total = jnp.zeros((1, D), F32)
        for at in range(0, N, 128):
            here = slice(at, at + 128)
            middle = middle_ref[here]
            scale = inverse_rms(middle)
            unit = middle * scale
            grad = dmlp_ref[here]
            total = total + jnp.sum(grad * unit, 0, keepdims=True)
            scaled = grad * mg_ref[...].astype(F32)
            d_middle = scale * (scaled - unit * jnp.mean(scaled * unit, -1, keepdims=True))
            d_middle = d_middle + cot_ref[here].astype(F32)
            dmid_ref[here] = d_middle
            datt_ref[here] = d_middle.astype(BF16)
        mgg_ref[...] = total
        hgg_ref[...] = jnp.zeros((1, VHEAD), F32)
        dmix_ref[...] = dot(datt_ref[...], ow_ref[...], 1, 1)

    block = m + 1 - 2 * lax.rem(m, 2)
    rows = pl.ds(pl.multiple_of(block * BLK, BLK), BLK)
    first = lax.rem(m, 2) == 0
    closing = cl_ref[pl.ds(block, 1), :]
    gain = hg_ref[...].astype(F32)
    for head in range(HEADS):
        chan = slice(head * KHEAD, (head + 1) * KHEAD)
        vals = slice(head * VHEAD, (head + 1) * VHEAD)
        out = heads_ref[:, vals]
        scale = inverse_rms(out)
        unit = out * scale
        gate = og_ref[:, vals]
        sig = sigmoid(gate)
        act = gate * sig
        d_mixed = dmix_ref[rows, vals]
        dog_ref[:, vals] = (d_mixed * (unit * gain) * (sig * (1.0 + gate * (1.0 - sig)))).astype(BF16)
        d_norm = d_mixed * act
        hgg_ref[...] += jnp.sum(d_norm * unit, 0, keepdims=True)
        scaled = d_norm * gain
        d_out = scale * (scaled - unit * jnp.mean(scaled * unit, -1, keepdims=True))
        dheads_ref[:, vals] = d_out
        adjoint = dot3(d_out, q_ref[:, chan] * jnp.exp(ld_ref[:, chan]), 0, 0)

        @pl.when(first)
        def _():
            adj_ref[0, head] = adjoint

        @pl.when(jnp.logical_not(first))
        def _():
            total = jnp.exp(closing[:, chan]) * adj_ref[0, head] + adjoint
            for half in range(2):
                out_ref[head * 2 + half] = total[half * 128 : (half + 1) * 128]

    sends_ref[:, :512] = datt_ref[rows, away].astype(F32)
    sends_ref[:, 512:] = dog_ref[:, away].astype(F32)


def back(core, middle, dmlp, cot, mg, ow, hg, heads, proj, ld, cl):
    full = lambda shape: pl.BlockSpec(shape, lambda m, c: (0,) * len(shape))
    block = lambda m: m + 1 - 2 * lax.rem(m, 2)
    return pl.pallas_call(
        back_kernel,
        grid_spec=pltpu.PrefetchScalarGridSpec(num_scalar_prefetch=1, grid=(4,), in_specs=[
            full((N, D)), full((N, D)), full((N, D)), full((1, D)), full((VALUE, D)), full((1, VHEAD)),
            pl.BlockSpec((BLK, VALUE), lambda m, c: (block(m), 0)),
            pl.BlockSpec((BLK, VALUE), lambda m, c: (block(m), 2)),
            pl.BlockSpec((BLK, KD), lambda m, c: (block(m), 0)),
            pl.BlockSpec((BLK, KD), lambda m, c: (block(m), 0)),
            full((8, KD)),
        ],
        out_specs=[
            full((N, D)), full((N, D)), full((1, D)), full((1, VHEAD)),
            pl.BlockSpec((BLK, VALUE), lambda m, c: (block(m), 0)),
            pl.BlockSpec((BLK, VALUE), lambda m, c: (block(m), 0)),
            pl.BlockSpec((BLK, D), lambda m, c: (block(m), 0)),
            pl.BlockSpec((1, HEADS, VHEAD, KHEAD), lambda m, c: (m // 2, 0, 0, 0)),
            pl.BlockSpec((8, 128, KHEAD), lambda m, c: (m // 2, 0, 0)),
        ],
        scratch_shapes=[pltpu.VMEM((N, VALUE), F32)]),
        out_shape=[
            jax.ShapeDtypeStruct((N, D), F32), jax.ShapeDtypeStruct((N, D), BF16),
            jax.ShapeDtypeStruct((1, D), F32), jax.ShapeDtypeStruct((1, VHEAD), F32),
            jax.ShapeDtypeStruct((N, VALUE), F32), jax.ShapeDtypeStruct((N, VALUE), BF16),
            jax.ShapeDtypeStruct((N, D), F32),
            jax.ShapeDtypeStruct((ROWS, HEADS, VHEAD, KHEAD), F32),
            jax.ShapeDtypeStruct((SEQ, 128, KHEAD), F32),
        ],
                compiler_params=params(),
        cost_estimate=cost(30),
        name="back",
    )(core, middle, dmlp, cot, mg, ow, hg, heads, proj, proj, ld, cl)


def inner_kernel(
    limit_ref, core_ref, q_ref, k_ref, v_ref, dout_ref, ld_ref, cl_ref, inc_ref, ret_ref, upd_ref, adj_ref,
    logit_ref, low_ref, gu_ref,
    dproj_ref, dprojs_ref, dlow_ref, gb_ref, gup_ref,
    dlg_ref,
):
    m = pl.program_id(0)
    row = m // 2
    part = lax.rem(m, 2)
    second = part == 1

    @pl.when(m == 0)
    def _():
        gb_ref[...] = jnp.zeros((1, KD), F32)
        gup_ref[...] = jnp.zeros((16, KD), F32)

    mask = lower((BLK, BLK))
    upper = lax.broadcasted_iota(jnp.int32, (BLK, BLK), 0) <= lax.broadcasted_iota(jnp.int32, (BLK, BLK), 1)
    upper = upper.astype(BF16)
    closing = cl_ref[pl.ds(m, 1), :]
    previous = cl_ref[pl.ds(row * 2, 1), :]
    following = cl_ref[pl.ds(row * 2 + 1, 1), :]
    alive = live(limit_ref, core_ref, row, part * BLK, BLK, VHEAD)
    alive_key = alive[:, :KHEAD]
    for head in range(HEADS):
        chan = slice(head * KHEAD, (head + 1) * KHEAD)
        vals = slice(head * VHEAD, (head + 1) * VHEAD)
        start = inc_ref[0, head]
        start = jnp.where(second, jnp.exp(previous[:, chan]) * start + upd_ref[0, 0, head], start)
        update = jnp.where(second, upd_ref[0, 1, head], upd_ref[0, 0, head])
        end_state = jnp.exp(closing[:, chan]) * start + update
        end_grad = ret_ref[0, head]
        end_grad = jnp.where(second, end_grad, jnp.exp(following[:, chan]) * end_grad + adj_ref[0, head])
        decay = ld_ref[:, chan]
        centre = decay[BLK // 2 - 1 : BLK // 2]
        query = q_ref[:, chan]
        key = k_ref[:, chan]
        value = v_ref[:, vals]
        d_out = dout_ref[:, vals]
        up_factor = jnp.exp(decay - centre)
        down_factor = jnp.exp(centre - decay)
        query_mid = query * up_factor
        key_mid = key * down_factor
        close_factor = jnp.exp(closing[:, chan] - decay)
        scores = jnp.where(mask, dot3(query_mid, key_mid, 1, 1), 0.0)
        d_scores = jnp.where(mask, dot3(d_out, value, 1, 1), 0.0)
        d_query = up_factor * dot3(d_scores, key_mid) + jnp.exp(decay) * dot3(d_out, start)
        d_key = down_factor * dot3(d_scores, query_mid, 0, 0) + close_factor * dot3(value, end_grad)
        d_value = dot3(scores, d_out, 0, 0) + dot3(key * close_factor, end_grad, 1, 1)
        d_decay = query * d_query - key * d_key
        dlg_ref[:, chan] = dot_ones(upper, d_decay) + jnp.sum(end_grad * end_state, 0, keepdims=True)
        dproj_ref[:, chan] = (d_query * KHEAD ** (-0.5)).astype(BF16)
        dproj_ref[:, KD + head * KHEAD : KD + (head + 1) * KHEAD] = (d_key * alive_key).astype(BF16)
        dproj_ref[:, 2 * KD + head * VHEAD : 2 * KD + (head + 1) * VHEAD] = (d_value * alive).astype(BF16)
    alive_gate = live(limit_ref, core_ref, row, part * BLK, BLK, KD)
    d_logit = dlg_ref[...] * alive_gate * (1.0 / (1.0 + jnp.exp(logit_ref[...]))) * (1.0 / 16.0)
    gb_ref[...] += jnp.sum(d_logit, 0, keepdims=True)
    gup_ref[...] += dot3(low_ref[...], d_logit, 0, 0)
    high, rest = split(d_logit)
    dlow_ref[...] = (dot(high, gu_ref[...], 1, 1) + dot(rest, gu_ref[...], 1, 1)).astype(BF16)
    away = pl.ds(pl.multiple_of((1 - core_ref[40]) * 1024, 1024), 1024)
    dprojs_ref[...] = dproj_ref[:, away].astype(F32)


def inner(limit, core, proj, dout, ld, cl, incoming, returned, upd, adj, logit, low, gu):
    full = lambda shape: pl.BlockSpec(shape, lambda m, s, c: (0,) * len(shape))
    by_row = pl.BlockSpec((1, HEADS, VHEAD, KHEAD), lambda m, s, c: (m // 2, 0, 0, 0))
    return pl.pallas_call(
        inner_kernel,
        grid_spec=pltpu.PrefetchScalarGridSpec(
            num_scalar_prefetch=2,
            grid=(4,),
            in_specs=[
                pl.BlockSpec((BLK, KD), lambda m, s, c: (m, 0)), pl.BlockSpec((BLK, KD), lambda m, s, c: (m, 1)),
                pl.BlockSpec((BLK, VALUE), lambda m, s, c: (m, 1)), pl.BlockSpec((BLK, VALUE), lambda m, s, c: (m, 0)),
                pl.BlockSpec((BLK, KD), lambda m, s, c: (m, 0)), full((8, KD)),
                by_row, by_row,
                pl.BlockSpec((1, 2, HEADS, VHEAD, KHEAD), lambda m, s, c: (m // 2, 0, 0, 0, 0)),
                by_row,
                pl.BlockSpec((BLK, KD), lambda m, s, c: (m, 0)), pl.BlockSpec((BLK, 16), lambda m, s, c: (m, 0)),
                full((16, KD)),
            ],
            out_specs=[
                pl.BlockSpec((BLK, 2048), lambda m, s, c: (m, 0)),
                pl.BlockSpec((BLK, 1024), lambda m, s, c: (m, 0)), pl.BlockSpec((BLK, 16), lambda m, s, c: (m, 0)),
                full((1, KD)), full((16, KD)),
            ],
            scratch_shapes=[pltpu.VMEM((BLK, KD), F32)],
        ),
        out_shape=[
            jax.ShapeDtypeStruct((N, 2048), BF16), jax.ShapeDtypeStruct((N, 1024), F32), jax.ShapeDtypeStruct((N, 16), BF16),
            jax.ShapeDtypeStruct((1, KD), F32), jax.ShapeDtypeStruct((16, KD), F32),
        ],
        compiler_params=params(),
        cost_estimate=cost(300),
        name="inner",
    )(limit, core, proj, proj, proj, dout, ld, cl, incoming, returned, upd, adj, logit, low, gu)


def outer_kernel(sets, extras, table_ref, *refs):
    count = 4 * len(sets)
    more, outs, (left_ref, right_ref) = refs[count : count + extras], refs[count + extras : -2], refs[-2:]
    at = 0
    for which, streams in enumerate(sets):
        x_ref, x_other, y_ref, y_other = refs[4 * which : 4 * which + 4]
        left_ref[:, :N] = x_ref[...].astype(BF16)
        left_ref[:, N:] = x_other[...].astype(BF16)
        for part, v in enumerate(streams):
            cols = slice(part * 512, (part + 1) * 512)
            right_ref[:N] = y_ref[:, cols]
            right_ref[N:] = y_other[:, cols].astype(BF16)
            value = dot(left_ref[...], right_ref[...])
            keep_ref, send_ref = outs[2 * at : 2 * at + 2]
            at += 1
            for chunk in range(SEQ):
                slot = table_ref[48 + v * SEQ + chunk]

                def put(target, index):
                    for slab in range(4):
                        target[index, slab * 64 : slab * 64 + 64] = value[
                            chunk * 64 : (chunk + 1) * 64, slab * 128 : slab * 128 + 128
                        ]
                    if extras:
                        own, got, own_too, got_too, pack = more
                        cut = slice(v * 64, v * 64 + 64)
                        target[index, 344:408] = own_too[chunk, cut] + got_too[chunk, cut]
                        if v == 1:
                            target[index, 408:432] = pack[chunk]
                        target[index, 256:344] = (
                            own[chunk, v * 88 : v * 88 + 88] + got[chunk, v * 88 : v * 88 + 88]
                        )

                @pl.when(slot < 8)
                def _():
                    put(keep_ref, slot)

                @pl.when(slot >= 8)
                def _():
                    put(send_ref, slot - 8)


def outer(table, sets, more=()):
    operands, specs, outs = [], [], []
    for x, x_other, rows, y, y_other, cols, streams in sets:
        width = 512 * len(streams)
        operands += [x, x_other, y, y_other]
        specs += [
            pl.BlockSpec((D, N), lambda i, t, r=rows: (r, 0)), pl.BlockSpec((D, N), lambda i, t, r=rows: (r, 0)),
            pl.BlockSpec((N, width), lambda i, t: (0, t[40])), pl.BlockSpec((N, width), lambda i, t, c=cols: (0, c)),
        ]
        for v in streams:
            total = 256 + (152 + 24 * v if more else 0)
            outs += [jax.ShapeDtypeStruct((8, total, 128), F32)] * 2
    for array in more:
        operands.append(array)
        specs.append(pl.BlockSpec(array.shape, lambda i, t: (0, 0, 0)))
    return pl.pallas_call(
        functools.partial(outer_kernel, [streams for *_, streams in sets], len(more)),
        grid_spec=pltpu.PrefetchScalarGridSpec(
            num_scalar_prefetch=1, grid=(1,), in_specs=specs,
            out_specs=[pl.BlockSpec(out.shape, lambda i, t: (0, 0, 0)) for out in outs],
            scratch_shapes=[pltpu.VMEM((D, 2 * N), BF16), pltpu.VMEM((2 * N, 512), BF16)],
        ),
        out_shape=outs,
        compiler_params=params(),
        cost_estimate=cost(0.1),
        name="outer",
    )(table, *operands)


def outer_x_kernel(table_ref, *refs):
    keep_ref, send_ref, left_ref, right_ref = refs[-4:]
    for which in range(2):
        x_ref, x_other, y_ref, y_other = refs[4 * which : 4 * which + 4]
        left_ref[:, :N] = x_ref[...].astype(BF16)
        left_ref[:, N:] = x_other[...].astype(BF16)
        right_ref[:N] = y_ref[...]
        right_ref[N:] = y_other[...].astype(BF16)
        value = dot(left_ref[...], right_ref[...]).reshape(SEQ, 64, 512)
        rows = slice(which * 64, which * 64 + 64)
        for slab in range(4):
            slot = table_ref[41 + slab]

            @pl.when(slot < 2)
            def _():
                keep_ref[slot, :, rows] = value[:, :, slab * 128 : (slab + 1) * 128]

            @pl.when(slot >= 2)
            def _():
                send_ref[slot - 2, :, rows] = value[:, :, slab * 128 : (slab + 1) * 128]


def outer_x(table, joint, joint_other, normed, normed_other, datt, dog, sends_other):
    left = lambda row: pl.BlockSpec((D, N), lambda i, t: (row, 0))
    own = pl.BlockSpec((N, 512), lambda i, t: (0, t[40]))
    other = lambda col: pl.BlockSpec((N, 512), lambda i, t: (0, col))
    out = pl.BlockSpec((2, SEQ, 128, 128), lambda i, t: (0, 0, 0, 0))
    return pl.pallas_call(
        outer_x_kernel,
        grid_spec=pltpu.PrefetchScalarGridSpec(
            num_scalar_prefetch=1, grid=(1,),
            in_specs=[left(1), left(1), own, other(0), left(0), left(0), own, other(1)],
            out_specs=[out, out],
            scratch_shapes=[pltpu.VMEM((D, 2 * N), BF16), pltpu.VMEM((2 * N, 512), BF16)],
        ),
        out_shape=[jax.ShapeDtypeStruct((2, SEQ, 128, 128), F32)] * 2,
        compiler_params=params(),
        cost_estimate=cost(0.1),
        name="outer_x",
    )(table, joint, joint_other, datt, sends_other, normed, normed_other, dog, sends_other)


def input_kernel(
    y_ref, og_ref, w_ref, dlow_ref, gd_ref, tok_ref, gain_ref, dmid_ref, normed_ref,
    gup_ref, gb_ref, hg_ref, mg_ref,
    grad_ref, pack_ref, acc_ref,
):
    t = pl.program_id(0)

    @pl.when(t == 0)
    def _():
        acc_ref[...] = dot(dlow_ref[...], gd_ref[...])
        grad_down = dot(dlow_ref[...], normed_ref[...], 0, 0)
        pack_ref[:, 16:24] = jnp.zeros((SEQ, 8, 128), F32)
        for chunk in range(SEQ):
            pack_ref[chunk, :16, :64] = grad_down[:, chunk * 64 : chunk * 64 + 64]
            pack_ref[chunk, :16, 64:96] = gup_ref[:, chunk * 32 : chunk * 32 + 32]
            pack_ref[chunk, :16, 96:] = jnp.zeros((16, 32), F32)
            pack_ref[chunk, 16:17, 64:] = mg_ref[:, chunk * 64 : chunk * 64 + 64]
            pack_ref[chunk, 17:18, :32] = gb_ref[:, chunk * 32 : chunk * 32 + 32]
            pack_ref[chunk, 17:18, 32:48] = hg_ref[:, chunk * 16 : chunk * 16 + 16]

    @pl.when(t < 4)
    def _():
        acc_ref[...] += dot(y_ref[...], w_ref[...], 1, 1)

    @pl.when(t >= 4)
    def _():
        acc_ref[...] += dot(og_ref[...], w_ref[...], 1, 1)

    @pl.when(t == 5)
    def _():
        total = jnp.zeros((1, D), F32)
        for at in range(0, N, 128):
            here = slice(at, at + 128)
            inputs = tok_ref[here].astype(F32)
            scale = inverse_rms(inputs)
            unit = inputs * scale
            grad = acc_ref[here]
            total = total + jnp.sum(grad * unit, 0, keepdims=True)
            scaled = grad * gain_ref[...].astype(F32)
            d_inputs = scale * (scaled - unit * jnp.mean(scaled * unit, -1, keepdims=True))
            grad_ref[here] = (dmid_ref[here] + d_inputs).astype(BF16)
        for chunk in range(SEQ):
            pack_ref[chunk, 16:17, :64] = total[:, chunk * 64 : chunk * 64 + 64]


def input_back(y, og, w, dlow, gd, tokens, gain, dmid, normed, gup, gb, hg, mg):
    full = lambda shape: pl.BlockSpec(shape, lambda t: (0,) * len(shape))
    return pl.pallas_call(
        input_kernel,
        grid=(6,),
        in_specs=[
            pl.BlockSpec((N, 512), lambda t: (0, jnp.minimum(t, 3))),
            pl.BlockSpec((N, 512), lambda t: (0, jnp.maximum(t - 4, 0))),
            pl.BlockSpec((D, 512), lambda t: (0, t)),
            full((N, 16)), full((16, D)), full((N, D)), full((1, D)), full((N, D)), full((N, D)),
            full((16, KD)), full((1, KD)), full((1, VHEAD)), full((1, D)),
        ],
        out_specs=[full((N, D)), full((SEQ, 24, 128))],
        out_shape=[
            jax.ShapeDtypeStruct((N, D), BF16), jax.ShapeDtypeStruct((SEQ, 24, 128), F32),
        ],
        scratch_shapes=[pltpu.VMEM((N, D), F32)],
        compiler_params=params(),
        cost_estimate=cost(12),
        name="input_back",
    )(y, og, w, dlow, gd, tokens, gain, dmid, normed, gup, gb, hg, mg)


SWAP = [(i, i ^ 1) for i in range(8)]
FLIP = {0: 1, 1: 3}
XORDER = ((0, 1), (1, 0))
ORDERS = (((0, 1, 2, 3), (1, 0, 3, 2)), ((2, 3, 0, 1), (3, 2, 1, 0)))


def bit_of(seq, which):
    at = seq // 4 if which < 2 else seq % 4
    return at // 2 if which % 2 else int(at in (1, 2))


def chunk_of(order, bits):
    value = dict(zip(order, bits))
    along = [[0, 1, 3, 2][2 * value[2 * a + 1] + value[2 * a]] for a in range(2)]
    return along[0] * 4 + along[1]


def partner(seq, which):
    z, y = seq // 4, seq % 4
    return (z ^ FLIP[which]) * 4 + y if which < 2 else z * 4 + (y ^ FLIP[which - 2])


def tables():
    table = np.zeros((128, 96), np.int32)
    for device in range(128):
        core, seq = (device // 16) % 2, device % 16
        for v in range(2):
            order = ORDERS[v][core]
            chunks = [chunk_of(order, [(i >> 3) & 1, (i >> 2) & 1, (i >> 1) & 1, i & 1]) for i in range(16)]
            mine = [bit_of(seq, which) for which in order]
            table[device, v * 16 : v * 16 + 8] = chunks[mine[0] * 8 : mine[0] * 8 + 8]
            table[device, v * 16 + 8 : v * 16 + 16] = chunks[(1 - mine[0]) * 8 : (1 - mine[0]) * 8 + 8]
            table[device, 32 + v * 4 : 36 + v * 4] = mine
            for slot in range(16):
                table[device, 48 + v * 16 + chunks[slot ^ (8 * mine[0])]] = slot
        table[device, 40] = core
        table[device, 46] = seq
        x, (near, far) = device // 32, XORDER[core]
        for slab in range(4):
            away = bit_of(slab * 4, near) != bit_of(x * 4, near)
            table[device, 41 + slab] = bit_of(slab * 4, far) + 2 * away
        table[device, 45] = bit_of(x * 4, far)
        for who in range(2):
            near, far = XORDER[core ^ who]
            table[device, 80 + 4 * who : 84 + 4 * who] = [x, x ^ FLIP[far], x ^ FLIP[near], x ^ 2]
    return table


TABLE = tables()
STEPS = [
    [
        [(d, (d // 16) * 16 + partner(d % 16, ORDERS[v][(d // 16) % 2][step])) for d in range(128)]
        for step in range(4)
    ]
    for v in range(2)
]
ACROSS = [
    [(i, ((i // 2) ^ FLIP[XORDER[i % 2][step]]) * 2 + i % 2) for i in range(8)] for step in range(2)
]


def exchange(value):
    return lax.all_to_all(value, "seq", 0, 0, tiled=True)


def swap(value):
    return lax.ppermute(value, "dp", SWAP)


def next_kernel(count, table_ref, *refs):
    del table_ref
    for stream in range(count):
        ks_ref, kk_ref, rs_ref, rk_ref = refs[4 * stream : 4 * stream + 4]
        send_ref, keep_ref = refs[4 * count + 2 * stream : 4 * count + 2 * stream + 2]
        send_ref[...] = ks_ref[...] + rs_ref[...]
        keep_ref[...] = kk_ref[...] + rk_ref[...]


def halve(table, streams):
    operands, specs, outs, out_specs = [], [], [], []
    half = streams[0][0].shape[0] // 2
    cut = streams[0][3]
    size = max(half // 2, 1)
    turns = half // size
    for keep, got, slot, _ in streams:
        rows = keep.shape[1] // cut
        mine = pl.BlockSpec((size, rows, 128), lambda i, j, t, s=slot: (t[s] * turns + i, j, 0))
        theirs = pl.BlockSpec((size, rows, 128), lambda i, j, t, s=slot: ((1 - t[s]) * turns + i, j, 0))
        operands += [keep, keep, got, got]
        specs += [theirs, mine, theirs, mine]
        outs += [jax.ShapeDtypeStruct((half, rows * cut, 128), F32)] * 2
        out_specs += [pl.BlockSpec((size, rows, 128), lambda i, j, t: (i, j, 0))] * 2
    total = sum(half * keep.shape[1] * 512 for keep, *_ in streams)
    return pl.pallas_call(
        functools.partial(next_kernel, len(streams)),
        grid_spec=pltpu.PrefetchScalarGridSpec(
            num_scalar_prefetch=1, grid=(turns, cut), in_specs=specs, out_specs=out_specs
        ),
        out_shape=outs,
        compiler_params=params(),
        cost_estimate=cost(0.1),
        name="halve",
    )(table, *operands)


def hop(v, step, value):
    return lax.ppermute(value, ("dp", "seq"), STEPS[v][step])


def hops(step, sends):
    return [hop(v, step, sends[v]) for v in range(2)]


def onward(table, step, keeps, gots):
    streams = [(keeps[v], gots[v], 32 + v * 4 + step, 1) for v in range(2)]
    send_0, keep_0, send_1, keep_1 = halve(table, streams)
    return (send_0, send_1), (keep_0, keep_1)


def along_x(step, value):
    return lax.ppermute(value, "dp", ACROSS[step])


def after(value, *others):
    return lax.optimization_barrier((value, *others))[0]


def unpack_kernel(
    table_ref, a_ref, a_other, b_ref, b_other,
    up_ref, down_ref, out_ref, in_ref, gd_ref, gu_ref, ng_ref, mg_ref, gb_ref, hg_ref,
):
    core = table_ref[40]

    def place(own_ref, other_ref, at, rows, slabs, target, first, second):
        for slab in range(slabs):
            own = own_ref[at : at + rows]
            other = other_ref[at : at + rows]
            low = jnp.where(core == 0, own, other)
            high = jnp.where(core == 0, other, own)
            target[:, first + slab * 128 : first + (slab + 1) * 128] = low
            target[:, second + slab * 128 : second + (slab + 1) * 128] = high
            at += rows
        return at

    place(a_ref, a_other, 0, 64, 22, up_ref, 0, FF)
    at = place(b_ref, b_other, 0, 64, 4, in_ref, 0, 1024)
    at = place(b_ref, b_other, at, 64, 4, in_ref, 512, 1536)
    small = b_ref[at : at + 24] + b_other[at : at + 24]
    gd_ref[...] = small[:16, :64]
    gu_ref[...] = small[:16, 64:96]
    ng_ref[...] = small[16:17, :64]
    mg_ref[...] = small[16:17, 64:128]
    gb_ref[...] = small[17:18, :32]
    hg_ref[...] = small[17:18, 32:48]
    for slab in range(4):
        first = at + 24 + slab * 304
        for ref, base, place_of in ((b_ref, core * 512, 80), (b_other, (1 - core) * 512, 84)):
            column = base + table_ref[place_of + slab] * 128
            cols = pl.ds(pl.multiple_of(column, 128), 128)
            down_ref[:88, cols] = ref[first : first + 88]
            out_ref[:, cols] = ref[first + 88 : first + 152]
            down_ref[88:, cols] = ref[first + 152 : first + 240]
            in_ref[:, pl.ds(pl.multiple_of(2048 + column, 128), 128)] = ref[first + 240 : first + 304]


def unpack(table, a, a_other, b, b_other):
    shapes = [
        (64, 2 * FF), (176, D), (64, D), (64, 3072), (16, 64), (16, 32), (1, 64), (1, 64), (1, 32), (1, 16),
    ]
    return pl.pallas_call(
        unpack_kernel,
        in_specs=[pl.BlockSpec(memory_space=pltpu.SMEM)] + [pl.BlockSpec(memory_space=pltpu.VMEM)] * 4,
        out_specs=[pl.BlockSpec(memory_space=pltpu.VMEM)] * len(shapes),
        out_shape=[jax.ShapeDtypeStruct(shape, F32) for shape in shapes],
        compiler_params=params(),
        cost_estimate=cost(4),
        name="unpack",
    )(table, a, a_other, b, b_other)


def chunks(value):
    return value.reshape(SEQ, value.shape[0] // SEQ, value.shape[1])


def shards(
    tokens, lengths, cotangent, norm_gain, in_weight, gate_down, gate_up, gate_bias, head_gain,
    out_weight, mlp_gain, up_weight, down_weight,
):
    device = lax.axis_index("dp") * SEQ + lax.axis_index("seq")
    table = lax.dynamic_slice(jnp.asarray(TABLE), (device, 0), (1, 96)).reshape(96)
    tok = tokens.reshape(N, D)
    cot = cotangent.reshape(N, D)
    line = lambda vector: vector.reshape(1, -1)
    flat = lambda value: value.reshape(2, -1, 128)

    down_t, up_t = gate_down.T, gate_up.T
    proj, normed, normed_t, cot_send, ld, cl, logit, low, upd, pieces = project(
        lengths, table, tok, cot, line(norm_gain), in_weight, down_t, up_t, line(gate_bias)
    )
    gathered = exchange(pieces)
    incoming = exchange(prefix(gathered, gathered, False)).reshape(ROWS, HEADS, VHEAD, KHEAD)
    heads, middle, mlp_in, joint = attend(
        proj, ld, cl, incoming, upd, tok, out_weight, line(head_gain), line(mlp_gain)
    )
    normed_other, cot_other = swap(normed_t), swap(cot_send)
    output, dmlp, act, act_send, hidden_t = mlp(
        table, after(mlp_in, normed_other, cot_other), cot, up_weight, down_weight, middle
    )
    hidden_other, act_other, joint_other = swap(hidden_t), swap(act_send), swap(joint)
    dmid, datt, g_mlp_gain, g_head_gain, dheads, dog, sends, adj, pieces_back = back(
        table, middle, dmlp, cot, line(mlp_gain), out_weight, line(head_gain), heads, proj, ld, cl
    )
    sends_other = swap(sends)
    owned = exchange(pieces_back)
    dn_keep, dn_send = down_grad(table, after(hidden_t, pieces_back), hidden_other, cot, cot_other)
    dn_got = along_x(0, after(flat(dn_send), owned))
    owned = prefix(after(owned, dn_keep), gathered, True)
    returned = exchange(owned)
    wide = up_grad(after(joint, owned, sends_other), joint_other, act, act_other)
    fr_keep, fr_send = outer_x(after(table, wide), joint, joint_other, normed_t, normed_other, datt, dog, sends_other)
    fr_got = along_x(0, flat(fr_send))
    early = lax.psum_scatter(after(wide, returned, dn_got), "seq", scatter_dimension=0, tiled=True)[0]
    returned = after(returned, fr_keep).reshape(ROWS, HEADS, VHEAD, KHEAD)
    dproj, dproj_send, dlow, g_gate_bias, g_gate_up = inner(
        lengths, table, proj, dheads, ld, cl, incoming, returned, upd, adj, logit, low, up_t
    )
    dproj_got = swap(after(dproj_send, fr_got))
    dn_send, dn_keep, fr_send, fr_keep = halve(
        table, [(after(flat(dn_keep), dlow), dn_got, 45, 4), (flat(fr_keep), fr_got, 45, 4)]
    )
    dn_got, fr_got = along_x(1, dn_send), along_x(1, fr_send)
    input_grad, pack = input_back(
        after(dproj, dn_keep), dog, in_weight, dlow, down_t, tok, line(norm_gain), dmid, normed,
        g_gate_up, g_gate_bias, g_head_gain, g_mlp_gain,
    )
    by_chunk = lambda value: value.reshape(SEQ, -1, 128)
    keep_p, send_p, keep_r, send_r = outer(
        table,
        [(normed_t, normed_other, 0, dproj, dproj_got, 0, (0, 1))],
        (by_chunk(dn_keep), by_chunk(dn_got), by_chunk(fr_keep), by_chunk(fr_got), pack),
    )
    five_keep = (keep_p, keep_r)
    five_got = hops(0, (send_p, send_r))
    five_send, five_keep = onward(table, 1, five_keep, five_got)
    five_got = hops(1, five_send)
    early = after(early, five_keep[0])
    early = early + along_x(0, early)
    five_send, five_keep = onward(table, 2, (after(five_keep[0], early), five_keep[1]), five_got)
    five_got = hops(2, five_send)
    early = early + along_x(1, early)
    five_send, five_keep = onward(table, 3, (after(five_keep[0], early), five_keep[1]), five_got)
    five_got = hops(3, five_send)
    early_other = swap(early)
    five = [(five_keep[v] + five_got[v])[0] for v in range(2)]
    late = jnp.concatenate([five[0][:256], five[1][:256], five[1][408:]], 0)
    slab = jnp.concatenate([five[0][256:], five[1][256:408]], 0)
    got = along_x(1, jnp.concatenate([late, slab], 0))
    late = jnp.concatenate([late + got[:536], slab, got[536:]], 0)
    got = along_x(0, late)
    late = jnp.concatenate([late[:536] + got[:536], late[536:], got[536:]], 0)
    grad_up, grad_down, grad_out, grad_in, g_down, g_upf, g_norm, g_mlp, g_bias, g_head = unpack(
        table, early, early_other, late, swap(late)
    )
    return (
        output.reshape(ROWS, SEG, D),
        input_grad.reshape(ROWS, SEG, D),
        g_norm.reshape(64),
        grad_in,
        g_down.T,
        g_upf.T,
        g_bias.reshape(32),
        g_head.reshape(16),
        grad_out,
        g_mlp.reshape(64),
        grad_up,
        grad_down,
    )


def solution(mesh):
    rows = P("dp", "seq", None)
    return jax.shard_map(
        shards,
        mesh=mesh,
        in_specs=(rows, P("dp"), rows) + (P(),) * 10,
        out_specs=(
            rows, rows, P("seq"), P("seq", None), P("seq", None), P("seq", None), P("seq"), P("seq"),
            P("seq", None), P("seq"), P("seq", None), P("seq", None),
        ),
        check_vma=False,
    )
```

```python
import functools

import jax
import jax.numpy as jnp
import numpy as np
from jax import lax
from jax.experimental import pallas as pl
from jax.experimental.pallas import tpu as pltpu
from jax.sharding import PartitionSpec as P

F32 = jnp.float32
BF16 = jnp.bfloat16
D = 1024
FF = 2816
HEADS = 4
KHEAD = 128
VHEAD = 256
KD = 512
VALUE = 1024
ROWS = 2
SEG = 256
BLK = 128
N = ROWS * SEG
SEQ = 16
TILE = 256
EPSILON = 1e-06
VMEM_LIMIT = 62 * 1024 * 1024


def params(**kw):
    return pltpu.CompilerParams(vmem_limit_bytes=VMEM_LIMIT, **kw)


def cost(us):
    return pl.CostEstimate(flops=0, bytes_accessed=int(us * 3e6), transcendentals=0)


def dot(a, b, ca=1, cb=0):
    return lax.dot_general(a, b, (((ca,), (cb,)), ((), ())), preferred_element_type=F32)


def split(a):
    high = a.astype(BF16)
    return high, (a - high.astype(F32)).astype(BF16)


def dot3(a, b, ca=1, cb=0):
    ah, al = split(a)
    bh, bl = split(b)
    return dot(ah, bh, ca, cb) + (dot(ah, bl, ca, cb) + dot(al, bh, ca, cb))


def dot_ones(ones, b, ca=1, cb=0):
    high = b.astype(BF16)
    rest = b - high.astype(F32)
    mid = rest.astype(BF16)
    low = (rest - mid.astype(F32)).astype(BF16)
    return dot(ones, high, ca, cb) + (dot(ones, mid, ca, cb) + dot(ones, low, ca, cb))


def sigmoid(u):
    return 1.0 / (1.0 + jnp.exp(-u))


def inverse_rms(u):
    return lax.rsqrt(jnp.mean(u * u, -1, keepdims=True) + EPSILON)


def live(lengths_ref, table_ref, row, first, count, width):
    where = lax.broadcasted_iota(jnp.int32, (count, width), 0) + (first + table_ref[46] * SEG)
    return (where < lengths_ref[row]).astype(F32)


def lower(shape):
    return lax.broadcasted_iota(jnp.int32, shape, 0) >= lax.broadcasted_iota(jnp.int32, shape, 1)


def proj_kernel(
    lengths_ref, table_ref, tok_ref, gain_ref, w_ref, gd_ref, gu_ref, gb_ref,
    k_ref, v_ref, normed_ref, ld_ref, cl_ref, logit_ref, low_ref, upd_ref, out_ref,
    kc_ref,
):
    n = pl.program_id(0)

    @pl.when(n == 0)
    def _():
        inputs = tok_ref[...].astype(F32)
        normed = (inputs * inverse_rms(inputs) * gain_ref[...].astype(F32)).astype(BF16)
        normed_ref[...] = normed
        low = dot(normed, gd_ref[...], 1, 1)
        low_ref[...] = low
        low_high, low_low = split(low)
        logit = dot(low_high, gu_ref[...]) + dot(low_low, gu_ref[...])
        logit = logit + gb_ref[...].astype(F32)
        logit_ref[...] = logit
        ones = lower((BLK, BLK)).astype(BF16)
        key = dot(normed, w_ref[...])
        for row in range(ROWS):
            for part in range(SEG // BLK):
                at = row * SEG + part * BLK
                here = slice(at, at + BLK)
                alive = live(lengths_ref, table_ref, row, part * BLK, BLK, KD)
                u = logit[here]
                log_gate = (jnp.minimum(u, 0.0) - jnp.log1p(jnp.exp(-jnp.abs(u)))) * (1.0 / 16.0)
                decay = dot_ones(ones, log_gate * alive)
                ld_ref[here] = decay
                m = row * (SEG // BLK) + part
                closing = decay[BLK - 1 : BLK]
                cl_ref[m : m + 1] = closing
                k_ref[here] = key[here] * alive
                kc_ref[here] = key[here] * alive * jnp.exp(closing - decay)
        cl_ref[4:8] = jnp.zeros((4, KD), F32)

    for step in (1, 2):

        @pl.when(n == step)
        def _():
            acc = dot(normed_ref[...], w_ref[...])
            for row in range(ROWS):
                values = []
                for part in range(SEG // BLK):
                    at = row * SEG + part * BLK
                    value = acc[at : at + BLK] * live(lengths_ref, table_ref, row, part * BLK, BLK, KD)
                    v_ref[at : at + BLK] = value
                    values.append(value)
                for sub in range(2):
                    head = (step - 1) * 2 + sub
                    chan = slice(head * KHEAD, (head + 1) * KHEAD)
                    total = None
                    for part in range(SEG // BLK):
                        at = row * SEG + part * BLK
                        m = row * (SEG // BLK) + part
                        update = dot3(
                            values[part][:, sub * VHEAD : (sub + 1) * VHEAD],
                            kc_ref[at : at + BLK, chan], 0, 0,
                        )
                        upd_ref[row, part, head] = update
                        if total is None:
                            total = update
                        else:
                            total = jnp.exp(cl_ref[m : m + 1, chan]) * total + update
                    base = row * (SEG // BLK)
                    gone = cl_ref[base : base + 1, chan] + cl_ref[base + 1 : base + 2, chan]
                    for half in range(2):
                        piece = (row * HEADS + head) * 2 + half
                        out_ref[piece, 0:128] = total[half * 128 : (half + 1) * 128]
                        out_ref[piece, 128:136] = jnp.broadcast_to(gone, (8, KHEAD))


def project(lengths, table, tokens, gain, w, gd, gu, gb):
    full = lambda shape: pl.BlockSpec(shape, lambda n, s, c: (0,) * len(shape))
    return pl.pallas_call(
        proj_kernel,
        grid_spec=pltpu.PrefetchScalarGridSpec(
            num_scalar_prefetch=2,
            grid=(3,),
            in_specs=[
                full((N, D)), full((1, D)), pl.BlockSpec((D, KD), lambda n, s, c: (0, n + 1)),
                full((16, D)), full((16, KD)), full((1, KD)),
            ],
            out_specs=[
                full((N, KD)), pl.BlockSpec((N, KD), lambda n, s, c: (0, jnp.maximum(n - 1, 0))),
                full((N, D)), full((N, KD)), full((8, KD)),
                full((N, KD)), full((N, 16)), full((ROWS, 2, HEADS, VHEAD, KHEAD)),
                full((SEQ, 136, KHEAD)),
            ],
            scratch_shapes=[pltpu.VMEM((N, KD), F32)],
        ),
        out_shape=[
            jax.ShapeDtypeStruct((N, KD), F32), jax.ShapeDtypeStruct((N, VALUE), F32),
            jax.ShapeDtypeStruct((N, D), BF16),
            jax.ShapeDtypeStruct((N, KD), F32), jax.ShapeDtypeStruct((8, KD), F32),
            jax.ShapeDtypeStruct((N, KD), F32), jax.ShapeDtypeStruct((N, 16), F32),
            jax.ShapeDtypeStruct((ROWS, 2, HEADS, VHEAD, KHEAD), F32),
            jax.ShapeDtypeStruct((SEQ, 136, KHEAD), F32),
        ],
        compiler_params=params(),
        cost_estimate=cost(10),
        name="project",
    )(lengths, table, tokens, gain, w, gd, gu, gb)


def rest_kernel(table_ref, normed_ref, w_ref, cot_ref, q_ref, og_ref, normt_ref, cots_ref):
    n = pl.program_id(0)
    acc = dot(normed_ref[...], w_ref[...])

    @pl.when(n == 0)
    def _():
        q_ref[...] = acc * KHEAD ** (-0.5)
        normt_ref[...] = normed_ref[...].T.astype(F32)

    @pl.when(n > 0)
    def _():
        og_ref[...] = acc

    @pl.when(n == 2)
    def _():
        cots_ref[...] = cot_ref[:, pl.ds(pl.multiple_of((1 - table_ref[40]) * 512, 512), 512)].astype(F32)


def project_rest(table, normed, w, cot):
    full = lambda shape: pl.BlockSpec(shape, lambda n, c: (0,) * len(shape))
    return pl.pallas_call(
        rest_kernel,
        grid_spec=pltpu.PrefetchScalarGridSpec(
            num_scalar_prefetch=1,
            grid=(3,),
            in_specs=[
                full((N, D)), pl.BlockSpec((D, KD), lambda n, c: (0, jnp.where(n == 0, 0, n + 3))), full((N, D)),
            ],
            out_specs=[
                full((N, KD)), pl.BlockSpec((N, KD), lambda n, c: (0, jnp.maximum(n - 1, 0))),
                full((D, N)), full((N, KD)),
            ],
        ),
        out_shape=[
            jax.ShapeDtypeStruct((N, KD), F32), jax.ShapeDtypeStruct((N, VALUE), F32),
            jax.ShapeDtypeStruct((D, N), F32), jax.ShapeDtypeStruct((N, KD), F32),
        ],
        compiler_params=params(),
        cost_estimate=cost(0.1),
        name="project_rest",
    )(table, normed, w, cot)


def local_kernel(q_ref, k_ref, v_ref, ld_ref, out_ref):
    mask = lower((BLK, BLK))
    for head in range(HEADS):
        chan = slice(head * KHEAD, (head + 1) * KHEAD)
        vals = slice(head * VHEAD, (head + 1) * VHEAD)
        decay = ld_ref[:, chan]
        centre = decay[BLK // 2 - 1 : BLK // 2]
        scores = dot3(q_ref[:, chan] * jnp.exp(decay - centre), k_ref[:, chan] * jnp.exp(centre - decay), 1, 1)
        out_ref[:, vals] = dot3(jnp.where(mask, scores, 0.0), v_ref[:, vals])


def local(q, k, v, ld):
    rows = lambda width: pl.BlockSpec((BLK, width), lambda m: (m, 0))
    return pl.pallas_call(
        local_kernel,
        grid=(4,),
        in_specs=[rows(KD), rows(KD), rows(VALUE), rows(KD)],
        out_specs=rows(VALUE),
        out_shape=jax.ShapeDtypeStruct((N, VALUE), F32),
        compiler_params=params(),
        cost_estimate=cost(0.1),
        name="local",
    )(q, k, v, ld)


def hidden_kernel(cot_ref, wd_ref, out_ref):
    out_ref[...] = dot(cot_ref[...], wd_ref[...], 1, 1)


def hidden_grad(cot, dnw):
    return pl.pallas_call(
        hidden_kernel,
        grid=(2,),
        in_specs=[pl.BlockSpec((N, D), lambda t: (0, 0)), pl.BlockSpec((FF // 2, D), lambda t: (t, 0))],
        out_specs=pl.BlockSpec((N, FF // 2), lambda t: (0, t)),
        out_shape=jax.ShapeDtypeStruct((N, FF), F32),
        compiler_params=params(),
        cost_estimate=cost(0.1),
        name="hidden_grad",
    )(cot, dnw)


def prefix_kernel(backward, part_ref, decay_ref, out_ref):
    run = jnp.zeros((128, KHEAD), F32)
    order = range(SEQ - 1, -1, -1) if backward else range(SEQ)
    for seg in order:
        out_ref[seg] = run
        run = jnp.exp(decay_ref[seg, 0:1]) * run + part_ref[seg, 0:128]


def prefix(parts, decays, backward):
    return pl.pallas_call(
        functools.partial(prefix_kernel, backward),
        grid=(1,),
        in_specs=[
            pl.BlockSpec((SEQ, 128, KHEAD), lambda n: (0, 0, 0)),
            pl.BlockSpec((SEQ, 8, KHEAD), lambda n: (0, 16, 0)),
        ],
        out_specs=pl.BlockSpec((SEQ, 128, KHEAD), lambda n: (0, 0, 0)),
        out_shape=jax.ShapeDtypeStruct((SEQ, 128, KHEAD), F32),
        compiler_params=params(),
        cost_estimate=cost(0.1),
        name="prefix",
    )(parts, decays)


def attend_kernel(
    q_ref, og_ref, ld_ref, within_ref, cl_ref, inc_ref, upd_ref, tok_ref, ow_ref, hg_ref, mg_ref,
    heads_ref, middle_ref, mlp_ref, both_ref,
    mixed_ref,
):
    m = pl.program_id(0)
    second = lax.rem(m, 2) == 1
    previous = cl_ref[pl.ds(m - lax.rem(m, 2), 1), :]
    gain = hg_ref[...].astype(F32)
    for head in range(HEADS):
        chan = slice(head * KHEAD, (head + 1) * KHEAD)
        vals = slice(head * VHEAD, (head + 1) * VHEAD)
        start = inc_ref[0, head]
        start = jnp.where(second, jnp.exp(previous[:, chan]) * start + upd_ref[0, 0, head], start)
        out = within_ref[:, vals] + dot3(q_ref[:, chan] * jnp.exp(ld_ref[:, chan]), start, 1, 1)
        heads_ref[:, vals] = out
        gate = og_ref[:, vals]
        mixed = out * inverse_rms(out) * gain * (gate * sigmoid(gate))
        mixed_ref[:, vals] = mixed.astype(BF16)

    middle = tok_ref[...].astype(F32) + dot(mixed_ref[...], ow_ref[...])
    middle_ref[...] = middle
    mlp_in = (middle * inverse_rms(middle) * mg_ref[...].astype(F32)).astype(BF16)
    mlp_ref[...] = mlp_in
    both_ref[:D] = mlp_in.T.astype(F32)
    both_ref[D:] = mixed_ref[...].T.astype(F32)


def attend(q, og, ld, within, cl, incoming, upd, tokens, ow, hg, mg):
    full = lambda shape: pl.BlockSpec(shape, lambda m: (0,) * len(shape))
    rows = lambda width: pl.BlockSpec((BLK, width), lambda m: (m, 0))
    return pl.pallas_call(
        attend_kernel,
        grid=(4,),
        in_specs=[
            rows(KD), rows(VALUE), rows(KD), rows(VALUE), full((8, KD)),
            pl.BlockSpec((1, HEADS, VHEAD, KHEAD), lambda m: (m // 2, 0, 0, 0)),
            pl.BlockSpec((1, 1, HEADS, VHEAD, KHEAD), lambda m: (m // 2, 0, 0, 0, 0)),
            rows(D), full((VALUE, D)), full((1, VHEAD)), full((1, D)),
        ],
        out_specs=[
            rows(VALUE), rows(D), rows(D), pl.BlockSpec((D + VALUE, BLK), lambda m: (0, m)),
        ],
        out_shape=[
            jax.ShapeDtypeStruct((N, VALUE), F32), jax.ShapeDtypeStruct((N, D), F32),
            jax.ShapeDtypeStruct((N, D), BF16), jax.ShapeDtypeStruct((D + VALUE, N), F32),
        ],
        scratch_shapes=[pltpu.VMEM((BLK, VALUE), BF16)],
        compiler_params=params(),
        cost_estimate=cost(13),
        name="attend",
    )(q, og, ld, within, cl, incoming, upd, tokens, ow, hg, mg)


TILES = FF // TILE


def mlp_kernel(
    core_ref, mlp_ref, dh_ref, wg_ref, wu_ref, wd_ref, middle_ref,
    out_ref, dmlp_ref, own_ref, send_ref, hidt_ref, acc_ref,
):
    t = pl.program_id(0)

    @pl.when(t == 0)
    def _():
        acc_ref[...] = middle_ref[...]
        dmlp_ref[...] = jnp.zeros((N, D), F32)

    mlp_in = mlp_ref[...]
    gate = dot(mlp_in, wg_ref[...])
    up = dot(mlp_in, wu_ref[...])
    d_hidden = dh_ref[...]
    sig = sigmoid(gate)
    act = gate * sig
    hidden = (act * up).astype(BF16)
    d_gate = (d_hidden * up * (sig * (1.0 + gate * (1.0 - sig)))).astype(BF16)
    d_up = (d_hidden * act).astype(BF16)
    acc_ref[...] += dot(hidden, wd_ref[...])
    dmlp_ref[...] += dot(d_gate, wg_ref[...], 1, 1) + dot(d_up, wu_ref[...], 1, 1)
    first = core_ref[40] == 0
    own_ref[...] = jnp.where(first, d_gate, d_up)
    send_ref[...] = jnp.where(first, d_up, d_gate).astype(F32)
    hidt_ref[...] = hidden.T.astype(F32)

    @pl.when(t == TILES - 1)
    def _():
        out_ref[...] = acc_ref[...].astype(BF16)


def mlp(core, mlp_in, d_hidden, upw, dnw, middle):
    full = lambda shape: pl.BlockSpec(shape, lambda t, c: (0,) * len(shape))
    column = lambda rows: pl.BlockSpec((rows, TILE), lambda t, c: (0, t))
    return pl.pallas_call(
        mlp_kernel,
        grid_spec=pltpu.PrefetchScalarGridSpec(
            num_scalar_prefetch=1,
            grid=(TILES,),
            in_specs=[
                full((N, D)), column(N), column(D),
                pl.BlockSpec((D, TILE), lambda t, c: (0, TILES + t)),
                pl.BlockSpec((TILE, D), lambda t, c: (t, 0)), full((N, D)),
            ],
            out_specs=[
                full((N, D)), full((N, D)), column(N), column(N),
                pl.BlockSpec((TILE, N), lambda t, c: (t, 0)),
            ],
            scratch_shapes=[pltpu.VMEM((N, D), F32)],
        ),
        out_shape=[
            jax.ShapeDtypeStruct((N, D), BF16), jax.ShapeDtypeStruct((N, D), F32),
            jax.ShapeDtypeStruct((N, FF), BF16), jax.ShapeDtypeStruct((N, FF), F32),
            jax.ShapeDtypeStruct((FF, N), F32),
        ],
        compiler_params=params(),
        cost_estimate=cost(30),
        name="mlp",
    )(core, mlp_in, d_hidden, upw, upw, dnw, middle)


def down_grad_kernel(
    table_ref, hid_ref, hid_other, cot_ref, cot_other, keep_ref, send_ref, cotb_ref, hidb_ref
):
    @pl.when(pl.program_id(0) == 0)
    def _():
        cotb_ref[:N] = cot_ref[...]
        cotb_ref[N:] = cot_other[...].astype(BF16)

    hidb_ref[:, :N] = hid_ref[...].reshape(TILE, N).astype(BF16)
    hidb_ref[:, N:] = hid_other[...].reshape(TILE, N).astype(BF16)
    down = dot(hidb_ref[...], cotb_ref[...]).reshape(SEQ, 16, 512)
    for slab in range(4):
        slot = table_ref[41 + slab]

        @pl.when(slot < 2)
        def _():
            keep_ref[slot] = down[:, :, slab * 128 : (slab + 1) * 128]

        @pl.when(slot >= 2)
        def _():
            send_ref[slot - 2] = down[:, :, slab * 128 : (slab + 1) * 128]


def down_grad(table, hid, hid_other, cot, cot_other):
    tall = pl.BlockSpec((SEQ, 16, N), lambda t, c: (0, t, 0))
    out = pl.BlockSpec((2, SEQ, 16, 128), lambda t, c: (0, 0, t, 0))
    return pl.pallas_call(
        down_grad_kernel,
        grid_spec=pltpu.PrefetchScalarGridSpec(
            num_scalar_prefetch=1,
            grid=(TILES,),
            in_specs=[
                tall, tall, pl.BlockSpec((N, 512), lambda t, c: (0, c[40])),
                pl.BlockSpec((N, 512), lambda t, c: (0, 0)),
            ],
            out_specs=[out, out],
            scratch_shapes=[pltpu.VMEM((2 * N, 512), BF16), pltpu.VMEM((TILE, 2 * N), BF16)],
        ),
        out_shape=[jax.ShapeDtypeStruct((2, SEQ, 176, 128), F32)] * 2,
        compiler_params=params(),
        cost_estimate=cost(0.1),
        name="down_grad",
    )(table, chunks(hid), chunks(hid_other), cot, cot_other)


def up_grad_kernel(
    table_ref, mlpt_ref, mlpt_other, act_ref, act_other, keep_0, send_0, keep_1, send_1,
    left_ref, right_ref, value_ref,
):
    @pl.when(pl.program_id(0) == 0)
    def _():
        left_ref[:, :N] = mlpt_ref[...].astype(BF16)
        left_ref[:, N:] = mlpt_other[...].astype(BF16)

    right_ref[:N] = act_ref[...]
    right_ref[N:] = act_other[...].astype(BF16)
    value_ref[...] = dot(left_ref[...], right_ref[...])
    for v, (keep_ref, send_ref) in enumerate(((keep_0, send_0), (keep_1, send_1))):
        cols = slice(v * 128, v * 128 + 128)
        for index in range(8):
            keep_ref[index] = value_ref[chunk_rows(table_ref, v, index), cols]
            send_ref[index] = value_ref[chunk_rows(table_ref, v, 8 + index), cols]


def chunk_rows(table_ref, v, index):
    return pl.ds(pl.multiple_of(table_ref[v * 16 + index] * 64, 64), 64)


def up_grad(table, mlpt, mlpt_other, act, act_other):
    full = lambda shape: pl.BlockSpec(shape, lambda t, c: (0,) * len(shape))
    wide = pl.BlockSpec((N, TILE), lambda t, c: (0, t))
    return pl.pallas_call(
        up_grad_kernel,
        grid_spec=pltpu.PrefetchScalarGridSpec(
            num_scalar_prefetch=1,
            grid=(TILES,),
            in_specs=[full((D, N)), full((D, N)), wide, wide],
            out_specs=[pl.BlockSpec((8, 64, 128), lambda t, c: (0, t, 0))] * 4,
            scratch_shapes=[
                pltpu.VMEM((D, 2 * N), BF16), pltpu.VMEM((2 * N, TILE), BF16), pltpu.VMEM((D, TILE), F32),
            ],
        ),
        out_shape=[jax.ShapeDtypeStruct((8, TILES * 64, 128), F32)] * 4,
        compiler_params=params(),
        cost_estimate=cost(0.1),
        name="up_grad",
    )(table, mlpt, mlpt_other, act, act_other)


def back_kernel(
    core_ref, middle_ref, dmlp_ref, cot_ref, mg_ref, ow_ref, hg_ref, heads_ref, og_ref, q_ref, ld_ref, cl_ref,
    dmid_ref, datt_ref, mgg_ref, hgg_ref, dheads_ref, dog_ref, sends_ref, adj_ref, out_ref,
    dmix_ref,
):
    away = pl.ds(pl.multiple_of((1 - core_ref[40]) * 512, 512), 512)
    m = pl.program_id(0)

    @pl.when(m == 0)
    def _():
        mgg_ref[...] = jnp.zeros((1, D), F32)
        hgg_ref[...] = jnp.zeros((1, VHEAD), F32)

    middle = middle_ref[...]
    scale_two = inverse_rms(middle)
    unit_two = middle * scale_two
    grad = dmlp_ref[...]
    mgg_ref[...] += jnp.sum(grad * unit_two, 0, keepdims=True)
    scaled = grad * mg_ref[...].astype(F32)
    d_middle = scale_two * (scaled - unit_two * jnp.mean(scaled * unit_two, -1, keepdims=True))
    d_middle = d_middle + cot_ref[...].astype(F32)
    dmid_ref[...] = d_middle
    datt_ref[...] = d_middle.astype(BF16)
    dmix_ref[...] = dot(datt_ref[...], ow_ref[...], 1, 1)
    block = m + 1 - 2 * lax.rem(m, 2)
    first = lax.rem(m, 2) == 0
    closing = cl_ref[pl.ds(block, 1), :]
    gain = hg_ref[...].astype(F32)
    for head in range(HEADS):
        chan = slice(head * KHEAD, (head + 1) * KHEAD)
        vals = slice(head * VHEAD, (head + 1) * VHEAD)
        out = heads_ref[:, vals]
        scale = inverse_rms(out)
        unit = out * scale
        gate = og_ref[:, vals]
        sig = sigmoid(gate)
        act = gate * sig
        d_mixed = dmix_ref[:, vals]
        dog_ref[:, vals] = (d_mixed * (unit * gain) * (sig * (1.0 + gate * (1.0 - sig)))).astype(BF16)
        d_norm = d_mixed * act
        hgg_ref[...] += jnp.sum(d_norm * unit, 0, keepdims=True)
        scaled = d_norm * gain
        d_out = scale * (scaled - unit * jnp.mean(scaled * unit, -1, keepdims=True))
        dheads_ref[:, vals] = d_out
        adjoint = dot3(d_out, q_ref[:, chan] * jnp.exp(ld_ref[:, chan]), 0, 0)

        @pl.when(first)
        def _():
            adj_ref[0, head] = adjoint

        @pl.when(jnp.logical_not(first))
        def _():
            total = jnp.exp(closing[:, chan]) * adj_ref[0, head] + adjoint
            for half in range(2):
                out_ref[head * 2 + half] = total[half * 128 : (half + 1) * 128]

    sends_ref[:, :512] = datt_ref[:, away].astype(F32)
    sends_ref[:, 512:] = dog_ref[:, away].astype(F32)


def back(core, middle, dmlp, cot, mg, ow, hg, heads, og, q, ld, cl):
    full = lambda shape: pl.BlockSpec(shape, lambda m, c: (0,) * len(shape))
    block = lambda m: m + 1 - 2 * lax.rem(m, 2)
    wide = pl.BlockSpec((BLK, D), lambda m, c: (block(m), 0))
    return pl.pallas_call(
        back_kernel,
        grid_spec=pltpu.PrefetchScalarGridSpec(num_scalar_prefetch=1, grid=(4,), in_specs=[
            wide, wide, wide, full((1, D)), full((VALUE, D)), full((1, VHEAD)),
            pl.BlockSpec((BLK, VALUE), lambda m, c: (block(m), 0)),
            pl.BlockSpec((BLK, VALUE), lambda m, c: (block(m), 0)),
            pl.BlockSpec((BLK, KD), lambda m, c: (block(m), 0)),
            pl.BlockSpec((BLK, KD), lambda m, c: (block(m), 0)),
            full((8, KD)),
        ],
        out_specs=[
            wide, wide, full((1, D)), full((1, VHEAD)),
            pl.BlockSpec((BLK, VALUE), lambda m, c: (block(m), 0)),
            pl.BlockSpec((BLK, VALUE), lambda m, c: (block(m), 0)),
            pl.BlockSpec((BLK, D), lambda m, c: (block(m), 0)),
            pl.BlockSpec((1, HEADS, VHEAD, KHEAD), lambda m, c: (m // 2, 0, 0, 0)),
            pl.BlockSpec((8, 128, KHEAD), lambda m, c: (m // 2, 0, 0)),
        ],
        scratch_shapes=[pltpu.VMEM((BLK, VALUE), F32)]),
        out_shape=[
            jax.ShapeDtypeStruct((N, D), F32), jax.ShapeDtypeStruct((N, D), BF16),
            jax.ShapeDtypeStruct((1, D), F32), jax.ShapeDtypeStruct((1, VHEAD), F32),
            jax.ShapeDtypeStruct((N, VALUE), F32), jax.ShapeDtypeStruct((N, VALUE), BF16),
            jax.ShapeDtypeStruct((N, D), F32),
            jax.ShapeDtypeStruct((ROWS, HEADS, VHEAD, KHEAD), F32),
            jax.ShapeDtypeStruct((SEQ, 128, KHEAD), F32),
        ],
                compiler_params=params(),
        cost_estimate=cost(30),
        name="back",
    )(core, middle, dmlp, cot, mg, ow, hg, heads, og, q, ld, cl)


def inner_kernel(
    limit_ref, core_ref, q_ref, k_ref, v_ref, dout_ref, ld_ref, cl_ref, inc_ref, ret_ref, upd_ref, adj_ref,
    logit_ref, low_ref, gu_ref, normed_ref, hg_ref, mg_ref,
    dproj_ref, dprojs_ref, dlow_ref, pack_ref,
    dlg_ref, gb_ref, gup_ref, gdn_ref,
):
    m = pl.program_id(0)
    row = m // 2
    part = lax.rem(m, 2)
    second = part == 1

    @pl.when(m == 0)
    def _():
        gb_ref[...] = jnp.zeros((1, KD), F32)
        gup_ref[...] = jnp.zeros((16, KD), F32)
        gdn_ref[...] = jnp.zeros((16, D), F32)

    mask = lower((BLK, BLK))
    upper = lax.broadcasted_iota(jnp.int32, (BLK, BLK), 0) <= lax.broadcasted_iota(jnp.int32, (BLK, BLK), 1)
    upper = upper.astype(BF16)
    closing = cl_ref[pl.ds(m, 1), :]
    previous = cl_ref[pl.ds(row * 2, 1), :]
    following = cl_ref[pl.ds(row * 2 + 1, 1), :]
    alive = live(limit_ref, core_ref, row, part * BLK, BLK, VHEAD)
    alive_key = alive[:, :KHEAD]
    for head in range(HEADS):
        chan = slice(head * KHEAD, (head + 1) * KHEAD)
        vals = slice(head * VHEAD, (head + 1) * VHEAD)
        start = inc_ref[0, head]
        start = jnp.where(second, jnp.exp(previous[:, chan]) * start + upd_ref[0, 0, head], start)
        update = jnp.where(second, upd_ref[0, 1, head], upd_ref[0, 0, head])
        end_state = jnp.exp(closing[:, chan]) * start + update
        end_grad = ret_ref[0, head]
        end_grad = jnp.where(second, end_grad, jnp.exp(following[:, chan]) * end_grad + adj_ref[0, head])
        decay = ld_ref[:, chan]
        centre = decay[BLK // 2 - 1 : BLK // 2]
        query = q_ref[:, chan]
        key = k_ref[:, chan]
        value = v_ref[:, vals]
        d_out = dout_ref[:, vals]
        up_factor = jnp.exp(decay - centre)
        down_factor = jnp.exp(centre - decay)
        query_mid = query * up_factor
        key_mid = key * down_factor
        close_factor = jnp.exp(closing[:, chan] - decay)
        scores = jnp.where(mask, dot3(query_mid, key_mid, 1, 1), 0.0)
        d_scores = jnp.where(mask, dot3(d_out, value, 1, 1), 0.0)
        d_query = up_factor * dot3(d_scores, key_mid) + jnp.exp(decay) * dot3(d_out, start)
        d_key = down_factor * dot3(d_scores, query_mid, 0, 0) + close_factor * dot3(value, end_grad)
        d_value = dot3(scores, d_out, 0, 0) + dot3(key * close_factor, end_grad, 1, 1)
        d_decay = query * d_query - key * d_key
        dlg_ref[:, chan] = dot_ones(upper, d_decay) + jnp.sum(end_grad * end_state, 0, keepdims=True)
        dproj_ref[:, chan] = (d_query * KHEAD ** (-0.5)).astype(BF16)
        dproj_ref[:, KD + head * KHEAD : KD + (head + 1) * KHEAD] = (d_key * alive_key).astype(BF16)
        dproj_ref[:, 2 * KD + head * VHEAD : 2 * KD + (head + 1) * VHEAD] = (d_value * alive).astype(BF16)
    alive_gate = live(limit_ref, core_ref, row, part * BLK, BLK, KD)
    d_logit = dlg_ref[...] * alive_gate * (1.0 / (1.0 + jnp.exp(logit_ref[...]))) * (1.0 / 16.0)
    gb_ref[...] += jnp.sum(d_logit, 0, keepdims=True)
    gup_ref[...] += dot3(low_ref[...], d_logit, 0, 0)
    high, rest = split(d_logit)
    d_low = (dot(high, gu_ref[...], 1, 1) + dot(rest, gu_ref[...], 1, 1)).astype(BF16)
    dlow_ref[...] = d_low
    gdn_ref[...] += dot(d_low, normed_ref[...], 0, 0)
    away = pl.ds(pl.multiple_of((1 - core_ref[40]) * 1024, 1024), 1024)
    dprojs_ref[...] = dproj_ref[:, away].astype(F32)

    @pl.when(m == 3)
    def _():
        pack_ref[:, 16:24] = jnp.zeros((SEQ, 8, 128), F32)
        for chunk in range(SEQ):
            pack_ref[chunk, :16, :64] = gdn_ref[:, chunk * 64 : chunk * 64 + 64]
            pack_ref[chunk, :16, 64:96] = gup_ref[:, chunk * 32 : chunk * 32 + 32]
            pack_ref[chunk, :16, 96:] = jnp.zeros((16, 32), F32)
            pack_ref[chunk, 16:17, 64:] = mg_ref[:, chunk * 64 : chunk * 64 + 64]
            pack_ref[chunk, 17:18, :32] = gb_ref[:, chunk * 32 : chunk * 32 + 32]
            pack_ref[chunk, 17:18, 32:48] = hg_ref[:, chunk * 16 : chunk * 16 + 16]


def inner(limit, core, q, k, v, dout, ld, cl, incoming, returned, upd, adj, logit, low, gu, normed, hg, mg):
    full = lambda shape: pl.BlockSpec(shape, lambda m, s, c: (0,) * len(shape))
    by_row = pl.BlockSpec((1, HEADS, VHEAD, KHEAD), lambda m, s, c: (m // 2, 0, 0, 0))
    return pl.pallas_call(
        inner_kernel,
        grid_spec=pltpu.PrefetchScalarGridSpec(
            num_scalar_prefetch=2,
            grid=(4,),
            in_specs=[
                pl.BlockSpec((BLK, KD), lambda m, s, c: (m, 0)), pl.BlockSpec((BLK, KD), lambda m, s, c: (m, 0)),
                pl.BlockSpec((BLK, VALUE), lambda m, s, c: (m, 0)), pl.BlockSpec((BLK, VALUE), lambda m, s, c: (m, 0)),
                pl.BlockSpec((BLK, KD), lambda m, s, c: (m, 0)), full((8, KD)),
                by_row, by_row,
                pl.BlockSpec((1, 2, HEADS, VHEAD, KHEAD), lambda m, s, c: (m // 2, 0, 0, 0, 0)),
                by_row,
                pl.BlockSpec((BLK, KD), lambda m, s, c: (m, 0)), pl.BlockSpec((BLK, 16), lambda m, s, c: (m, 0)),
                full((16, KD)), pl.BlockSpec((BLK, D), lambda m, s, c: (m, 0)), full((1, VHEAD)), full((1, D)),
            ],
            out_specs=[
                pl.BlockSpec((BLK, 2048), lambda m, s, c: (m, 0)),
                pl.BlockSpec((BLK, 1024), lambda m, s, c: (m, 0)), pl.BlockSpec((BLK, 16), lambda m, s, c: (m, 0)),
                full((SEQ, 24, 128)),
            ],
            scratch_shapes=[
                pltpu.VMEM((BLK, KD), F32), pltpu.VMEM((1, KD), F32), pltpu.VMEM((16, KD), F32), pltpu.VMEM((16, D), F32),
            ],
        ),
        out_shape=[
            jax.ShapeDtypeStruct((N, 2048), BF16), jax.ShapeDtypeStruct((N, 1024), F32), jax.ShapeDtypeStruct((N, 16), BF16),
            jax.ShapeDtypeStruct((SEQ, 24, 128), F32),
        ],
        compiler_params=params(),
        cost_estimate=cost(300),
        name="inner",
    )(limit, core, q, k, v, dout, ld, cl, incoming, returned, upd, adj, logit, low, gu, normed, hg, mg)


def outer_kernel(sets, extras, table_ref, *refs):
    count = 4 * len(sets)
    more, outs = refs[count : count + extras], refs[count + extras : -3]
    left_ref, right_ref, value_ref = refs[-3:]
    at = 0
    for which, streams in enumerate(sets):
        x_ref, x_other, y_ref, y_other = refs[4 * which : 4 * which + 4]
        left_ref[:, :N] = x_ref[...].astype(BF16)
        left_ref[:, N:] = x_other[...].astype(BF16)
        for part, v in enumerate(streams):
            cols = slice(part * 512, (part + 1) * 512)
            right_ref[:N] = y_ref[:, cols]
            right_ref[N:] = y_other[:, cols].astype(BF16)
            value_ref[...] = dot(left_ref[...], right_ref[...])
            for side, target in enumerate(outs[2 * at : 2 * at + 2]):
                for index in range(8):
                    rows = chunk_rows(table_ref, v, side * 8 + index)
                    for slab in range(4):
                        target[index, slab * 64 : slab * 64 + 64] = value_ref[rows, slab * 128 : slab * 128 + 128]
                    if extras:
                        own, got, pack = more
                        chunk = table_ref[v * 16 + side * 8 + index]
                        cut = slice(v * 88, v * 88 + 88)
                        target[index, 256:344] = own[chunk, cut] + got[chunk, cut]
                        if v == 1:
                            target[index, 344:368] = pack[chunk]
            at += 1


def outer(table, sets, more=()):
    operands, specs, outs = [], [], []
    for x, x_other, rows, y, y_other, cols, streams in sets:
        width = 512 * len(streams)
        operands += [x, x_other, y, y_other]
        specs += [
            pl.BlockSpec((D, N), lambda i, t, r=rows: (r, 0)), pl.BlockSpec((D, N), lambda i, t, r=rows: (r, 0)),
            pl.BlockSpec((N, width), lambda i, t: (0, t[40])), pl.BlockSpec((N, width), lambda i, t, c=cols: (0, c)),
        ]
        for v in streams:
            total = 256 + (88 + 24 * v if more else 0)
            outs += [jax.ShapeDtypeStruct((8, total, 128), F32)] * 2
    for array in more:
        operands.append(array)
        specs.append(pl.BlockSpec(array.shape, lambda i, t: (0, 0, 0)))
    return pl.pallas_call(
        functools.partial(outer_kernel, [streams for *_, streams in sets], len(more)),
        grid_spec=pltpu.PrefetchScalarGridSpec(
            num_scalar_prefetch=1, grid=(1,), in_specs=specs,
            out_specs=[pl.BlockSpec(out.shape, lambda i, t: (0, 0, 0)) for out in outs],
            scratch_shapes=[
                pltpu.VMEM((D, 2 * N), BF16), pltpu.VMEM((2 * N, 512), BF16), pltpu.VMEM((D, 512), F32),
            ],
        ),
        out_shape=outs,
        compiler_params=params(),
        cost_estimate=cost(0.1),
        name="outer",
    )(table, *operands)


def input_kernel(
    y_ref, og_ref, w_ref, dlow_ref, gd_ref, tok_ref, gain_ref, dmid_ref, pack_in,
    grad_ref, pack_ref, acc_ref,
):
    t = pl.program_id(0)

    @pl.when(t == 0)
    def _():
        acc_ref[...] = dot(dlow_ref[...], gd_ref[...])

    @pl.when(t < 4)
    def _():
        acc_ref[...] += dot(y_ref[...], w_ref[...], 1, 1)

    @pl.when(t >= 4)
    def _():
        acc_ref[...] += dot(og_ref[...], w_ref[...], 1, 1)

    @pl.when(t == 5)
    def _():
        total = jnp.zeros((1, D), F32)
        for at in range(0, N, 128):
            here = slice(at, at + 128)
            inputs = tok_ref[here].astype(F32)
            scale = inverse_rms(inputs)
            unit = inputs * scale
            grad = acc_ref[here]
            total = total + jnp.sum(grad * unit, 0, keepdims=True)
            scaled = grad * gain_ref[...].astype(F32)
            d_inputs = scale * (scaled - unit * jnp.mean(scaled * unit, -1, keepdims=True))
            grad_ref[here] = (dmid_ref[here] + d_inputs).astype(BF16)
        pack_ref[...] = pack_in[...]
        for chunk in range(SEQ):
            pack_ref[chunk, 16:17, :64] = total[:, chunk * 64 : chunk * 64 + 64]


def input_back(y, og, w, dlow, gd, tokens, gain, dmid, pack):
    full = lambda shape: pl.BlockSpec(shape, lambda t: (0,) * len(shape))
    return pl.pallas_call(
        input_kernel,
        grid=(6,),
        in_specs=[
            pl.BlockSpec((N, 512), lambda t: (0, jnp.minimum(t, 3))),
            pl.BlockSpec((N, 512), lambda t: (0, jnp.maximum(t - 4, 0))),
            pl.BlockSpec((D, 512), lambda t: (0, t)),
            full((N, 16)), full((16, D)), full((N, D)), full((1, D)), full((N, D)),
            full((SEQ, 24, 128)),
        ],
        out_specs=[full((N, D)), full((SEQ, 24, 128))],
        out_shape=[
            jax.ShapeDtypeStruct((N, D), BF16), jax.ShapeDtypeStruct((SEQ, 24, 128), F32),
        ],
        scratch_shapes=[pltpu.VMEM((N, D), F32)],
        compiler_params=params(),
        cost_estimate=cost(12),
        name="input_back",
    )(y, og, w, dlow, gd, tokens, gain, dmid, pack)


SWAP = [(i, i ^ 1) for i in range(8)]
FLIP = {0: 1, 1: 3}
XORDER = ((0, 1), (1, 0))
ORDERS = (((0, 1, 2, 3), (1, 0, 3, 2)), ((2, 3, 0, 1), (3, 2, 1, 0)))


def bit_of(seq, which):
    at = seq // 4 if which < 2 else seq % 4
    return at // 2 if which % 2 else int(at in (1, 2))


def chunk_of(order, bits):
    value = dict(zip(order, bits))
    along = [[0, 1, 3, 2][2 * value[2 * a + 1] + value[2 * a]] for a in range(2)]
    return along[0] * 4 + along[1]


def partner(seq, which):
    z, y = seq // 4, seq % 4
    return (z ^ FLIP[which]) * 4 + y if which < 2 else z * 4 + (y ^ FLIP[which - 2])


def tables():
    table = np.zeros((128, 96), np.int32)
    for device in range(128):
        core, seq = (device // 16) % 2, device % 16
        for v in range(2):
            order = ORDERS[v][core]
            chunks = [chunk_of(order, [(i >> 3) & 1, (i >> 2) & 1, (i >> 1) & 1, i & 1]) for i in range(16)]
            mine = [bit_of(seq, which) for which in order]
            table[device, v * 16 : v * 16 + 8] = chunks[mine[0] * 8 : mine[0] * 8 + 8]
            table[device, v * 16 + 8 : v * 16 + 16] = chunks[(1 - mine[0]) * 8 : (1 - mine[0]) * 8 + 8]
            table[device, 32 + v * 4 : 36 + v * 4] = mine
            for slot in range(16):
                table[device, 48 + v * 16 + chunks[slot ^ (8 * mine[0])]] = slot
        table[device, 40] = core
        table[device, 46] = seq
        x, (near, far) = device // 32, XORDER[core]
        for slab in range(4):
            away = bit_of(slab * 4, near) != bit_of(x * 4, near)
            table[device, 41 + slab] = bit_of(slab * 4, far) + 2 * away
        table[device, 45] = bit_of(x * 4, far)
        for who in range(2):
            near, far = XORDER[core ^ who]
            table[device, 80 + 4 * who : 84 + 4 * who] = [x, x ^ FLIP[far], x ^ FLIP[near], x ^ 2]
    return table


TABLE = tables()
STEPS = [
    [
        [(d, (d // 16) * 16 + partner(d % 16, ORDERS[v][(d // 16) % 2][step])) for d in range(128)]
        for step in range(4)
    ]
    for v in range(2)
]
ACROSS = [
    [(i, ((i // 2) ^ FLIP[XORDER[i % 2][step]]) * 2 + i % 2) for i in range(8)] for step in range(2)
]


def exchange(value):
    return lax.all_to_all(value, "seq", 0, 0, tiled=True)


def swap(value):
    return lax.ppermute(value, "dp", SWAP)


def halve_kernel(counts, table_ref, *refs):
    del table_ref
    ins, outs = refs[: 4 * sum(counts)], refs[4 * sum(counts) :]
    at = 0
    for stream, count in enumerate(counts):
        send_ref, keep_ref = outs[2 * stream : 2 * stream + 2]
        row = 0
        for _ in range(count):
            ks_ref, kk_ref, rs_ref, rk_ref = ins[4 * at : 4 * at + 4]
            rows = ks_ref.shape[1]
            send_ref[:, row : row + rows] = ks_ref[...] + rs_ref[...]
            keep_ref[:, row : row + rows] = kk_ref[...] + rk_ref[...]
            row += rows
            at += 1


def halve(table, streams, cut=1):
    operands, specs, outs, out_specs = [], [], [], []
    half = streams[0][1].shape[0] // 2
    size = max(half // 2, 1)
    turns = half // size
    for slot, *pairs in streams:
        total = 0
        for keep, got in zip(pairs[::2], pairs[1::2]):
            rows = keep.shape[1] // cut
            mine = pl.BlockSpec((size, rows, 128), lambda i, j, t, s=slot: (t[s] * turns + i, j, 0))
            theirs = pl.BlockSpec((size, rows, 128), lambda i, j, t, s=slot: ((1 - t[s]) * turns + i, j, 0))
            operands += [keep, keep, got, got]
            specs += [theirs, mine, theirs, mine]
            total += rows
        outs += [jax.ShapeDtypeStruct((half, total * cut, 128), F32)] * 2
        out_specs += [pl.BlockSpec((size, total, 128), lambda i, j, t: (i, j, 0))] * 2
    return pl.pallas_call(
        functools.partial(halve_kernel, [len(stream) // 2 for stream in streams]),
        grid_spec=pltpu.PrefetchScalarGridSpec(
            num_scalar_prefetch=1, grid=(turns, cut), in_specs=specs, out_specs=out_specs
        ),
        out_shape=outs,
        compiler_params=params(),
        cost_estimate=cost(0.1),
        name="halve",
    )(table, *operands)


def hop(v, step, value):
    return lax.ppermute(value, ("dp", "seq"), STEPS[v][step])


def hops(step, sends):
    return [hop(v, step, sends[v]) for v in range(2)]


def onward(table, step, *groups):
    streams = []
    for v in range(2):
        stream = [32 + v * 4 + step]
        for keeps, gots in groups:
            if keeps[v] is not None:
                stream += [keeps[v], gots[v]]
        streams.append(stream)
    send_0, keep_0, send_1, keep_1 = halve(table, streams)
    return (send_0, send_1), (keep_0, keep_1)


def along_x(step, value):
    return lax.ppermute(value, "dp", ACROSS[step])


def after(value, *others):
    return lax.optimization_barrier((value, *others))[0]


def unpack_kernel(
    table_ref, a_ref, a_other, b_ref, b_other,
    up_ref, down_ref, out_ref, in_ref, gd_ref, gu_ref, ng_ref, mg_ref, gb_ref, hg_ref,
):
    core = table_ref[40]

    def place(own_ref, other_ref, at, rows, slabs, target, first, second):
        for slab in range(slabs):
            own = own_ref[at : at + rows]
            other = other_ref[at : at + rows]
            low = jnp.where(core == 0, own, other)
            high = jnp.where(core == 0, other, own)
            target[:, first + slab * 128 : first + (slab + 1) * 128] = low
            target[:, second + slab * 128 : second + (slab + 1) * 128] = high
            at += rows
        return at

    for v in range(2):
        for tile in range(TILES):
            column = tile * TILE + v * 128
            place(a_ref, a_other, (v * TILES + tile) * 64, 64, 1, up_ref, column, FF + column)
    at = place(b_ref, b_other, 0, 64, 4, out_ref, 0, 512)
    at = place(b_ref, b_other, at, 64, 4, in_ref, 2048, 2560)
    at = place(b_ref, b_other, at, 64, 4, in_ref, 0, 1024)
    at = place(b_ref, b_other, at, 64, 4, in_ref, 512, 1536)
    small = b_ref[at : at + 24] + b_other[at : at + 24]
    gd_ref[...] = small[:16, :64]
    gu_ref[...] = small[:16, 64:96]
    ng_ref[...] = small[16:17, :64]
    mg_ref[...] = small[16:17, 64:128]
    gb_ref[...] = small[17:18, :32]
    hg_ref[...] = small[17:18, 32:48]
    for slab in range(4):
        first = at + 24 + slab * 176
        for ref, base, place_of in ((b_ref, core * 512, 80), (b_other, (1 - core) * 512, 84)):
            cols = pl.ds(pl.multiple_of(base + table_ref[place_of + slab] * 128, 128), 128)
            down_ref[:, cols] = ref[first : first + 176]


def unpack(table, a, a_other, b, b_other):
    shapes = [
        (64, 2 * FF), (176, D), (64, D), (64, 3072), (16, 64), (16, 32), (1, 64), (1, 64), (1, 32), (1, 16),
    ]
    return pl.pallas_call(
        unpack_kernel,
        in_specs=[pl.BlockSpec(memory_space=pltpu.SMEM)] + [pl.BlockSpec(memory_space=pltpu.VMEM)] * 4,
        out_specs=[pl.BlockSpec(memory_space=pltpu.VMEM)] * len(shapes),
        out_shape=[jax.ShapeDtypeStruct(shape, F32) for shape in shapes],
        compiler_params=params(),
        cost_estimate=cost(4),
        name="unpack",
    )(table, a, a_other, b, b_other)


def chunks(value):
    return value.reshape(SEQ, value.shape[0] // SEQ, value.shape[1])


def shards(
    tokens, lengths, cotangent, norm_gain, in_weight, gate_down, gate_up, gate_bias, head_gain,
    out_weight, mlp_gain, up_weight, down_weight,
):
    device = lax.axis_index("dp") * SEQ + lax.axis_index("seq")
    table = lax.dynamic_slice(jnp.asarray(TABLE), (device, 0), (1, 96)).reshape(96)
    tok = tokens.reshape(N, D)
    cot = cotangent.reshape(N, D)
    line = lambda vector: vector.reshape(1, -1)
    flat = lambda value: value.reshape(2, -1, 128)

    down_t, up_t = gate_down.T, gate_up.T
    k, v, normed, ld, cl, logit, low, upd, pieces = project(
        lengths, table, tok, line(norm_gain), in_weight, down_t, up_t, line(gate_bias)
    )
    gathered = exchange(pieces)
    q, og, normed_t, cot_send = project_rest(table, after(normed, pieces), in_weight, cot)
    incoming = prefix(after(gathered, q), gathered, False)
    normed_other, cot_other = swap(after(normed_t, incoming)), swap(after(cot_send, incoming))
    within = local(after(q, incoming), k, v, ld)
    d_hidden = hidden_grad(after(cot, within), down_weight)
    incoming = after(exchange(incoming), d_hidden).reshape(ROWS, HEADS, VHEAD, KHEAD)
    heads, middle, mlp_in, joint = attend(
        q, og, ld, within, cl, incoming, upd, tok, out_weight, line(head_gain), line(mlp_gain)
    )
    output, dmlp, act, act_send, hidden_t = mlp(
        table, after(mlp_in, normed_other, cot_other), d_hidden, up_weight, down_weight, middle
    )
    hidden_other, act_other, joint_other = swap(hidden_t), swap(act_send), swap(joint)
    dmid, datt, g_mlp_gain, g_head_gain, dheads, dog, sends, adj, pieces_back = back(
        table, middle, dmlp, cot, line(mlp_gain), out_weight, line(head_gain), heads, og, q, ld, cl
    )
    sends_other = swap(sends)
    owned = exchange(pieces_back)
    dn_keep, dn_send = down_grad(table, after(hidden_t, pieces_back), hidden_other, cot, cot_other)
    dn_got = along_x(0, after(flat(dn_send), owned))
    owned = prefix(after(owned, dn_keep), gathered, True)
    returned = exchange(owned)
    up_0, up_send_0, up_1, up_send_1 = up_grad(
        table, after(joint, owned, sends_other), joint_other, act, act_other
    )
    up_gots = hops(0, (after(up_send_0, returned), after(up_send_1, returned)))
    keep_o, send_o, keep_g, send_g = outer(
        after(table, up_0),
        [
            (joint, joint_other, 1, datt, sends_other, 0, (0,)),
            (normed_t, normed_other, 0, dog, sends_other, 1, (1,)),
        ],
    )
    four_got = hops(0, (send_o, send_g))
    dn_send, dn_keep = halve(table, [(45, after(flat(dn_keep), keep_o), dn_got)], 4)
    dn_got = along_x(1, dn_send)
    returned = after(returned, dn_keep).reshape(ROWS, HEADS, VHEAD, KHEAD)
    dproj, dproj_send, dlow, pack = inner(
        lengths, table, q, k, v, dheads, ld, cl, incoming, returned, upd, adj, logit, low, up_t, normed,
        g_head_gain, g_mlp_gain,
    )
    input_grad, pack = input_back(
        dproj, dog, in_weight, dlow, down_t, tok, line(norm_gain), dmid, pack
    )
    dproj_got = swap(after(dproj_send, dn_got, pack, *up_gots, *four_got))
    up_sends, up_keeps = onward(table, 1, ((after(up_0, pack), up_1), up_gots))
    up_gots = hops(1, up_sends)
    by_chunk = lambda value: value.reshape(SEQ, -1, 128)
    keep_p, send_p, keep_r, send_r = outer(
        after(table, up_keeps[0]),
        [(normed_t, normed_other, 0, dproj, dproj_got, 0, (0, 1))],
        (by_chunk(dn_keep), by_chunk(dn_got), pack),
    )
    sends = hops(0, (send_p, send_r))
    up_sends, up_keeps = onward(table, 2, ((after(up_keeps[0], keep_p), up_keeps[1]), up_gots))
    up_gots = hops(2, up_sends)
    sends, keeps = onward(
        table, 1, ((after(keep_o, up_keeps[0]), keep_g), four_got), ((keep_p, keep_r), sends)
    )
    gots = hops(1, sends)
    up_sends, up_keeps = onward(table, 3, ((after(up_keeps[0], keeps[0]), up_keeps[1]), up_gots))
    up_gots = hops(3, up_sends)
    sends, keeps = onward(table, 2, ((after(keeps[0], up_keeps[0]), keeps[1]), gots))
    gots = hops(2, sends)
    early = jnp.concatenate([(up_keeps[v] + up_gots[v])[0] for v in range(2)], 0)
    early = early + along_x(0, early)
    sends, keeps = onward(table, 3, ((after(keeps[0], early), keeps[1]), gots))
    gots = hops(3, sends)
    early = early + along_x(1, early)
    first, second = [(keeps[v] + gots[v])[0] for v in range(2)]
    late = jnp.concatenate([first[:256], second[:256], first[256:512], second[256:512], second[600:]], 0)
    slab = jnp.concatenate([first[512:], second[512:600]], 0)
    got = along_x(1, jnp.concatenate([late, slab], 0))
    early_other = swap(early)
    late = jnp.concatenate([late + got[:1048], slab, got[1048:]], 0)
    got = along_x(0, late)
    late = jnp.concatenate([late[:1048] + got[:1048], late[1048:], got[1048:]], 0)
    grad_up, grad_down, grad_out, grad_in, g_down, g_upf, g_norm, g_mlp, g_bias, g_head = unpack(
        table, early, early_other, late, swap(late)
    )
    return (
        output.reshape(ROWS, SEG, D),
        input_grad.reshape(ROWS, SEG, D),
        g_norm.reshape(64),
        grad_in,
        g_down.T,
        g_upf.T,
        g_bias.reshape(32),
        g_head.reshape(16),
        grad_out,
        g_mlp.reshape(64),
        grad_up,
        grad_down,
    )


def solution(mesh):
    rows = P("dp", "seq", None)
    return jax.shard_map(
        shards,
        mesh=mesh,
        in_specs=(rows, P("dp"), rows) + (P(),) * 10,
        out_specs=(
            rows, rows, P("seq"), P("seq", None), P("seq", None), P("seq", None), P("seq"), P("seq"),
            P("seq", None), P("seq"), P("seq", None), P("seq", None),
        ),
        check_vma=False,
    )
```

```python
import functools

import jax
import jax.numpy as jnp
import numpy as np
from jax import lax
from jax.experimental import pallas as pl
from jax.experimental.pallas import tpu as pltpu
from jax.sharding import PartitionSpec as P

F32 = jnp.float32
BF16 = jnp.bfloat16
D = 1024
FF = 2816
HEADS = 4
KHEAD = 128
VHEAD = 256
KD = 512
VALUE = 1024
ROWS = 2
SEG = 256
BLK = 128
N = ROWS * SEG
SEQ = 16
TILE = 256
EPSILON = 1e-06
VMEM_LIMIT = 64 * 1024 * 1024


def params(**kw):
    return pltpu.CompilerParams(vmem_limit_bytes=VMEM_LIMIT, **kw)


def cost(us):
    return pl.CostEstimate(flops=0, bytes_accessed=int(us * 3e6), transcendentals=0)


def dot(a, b, ca=1, cb=0):
    return lax.dot_general(a, b, (((ca,), (cb,)), ((), ())), preferred_element_type=F32)


def split(a):
    high = a.astype(BF16)
    return high, (a - high.astype(F32)).astype(BF16)


def dot3(a, b, ca=1, cb=0):
    ah, al = split(a)
    bh, bl = split(b)
    return dot(ah, bh, ca, cb) + (dot(ah, bl, ca, cb) + dot(al, bh, ca, cb))


def dot_ones(ones, b, ca=1, cb=0):
    high = b.astype(BF16)
    rest = b - high.astype(F32)
    mid = rest.astype(BF16)
    low = (rest - mid.astype(F32)).astype(BF16)
    return dot(ones, high, ca, cb) + (dot(ones, mid, ca, cb) + dot(ones, low, ca, cb))


def sigmoid(u):
    return 1.0 / (1.0 + jnp.exp(-u))


def inverse_rms(u):
    return lax.rsqrt(jnp.mean(u * u, -1, keepdims=True) + EPSILON)


def live(lengths_ref, table_ref, row, first, count, width):
    where = lax.broadcasted_iota(jnp.int32, (count, width), 0) + (first + table_ref[46] * SEG)
    return (where < lengths_ref[row]).astype(F32)


def lower(shape):
    return lax.broadcasted_iota(jnp.int32, shape, 0) >= lax.broadcasted_iota(jnp.int32, shape, 1)


def proj_kernel(
    lengths_ref, table_ref, tok_ref, gain_ref, w_ref, gd_ref, gu_ref, gb_ref,
    k_ref, v_ref, normed_ref, ld_ref, cl_ref, logit_ref, low_ref, upd_ref, out_ref,
    kc_ref,
):
    n = pl.program_id(0)

    @pl.when(n == 0)
    def _():
        inputs = tok_ref[...].astype(F32)
        normed = (inputs * inverse_rms(inputs) * gain_ref[...].astype(F32)).astype(BF16)
        normed_ref[...] = normed
        low = dot(normed, gd_ref[...], 1, 1)
        low_ref[...] = low
        low_high, low_low = split(low)
        logit = dot(low_high, gu_ref[...]) + dot(low_low, gu_ref[...])
        logit = logit + gb_ref[...].astype(F32)
        logit_ref[...] = logit
        ones = lower((BLK, BLK)).astype(BF16)
        key = dot(normed, w_ref[...])
        for row in range(ROWS):
            for part in range(SEG // BLK):
                at = row * SEG + part * BLK
                here = slice(at, at + BLK)
                alive = live(lengths_ref, table_ref, row, part * BLK, BLK, KD)
                u = logit[here]
                log_gate = (jnp.minimum(u, 0.0) - jnp.log1p(jnp.exp(-jnp.abs(u)))) * (1.0 / 16.0)
                decay = dot_ones(ones, log_gate * alive)
                ld_ref[here] = decay
                m = row * (SEG // BLK) + part
                closing = decay[BLK - 1 : BLK]
                cl_ref[m : m + 1] = closing
                k_ref[here] = key[here] * alive
                kc_ref[here] = key[here] * alive * jnp.exp(closing - decay)
        cl_ref[4:8] = jnp.zeros((4, KD), F32)

    for step in (1, 2):

        @pl.when(n == step)
        def _():
            acc = dot(normed_ref[...], w_ref[...])
            for row in range(ROWS):
                values = []
                for part in range(SEG // BLK):
                    at = row * SEG + part * BLK
                    value = acc[at : at + BLK] * live(lengths_ref, table_ref, row, part * BLK, BLK, KD)
                    v_ref[at : at + BLK] = value
                    values.append(value)
                for sub in range(2):
                    head = (step - 1) * 2 + sub
                    chan = slice(head * KHEAD, (head + 1) * KHEAD)
                    total = None
                    for part in range(SEG // BLK):
                        at = row * SEG + part * BLK
                        m = row * (SEG // BLK) + part
                        update = dot3(
                            values[part][:, sub * VHEAD : (sub + 1) * VHEAD],
                            kc_ref[at : at + BLK, chan], 0, 0,
                        )
                        upd_ref[row, part, head] = update
                        if total is None:
                            total = update
                        else:
                            total = jnp.exp(cl_ref[m : m + 1, chan]) * total + update
                    base = row * (SEG // BLK)
                    gone = cl_ref[base : base + 1, chan] + cl_ref[base + 1 : base + 2, chan]
                    for half in range(2):
                        piece = (row * HEADS + head) * 2 + half
                        out_ref[piece, 0:128] = total[half * 128 : (half + 1) * 128]
                        out_ref[piece, 128:136] = jnp.broadcast_to(gone, (8, KHEAD))


def project(lengths, table, tokens, gain, w, gd, gu, gb):
    full = lambda shape: pl.BlockSpec(shape, lambda n, s, c: (0,) * len(shape))
    return pl.pallas_call(
        proj_kernel,
        grid_spec=pltpu.PrefetchScalarGridSpec(
            num_scalar_prefetch=2,
            grid=(3,),
            in_specs=[
                full((N, D)), full((1, D)), pl.BlockSpec((D, KD), lambda n, s, c: (0, n + 1)),
                full((16, D)), full((16, KD)), full((1, KD)),
            ],
            out_specs=[
                full((N, KD)), pl.BlockSpec((N, KD), lambda n, s, c: (0, jnp.maximum(n - 1, 0))),
                full((N, D)), full((N, KD)), full((8, KD)),
                full((N, KD)), full((N, 16)), full((ROWS, 2, HEADS, VHEAD, KHEAD)),
                full((SEQ, 136, KHEAD)),
            ],
            scratch_shapes=[pltpu.VMEM((N, KD), F32)],
        ),
        out_shape=[
            jax.ShapeDtypeStruct((N, KD), F32), jax.ShapeDtypeStruct((N, VALUE), F32),
            jax.ShapeDtypeStruct((N, D), BF16),
            jax.ShapeDtypeStruct((N, KD), F32), jax.ShapeDtypeStruct((8, KD), F32),
            jax.ShapeDtypeStruct((N, KD), F32), jax.ShapeDtypeStruct((N, 16), F32),
            jax.ShapeDtypeStruct((ROWS, 2, HEADS, VHEAD, KHEAD), F32),
            jax.ShapeDtypeStruct((SEQ, 136, KHEAD), F32),
        ],
        compiler_params=params(),
        cost_estimate=cost(10),
        name="project",
    )(lengths, table, tokens, gain, w, gd, gu, gb)


def rest_kernel(table_ref, normed_ref, w_ref, cot_ref, q_ref, og_ref, normt_ref, cots_ref):
    n = pl.program_id(0)
    acc = dot(normed_ref[...], w_ref[...])

    @pl.when(n == 0)
    def _():
        q_ref[...] = acc * KHEAD ** (-0.5)
        normt_ref[...] = normed_ref[...].T.astype(F32)

    @pl.when(n > 0)
    def _():
        og_ref[...] = acc

    @pl.when(n == 2)
    def _():
        cots_ref[...] = cot_ref[:, pl.ds(pl.multiple_of((1 - table_ref[40]) * 512, 512), 512)].astype(F32)


def project_rest(table, normed, w, cot):
    full = lambda shape: pl.BlockSpec(shape, lambda n, c: (0,) * len(shape))
    return pl.pallas_call(
        rest_kernel,
        grid_spec=pltpu.PrefetchScalarGridSpec(
            num_scalar_prefetch=1,
            grid=(3,),
            in_specs=[
                full((N, D)), pl.BlockSpec((D, KD), lambda n, c: (0, jnp.where(n == 0, 0, n + 3))), full((N, D)),
            ],
            out_specs=[
                full((N, KD)), pl.BlockSpec((N, KD), lambda n, c: (0, jnp.maximum(n - 1, 0))),
                full((D, N)), full((N, KD)),
            ],
        ),
        out_shape=[
            jax.ShapeDtypeStruct((N, KD), F32), jax.ShapeDtypeStruct((N, VALUE), F32),
            jax.ShapeDtypeStruct((D, N), F32), jax.ShapeDtypeStruct((N, KD), F32),
        ],
        compiler_params=params(),
        cost_estimate=cost(0.1),
        name="project_rest",
    )(table, normed, w, cot)


def local_kernel(q_ref, k_ref, v_ref, ld_ref, out_ref):
    mask = lower((BLK, BLK))
    for head in range(HEADS):
        chan = slice(head * KHEAD, (head + 1) * KHEAD)
        vals = slice(head * VHEAD, (head + 1) * VHEAD)
        decay = ld_ref[:, chan]
        centre = decay[BLK // 2 - 1 : BLK // 2]
        scores = dot3(q_ref[:, chan] * jnp.exp(decay - centre), k_ref[:, chan] * jnp.exp(centre - decay), 1, 1)
        out_ref[:, vals] = dot3(jnp.where(mask, scores, 0.0), v_ref[:, vals])


def local(q, k, v, ld):
    rows = lambda width: pl.BlockSpec((BLK, width), lambda m: (m, 0))
    return pl.pallas_call(
        local_kernel,
        grid=(4,),
        in_specs=[rows(KD), rows(KD), rows(VALUE), rows(KD)],
        out_specs=rows(VALUE),
        out_shape=jax.ShapeDtypeStruct((N, VALUE), F32),
        compiler_params=params(),
        cost_estimate=cost(0.1),
        name="local",
    )(q, k, v, ld)


def hidden_kernel(cot_ref, wd_ref, out_ref):
    out_ref[...] = dot(cot_ref[...], wd_ref[...], 1, 1)


def hidden_grad(cot, dnw):
    return pl.pallas_call(
        hidden_kernel,
        grid=(2,),
        in_specs=[pl.BlockSpec((N, D), lambda t: (0, 0)), pl.BlockSpec((FF // 2, D), lambda t: (t, 0))],
        out_specs=pl.BlockSpec((N, FF // 2), lambda t: (0, t)),
        out_shape=jax.ShapeDtypeStruct((N, FF), F32),
        compiler_params=params(),
        cost_estimate=cost(0.1),
        name="hidden_grad",
    )(cot, dnw)


def prefix_kernel(backward, part_ref, decay_ref, out_ref):
    run = jnp.zeros((128, KHEAD), F32)
    order = range(SEQ - 1, -1, -1) if backward else range(SEQ)
    for seg in order:
        out_ref[seg] = run
        run = jnp.exp(decay_ref[seg, 0:1]) * run + part_ref[seg, 0:128]


def prefix(parts, decays, backward):
    return pl.pallas_call(
        functools.partial(prefix_kernel, backward),
        grid=(1,),
        in_specs=[
            pl.BlockSpec((SEQ, 128, KHEAD), lambda n: (0, 0, 0)),
            pl.BlockSpec((SEQ, 8, KHEAD), lambda n: (0, 16, 0)),
        ],
        out_specs=pl.BlockSpec((SEQ, 128, KHEAD), lambda n: (0, 0, 0)),
        out_shape=jax.ShapeDtypeStruct((SEQ, 128, KHEAD), F32),
        compiler_params=params(),
        cost_estimate=cost(0.1),
        name="prefix",
    )(parts, decays)


def attend_kernel(
    q_ref, og_ref, ld_ref, within_ref, cl_ref, inc_ref, upd_ref, tok_ref, ow_ref, hg_ref, mg_ref,
    heads_ref, middle_ref, mlp_ref, both_ref,
    mixed_ref,
):
    m = pl.program_id(0)
    second = lax.rem(m, 2) == 1
    previous = cl_ref[pl.ds(m - lax.rem(m, 2), 1), :]
    gain = hg_ref[...].astype(F32)
    for head in range(HEADS):
        chan = slice(head * KHEAD, (head + 1) * KHEAD)
        vals = slice(head * VHEAD, (head + 1) * VHEAD)
        start = inc_ref[0, head]
        start = jnp.where(second, jnp.exp(previous[:, chan]) * start + upd_ref[0, 0, head], start)
        out = within_ref[:, vals] + dot3(q_ref[:, chan] * jnp.exp(ld_ref[:, chan]), start, 1, 1)
        heads_ref[:, vals] = out
        gate = og_ref[:, vals]
        mixed = out * inverse_rms(out) * gain * (gate * sigmoid(gate))
        mixed_ref[:, vals] = mixed.astype(BF16)

    middle = tok_ref[...].astype(F32) + dot(mixed_ref[...], ow_ref[...])
    middle_ref[...] = middle
    mlp_in = (middle * inverse_rms(middle) * mg_ref[...].astype(F32)).astype(BF16)
    mlp_ref[...] = mlp_in
    both_ref[:D] = mlp_in.T.astype(F32)
    both_ref[D:] = mixed_ref[...].T.astype(F32)


def attend(q, og, ld, within, cl, incoming, upd, tokens, ow, hg, mg):
    full = lambda shape: pl.BlockSpec(shape, lambda m: (0,) * len(shape))
    rows = lambda width: pl.BlockSpec((BLK, width), lambda m: (m, 0))
    return pl.pallas_call(
        attend_kernel,
        grid=(4,),
        in_specs=[
            rows(KD), rows(VALUE), rows(KD), rows(VALUE), full((8, KD)),
            pl.BlockSpec((1, HEADS, VHEAD, KHEAD), lambda m: (m // 2, 0, 0, 0)),
            pl.BlockSpec((1, 1, HEADS, VHEAD, KHEAD), lambda m: (m // 2, 0, 0, 0, 0)),
            rows(D), full((VALUE, D)), full((1, VHEAD)), full((1, D)),
        ],
        out_specs=[
            rows(VALUE), rows(D), rows(D), pl.BlockSpec((D + VALUE, BLK), lambda m: (0, m)),
        ],
        out_shape=[
            jax.ShapeDtypeStruct((N, VALUE), F32), jax.ShapeDtypeStruct((N, D), F32),
            jax.ShapeDtypeStruct((N, D), BF16), jax.ShapeDtypeStruct((D + VALUE, N), F32),
        ],
        scratch_shapes=[pltpu.VMEM((BLK, VALUE), BF16)],
        compiler_params=params(),
        cost_estimate=cost(13),
        name="attend",
    )(q, og, ld, within, cl, incoming, upd, tokens, ow, hg, mg)


TILES = FF // TILE


def mlp_kernel(
    core_ref, mlp_ref, dh_ref, wg_ref, wu_ref, wd_ref, middle_ref,
    out_ref, dmlp_ref, own_ref, send_ref, hidt_ref, acc_ref,
):
    t = pl.program_id(0)

    @pl.when(t == 0)
    def _():
        acc_ref[...] = middle_ref[...]
        dmlp_ref[...] = jnp.zeros((N, D), F32)

    mlp_in = mlp_ref[...]
    gate = dot(mlp_in, wg_ref[...])
    up = dot(mlp_in, wu_ref[...])
    d_hidden = dh_ref[...]
    sig = sigmoid(gate)
    act = gate * sig
    hidden = (act * up).astype(BF16)
    d_gate = (d_hidden * up * (sig * (1.0 + gate * (1.0 - sig)))).astype(BF16)
    d_up = (d_hidden * act).astype(BF16)
    acc_ref[...] += dot(hidden, wd_ref[...])
    dmlp_ref[...] += dot(d_gate, wg_ref[...], 1, 1) + dot(d_up, wu_ref[...], 1, 1)
    first = core_ref[40] == 0
    own_ref[...] = jnp.where(first, d_gate, d_up)
    send_ref[...] = jnp.where(first, d_up, d_gate).astype(F32)
    hidt_ref[...] = hidden.T.astype(F32)

    @pl.when(t == TILES - 1)
    def _():
        out_ref[...] = acc_ref[...].astype(BF16)


def mlp(core, mlp_in, d_hidden, upw, dnw, middle):
    full = lambda shape: pl.BlockSpec(shape, lambda t, c: (0,) * len(shape))
    column = lambda rows: pl.BlockSpec((rows, TILE), lambda t, c: (0, t))
    return pl.pallas_call(
        mlp_kernel,
        grid_spec=pltpu.PrefetchScalarGridSpec(
            num_scalar_prefetch=1,
            grid=(TILES,),
            in_specs=[
                full((N, D)), column(N), column(D),
                pl.BlockSpec((D, TILE), lambda t, c: (0, TILES + t)),
                pl.BlockSpec((TILE, D), lambda t, c: (t, 0)), full((N, D)),
            ],
            out_specs=[
                full((N, D)), full((N, D)), column(N), column(N),
                pl.BlockSpec((TILE, N), lambda t, c: (t, 0)),
            ],
            scratch_shapes=[pltpu.VMEM((N, D), F32)],
        ),
        out_shape=[
            jax.ShapeDtypeStruct((N, D), BF16), jax.ShapeDtypeStruct((N, D), F32),
            jax.ShapeDtypeStruct((N, FF), BF16), jax.ShapeDtypeStruct((N, FF), F32),
            jax.ShapeDtypeStruct((FF, N), F32),
        ],
        compiler_params=params(),
        cost_estimate=cost(30),
        name="mlp",
    )(core, mlp_in, d_hidden, upw, upw, dnw, middle)


def down_grad_kernel(
    table_ref, hid_ref, hid_other, cot_ref, cot_other, keep_ref, send_ref, cotb_ref, hidb_ref
):
    @pl.when(pl.program_id(0) == 0)
    def _():
        cotb_ref[:N] = cot_ref[...]
        cotb_ref[N:] = cot_other[...].astype(BF16)

    hidb_ref[:, :N] = hid_ref[...].reshape(TILE, N).astype(BF16)
    hidb_ref[:, N:] = hid_other[...].reshape(TILE, N).astype(BF16)
    down = dot(hidb_ref[...], cotb_ref[...]).reshape(SEQ, 16, 512)
    for slab in range(4):
        slot = table_ref[41 + slab]

        @pl.when(slot < 2)
        def _():
            keep_ref[slot] = down[:, :, slab * 128 : (slab + 1) * 128]

        @pl.when(slot >= 2)
        def _():
            send_ref[slot - 2] = down[:, :, slab * 128 : (slab + 1) * 128]


def down_grad(table, hid, hid_other, cot, cot_other):
    tall = pl.BlockSpec((SEQ, 16, N), lambda t, c: (0, t, 0))
    out = pl.BlockSpec((2, SEQ, 16, 128), lambda t, c: (0, 0, t, 0))
    return pl.pallas_call(
        down_grad_kernel,
        grid_spec=pltpu.PrefetchScalarGridSpec(
            num_scalar_prefetch=1,
            grid=(TILES,),
            in_specs=[
                tall, tall, pl.BlockSpec((N, 512), lambda t, c: (0, c[40])),
                pl.BlockSpec((N, 512), lambda t, c: (0, 0)),
            ],
            out_specs=[out, out],
            scratch_shapes=[pltpu.VMEM((2 * N, 512), BF16), pltpu.VMEM((TILE, 2 * N), BF16)],
        ),
        out_shape=[jax.ShapeDtypeStruct((2, SEQ, 176, 128), F32)] * 2,
        compiler_params=params(),
        cost_estimate=cost(0.1),
        name="down_grad",
    )(table, chunks(hid), chunks(hid_other), cot, cot_other)


def up_grad_kernel(
    table_ref, mlpt_ref, mlpt_other, act_ref, act_other, keep_0, send_0, keep_1, send_1,
    left_ref, right_ref, value_ref,
):
    @pl.when(pl.program_id(0) == 0)
    def _():
        left_ref[:, :N] = mlpt_ref[...].astype(BF16)
        left_ref[:, N:] = mlpt_other[...].astype(BF16)

    right_ref[:N] = act_ref[...]
    right_ref[N:] = act_other[...].astype(BF16)
    value_ref[...] = dot(left_ref[...], right_ref[...])
    for v, (keep_ref, send_ref) in enumerate(((keep_0, send_0), (keep_1, send_1))):
        cols = slice(v * 128, v * 128 + 128)
        for index in range(8):
            keep_ref[index] = value_ref[chunk_rows(table_ref, v, index), cols]
            send_ref[index] = value_ref[chunk_rows(table_ref, v, 8 + index), cols]


def chunk_rows(table_ref, v, index):
    return pl.ds(pl.multiple_of(table_ref[v * 16 + index] * 64, 64), 64)


def up_grad(table, mlpt, mlpt_other, act, act_other):
    full = lambda shape: pl.BlockSpec(shape, lambda t, c: (0,) * len(shape))
    wide = pl.BlockSpec((N, TILE), lambda t, c: (0, t))
    return pl.pallas_call(
        up_grad_kernel,
        grid_spec=pltpu.PrefetchScalarGridSpec(
            num_scalar_prefetch=1,
            grid=(TILES,),
            in_specs=[full((D, N)), full((D, N)), wide, wide],
            out_specs=[pl.BlockSpec((8, 64, 128), lambda t, c: (0, t, 0))] * 4,
            scratch_shapes=[
                pltpu.VMEM((D, 2 * N), BF16), pltpu.VMEM((2 * N, TILE), BF16), pltpu.VMEM((D, TILE), F32),
            ],
        ),
        out_shape=[jax.ShapeDtypeStruct((8, TILES * 64, 128), F32)] * 4,
        compiler_params=params(),
        cost_estimate=cost(0.1),
        name="up_grad",
    )(table, mlpt, mlpt_other, act, act_other)


def back_kernel(
    core_ref, middle_ref, dmlp_ref, cot_ref, mg_ref, ow_ref, hg_ref, heads_ref, og_ref, q_ref, ld_ref, cl_ref,
    dmid_ref, datt_ref, mgg_ref, hgg_ref, dheads_ref, dog_ref, sends_ref, adj_ref, out_ref,
    dmix_ref,
):
    away = pl.ds(pl.multiple_of((1 - core_ref[40]) * 512, 512), 512)
    m = pl.program_id(0)

    @pl.when(m == 0)
    def _():
        mgg_ref[...] = jnp.zeros((1, D), F32)
        hgg_ref[...] = jnp.zeros((1, VHEAD), F32)

    middle = middle_ref[...]
    scale_two = inverse_rms(middle)
    unit_two = middle * scale_two
    grad = dmlp_ref[...]
    mgg_ref[...] += jnp.sum(grad * unit_two, 0, keepdims=True)
    scaled = grad * mg_ref[...].astype(F32)
    d_middle = scale_two * (scaled - unit_two * jnp.mean(scaled * unit_two, -1, keepdims=True))
    d_middle = d_middle + cot_ref[...].astype(F32)
    dmid_ref[...] = d_middle
    datt_ref[...] = d_middle.astype(BF16)
    dmix_ref[...] = dot(datt_ref[...], ow_ref[...], 1, 1)
    block = m + 1 - 2 * lax.rem(m, 2)
    first = lax.rem(m, 2) == 0
    closing = cl_ref[pl.ds(block, 1), :]
    gain = hg_ref[...].astype(F32)
    for head in range(HEADS):
        chan = slice(head * KHEAD, (head + 1) * KHEAD)
        vals = slice(head * VHEAD, (head + 1) * VHEAD)
        out = heads_ref[:, vals]
        scale = inverse_rms(out)
        unit = out * scale
        gate = og_ref[:, vals]
        sig = sigmoid(gate)
        act = gate * sig
        d_mixed = dmix_ref[:, vals]
        dog_ref[:, vals] = (d_mixed * (unit * gain) * (sig * (1.0 + gate * (1.0 - sig)))).astype(BF16)
        d_norm = d_mixed * act
        hgg_ref[...] += jnp.sum(d_norm * unit, 0, keepdims=True)
        scaled = d_norm * gain
        d_out = scale * (scaled - unit * jnp.mean(scaled * unit, -1, keepdims=True))
        dheads_ref[:, vals] = d_out
        adjoint = dot3(d_out, q_ref[:, chan] * jnp.exp(ld_ref[:, chan]), 0, 0)

        @pl.when(first)
        def _():
            adj_ref[0, head] = adjoint

        @pl.when(jnp.logical_not(first))
        def _():
            total = jnp.exp(closing[:, chan]) * adj_ref[0, head] + adjoint
            for half in range(2):
                out_ref[head * 2 + half] = total[half * 128 : (half + 1) * 128]

    sends_ref[:, :512] = datt_ref[:, away].astype(F32)
    sends_ref[:, 512:] = dog_ref[:, away].astype(F32)


def back(core, middle, dmlp, cot, mg, ow, hg, heads, og, q, ld, cl):
    full = lambda shape: pl.BlockSpec(shape, lambda m, c: (0,) * len(shape))
    block = lambda m: m + 1 - 2 * lax.rem(m, 2)
    wide = pl.BlockSpec((BLK, D), lambda m, c: (block(m), 0))
    return pl.pallas_call(
        back_kernel,
        grid_spec=pltpu.PrefetchScalarGridSpec(num_scalar_prefetch=1, grid=(4,), in_specs=[
            wide, wide, wide, full((1, D)), full((VALUE, D)), full((1, VHEAD)),
            pl.BlockSpec((BLK, VALUE), lambda m, c: (block(m), 0)),
            pl.BlockSpec((BLK, VALUE), lambda m, c: (block(m), 0)),
            pl.BlockSpec((BLK, KD), lambda m, c: (block(m), 0)),
            pl.BlockSpec((BLK, KD), lambda m, c: (block(m), 0)),
            full((8, KD)),
        ],
        out_specs=[
            wide, wide, full((1, D)), full((1, VHEAD)),
            pl.BlockSpec((BLK, VALUE), lambda m, c: (block(m), 0)),
            pl.BlockSpec((BLK, VALUE), lambda m, c: (block(m), 0)),
            pl.BlockSpec((BLK, D), lambda m, c: (block(m), 0)),
            pl.BlockSpec((1, HEADS, VHEAD, KHEAD), lambda m, c: (m // 2, 0, 0, 0)),
            pl.BlockSpec((8, 128, KHEAD), lambda m, c: (m // 2, 0, 0)),
        ],
        scratch_shapes=[pltpu.VMEM((BLK, VALUE), F32)]),
        out_shape=[
            jax.ShapeDtypeStruct((N, D), F32), jax.ShapeDtypeStruct((N, D), BF16),
            jax.ShapeDtypeStruct((1, D), F32), jax.ShapeDtypeStruct((1, VHEAD), F32),
            jax.ShapeDtypeStruct((N, VALUE), F32), jax.ShapeDtypeStruct((N, VALUE), BF16),
            jax.ShapeDtypeStruct((N, D), F32),
            jax.ShapeDtypeStruct((ROWS, HEADS, VHEAD, KHEAD), F32),
            jax.ShapeDtypeStruct((SEQ, 128, KHEAD), F32),
        ],
                compiler_params=params(),
        cost_estimate=cost(30),
        name="back",
    )(core, middle, dmlp, cot, mg, ow, hg, heads, og, q, ld, cl)


def inner_kernel(
    limit_ref, core_ref, q_ref, k_ref, v_ref, dout_ref, ld_ref, cl_ref, inc_ref, ret_ref, upd_ref, adj_ref,
    logit_ref, low_ref, gu_ref, normed_ref, hg_ref, mg_ref,
    dproj_ref, dprojs_ref, dlow_ref, pack_ref,
    dlg_ref, gb_ref, gup_ref, gdn_ref,
):
    m = pl.program_id(0)
    row = m // 2
    part = lax.rem(m, 2)
    second = part == 1

    @pl.when(m == 0)
    def _():
        gb_ref[...] = jnp.zeros((1, KD), F32)
        gup_ref[...] = jnp.zeros((16, KD), F32)
        gdn_ref[...] = jnp.zeros((16, D), F32)

    mask = lower((BLK, BLK))
    upper = lax.broadcasted_iota(jnp.int32, (BLK, BLK), 0) <= lax.broadcasted_iota(jnp.int32, (BLK, BLK), 1)
    upper = upper.astype(BF16)
    closing = cl_ref[pl.ds(m, 1), :]
    previous = cl_ref[pl.ds(row * 2, 1), :]
    following = cl_ref[pl.ds(row * 2 + 1, 1), :]
    alive = live(limit_ref, core_ref, row, part * BLK, BLK, VHEAD)
    alive_key = alive[:, :KHEAD]
    for head in range(HEADS):
        chan = slice(head * KHEAD, (head + 1) * KHEAD)
        vals = slice(head * VHEAD, (head + 1) * VHEAD)
        start = inc_ref[0, head]
        start = jnp.where(second, jnp.exp(previous[:, chan]) * start + upd_ref[0, 0, head], start)
        update = jnp.where(second, upd_ref[0, 1, head], upd_ref[0, 0, head])
        end_state = jnp.exp(closing[:, chan]) * start + update
        end_grad = ret_ref[0, head]
        end_grad = jnp.where(second, end_grad, jnp.exp(following[:, chan]) * end_grad + adj_ref[0, head])
        decay = ld_ref[:, chan]
        centre = decay[BLK // 2 - 1 : BLK // 2]
        query = q_ref[:, chan]
        key = k_ref[:, chan]
        value = v_ref[:, vals]
        d_out = dout_ref[:, vals]
        up_factor = jnp.exp(decay - centre)
        down_factor = jnp.exp(centre - decay)
        query_mid = query * up_factor
        key_mid = key * down_factor
        close_factor = jnp.exp(closing[:, chan] - decay)
        scores = jnp.where(mask, dot3(query_mid, key_mid, 1, 1), 0.0)
        d_scores = jnp.where(mask, dot3(d_out, value, 1, 1), 0.0)
        d_query = up_factor * dot3(d_scores, key_mid) + jnp.exp(decay) * dot3(d_out, start)
        d_key = down_factor * dot3(d_scores, query_mid, 0, 0) + close_factor * dot3(value, end_grad)
        d_value = dot3(scores, d_out, 0, 0) + dot3(key * close_factor, end_grad, 1, 1)
        d_decay = query * d_query - key * d_key
        dlg_ref[:, chan] = dot_ones(upper, d_decay) + jnp.sum(end_grad * end_state, 0, keepdims=True)
        dproj_ref[:, chan] = (d_query * KHEAD ** (-0.5)).astype(BF16)
        dproj_ref[:, KD + head * KHEAD : KD + (head + 1) * KHEAD] = (d_key * alive_key).astype(BF16)
        dproj_ref[:, 2 * KD + head * VHEAD : 2 * KD + (head + 1) * VHEAD] = (d_value * alive).astype(BF16)
    alive_gate = live(limit_ref, core_ref, row, part * BLK, BLK, KD)
    d_logit = dlg_ref[...] * alive_gate * (1.0 / (1.0 + jnp.exp(logit_ref[...]))) * (1.0 / 16.0)
    gb_ref[...] += jnp.sum(d_logit, 0, keepdims=True)
    gup_ref[...] += dot3(low_ref[...], d_logit, 0, 0)
    high, rest = split(d_logit)
    d_low = (dot(high, gu_ref[...], 1, 1) + dot(rest, gu_ref[...], 1, 1)).astype(BF16)
    dlow_ref[...] = d_low
    gdn_ref[...] += dot(d_low, normed_ref[...], 0, 0)
    away = pl.ds(pl.multiple_of((1 - core_ref[40]) * 1024, 1024), 1024)
    dprojs_ref[...] = dproj_ref[:, away].astype(F32)

    @pl.when(m == 3)
    def _():
        pack_ref[:, 16:24] = jnp.zeros((SEQ, 8, 128), F32)
        for chunk in range(SEQ):
            pack_ref[chunk, :16, :64] = gdn_ref[:, chunk * 64 : chunk * 64 + 64]
            pack_ref[chunk, :16, 64:96] = gup_ref[:, chunk * 32 : chunk * 32 + 32]
            pack_ref[chunk, :16, 96:] = jnp.zeros((16, 32), F32)
            pack_ref[chunk, 16:17, 64:] = mg_ref[:, chunk * 64 : chunk * 64 + 64]
            pack_ref[chunk, 17:18, :32] = gb_ref[:, chunk * 32 : chunk * 32 + 32]
            pack_ref[chunk, 17:18, 32:48] = hg_ref[:, chunk * 16 : chunk * 16 + 16]


def inner(limit, core, q, k, v, dout, ld, cl, incoming, returned, upd, adj, logit, low, gu, normed, hg, mg):
    full = lambda shape: pl.BlockSpec(shape, lambda m, s, c: (0,) * len(shape))
    by_row = pl.BlockSpec((1, HEADS, VHEAD, KHEAD), lambda m, s, c: (m // 2, 0, 0, 0))
    return pl.pallas_call(
        inner_kernel,
        grid_spec=pltpu.PrefetchScalarGridSpec(
            num_scalar_prefetch=2,
            grid=(4,),
            in_specs=[
                pl.BlockSpec((BLK, KD), lambda m, s, c: (m, 0)), pl.BlockSpec((BLK, KD), lambda m, s, c: (m, 0)),
                pl.BlockSpec((BLK, VALUE), lambda m, s, c: (m, 0)), pl.BlockSpec((BLK, VALUE), lambda m, s, c: (m, 0)),
                pl.BlockSpec((BLK, KD), lambda m, s, c: (m, 0)), full((8, KD)),
                by_row, by_row,
                pl.BlockSpec((1, 2, HEADS, VHEAD, KHEAD), lambda m, s, c: (m // 2, 0, 0, 0, 0)),
                by_row,
                pl.BlockSpec((BLK, KD), lambda m, s, c: (m, 0)), pl.BlockSpec((BLK, 16), lambda m, s, c: (m, 0)),
                full((16, KD)), pl.BlockSpec((BLK, D), lambda m, s, c: (m, 0)), full((1, VHEAD)), full((1, D)),
            ],
            out_specs=[
                pl.BlockSpec((BLK, 2048), lambda m, s, c: (m, 0)),
                pl.BlockSpec((BLK, 1024), lambda m, s, c: (m, 0)), pl.BlockSpec((BLK, 16), lambda m, s, c: (m, 0)),
                full((SEQ, 24, 128)),
            ],
            scratch_shapes=[
                pltpu.VMEM((BLK, KD), F32), pltpu.VMEM((1, KD), F32), pltpu.VMEM((16, KD), F32), pltpu.VMEM((16, D), F32),
            ],
        ),
        out_shape=[
            jax.ShapeDtypeStruct((N, 2048), BF16), jax.ShapeDtypeStruct((N, 1024), F32), jax.ShapeDtypeStruct((N, 16), BF16),
            jax.ShapeDtypeStruct((SEQ, 24, 128), F32),
        ],
        compiler_params=params(),
        cost_estimate=cost(300),
        name="inner",
    )(limit, core, q, k, v, dout, ld, cl, incoming, returned, upd, adj, logit, low, gu, normed, hg, mg)


def outer_kernel(sets, extras, table_ref, *refs):
    count = 4 * len(sets)
    more, outs = refs[count : count + extras], refs[count + extras : -3]
    left_ref, right_ref, value_ref = refs[-3:]
    at = 0
    for which, streams in enumerate(sets):
        x_ref, x_other, y_ref, y_other = refs[4 * which : 4 * which + 4]
        left_ref[:, :N] = x_ref[...].astype(BF16)
        left_ref[:, N:] = x_other[...].astype(BF16)
        for part, v in enumerate(streams):
            cols = slice(part * 512, (part + 1) * 512)
            right_ref[:N] = y_ref[:, cols]
            right_ref[N:] = y_other[:, cols].astype(BF16)
            value_ref[...] = dot(left_ref[...], right_ref[...])
            for side, target in enumerate(outs[2 * at : 2 * at + 2]):
                for index in range(8):
                    rows = chunk_rows(table_ref, v, side * 8 + index)
                    for slab in range(4):
                        target[index, slab * 64 : slab * 64 + 64] = value_ref[rows, slab * 128 : slab * 128 + 128]
                    if extras:
                        own, first, got, pack = more
                        chunk = table_ref[v * 16 + side * 8 + index]
                        cut = slice(v * 88, v * 88 + 88)
                        target[index, 256:344] = own[0, chunk, cut] + first[0, chunk, cut] + got[chunk, cut]
                        if v == 1:
                            target[index, 344:368] = pack[chunk]
            at += 1


def outer(table, sets, more=()):
    operands, specs, outs = [], [], []
    for x, x_other, rows, y, y_other, cols, streams in sets:
        width = 512 * len(streams)
        operands += [x, x_other, y, y_other]
        specs += [
            pl.BlockSpec((D, N), lambda i, t, r=rows: (r, 0)), pl.BlockSpec((D, N), lambda i, t, r=rows: (r, 0)),
            pl.BlockSpec((N, width), lambda i, t: (0, t[40])), pl.BlockSpec((N, width), lambda i, t, c=cols: (0, c)),
        ]
        for v in streams:
            total = 256 + (88 + 24 * v if more else 0)
            outs += [jax.ShapeDtypeStruct((8, total, 128), F32)] * 2
    for array in more:
        operands.append(array)
        if array.ndim == 4:
            specs.append(pl.BlockSpec((1,) + array.shape[1:], lambda i, t: (t[45], 0, 0, 0)))
        else:
            specs.append(pl.BlockSpec(array.shape, lambda i, t: (0, 0, 0)))
    return pl.pallas_call(
        functools.partial(outer_kernel, [streams for *_, streams in sets], len(more)),
        grid_spec=pltpu.PrefetchScalarGridSpec(
            num_scalar_prefetch=1, grid=(1,), in_specs=specs,
            out_specs=[pl.BlockSpec(out.shape, lambda i, t: (0, 0, 0)) for out in outs],
            scratch_shapes=[
                pltpu.VMEM((D, 2 * N), BF16), pltpu.VMEM((2 * N, 512), BF16), pltpu.VMEM((D, 512), F32),
            ],
        ),
        out_shape=outs,
        compiler_params=params(),
        cost_estimate=cost(0.1),
        name="outer",
    )(table, *operands)


def input_kernel(
    y_ref, og_ref, w_ref, dlow_ref, gd_ref, tok_ref, gain_ref, dmid_ref, pack_in,
    grad_ref, pack_ref, acc_ref,
):
    t = pl.program_id(0)

    @pl.when(t == 0)
    def _():
        acc_ref[...] = dot(dlow_ref[...], gd_ref[...])

    @pl.when(t < 4)
    def _():
        acc_ref[...] += dot(y_ref[...], w_ref[...], 1, 1)

    @pl.when(t >= 4)
    def _():
        acc_ref[...] += dot(og_ref[...], w_ref[...], 1, 1)

    @pl.when(t == 5)
    def _():
        total = jnp.zeros((1, D), F32)
        for at in range(0, N, 128):
            here = slice(at, at + 128)
            inputs = tok_ref[here].astype(F32)
            scale = inverse_rms(inputs)
            unit = inputs * scale
            grad = acc_ref[here]
            total = total + jnp.sum(grad * unit, 0, keepdims=True)
            scaled = grad * gain_ref[...].astype(F32)
            d_inputs = scale * (scaled - unit * jnp.mean(scaled * unit, -1, keepdims=True))
            grad_ref[here] = (dmid_ref[here] + d_inputs).astype(BF16)
        pack_ref[...] = pack_in[...]
        for chunk in range(SEQ):
            pack_ref[chunk, 16:17, :64] = total[:, chunk * 64 : chunk * 64 + 64]


def input_back(y, og, w, dlow, gd, tokens, gain, dmid, pack):
    full = lambda shape: pl.BlockSpec(shape, lambda t: (0,) * len(shape))
    return pl.pallas_call(
        input_kernel,
        grid=(6,),
        in_specs=[
            pl.BlockSpec((N, 512), lambda t: (0, jnp.minimum(t, 3))),
            pl.BlockSpec((N, 512), lambda t: (0, jnp.maximum(t - 4, 0))),
            pl.BlockSpec((D, 512), lambda t: (0, t)),
            full((N, 16)), full((16, D)), full((N, D)), full((1, D)), full((N, D)),
            full((SEQ, 24, 128)),
        ],
        out_specs=[full((N, D)), full((SEQ, 24, 128))],
        out_shape=[
            jax.ShapeDtypeStruct((N, D), BF16), jax.ShapeDtypeStruct((SEQ, 24, 128), F32),
        ],
        scratch_shapes=[pltpu.VMEM((N, D), F32)],
        compiler_params=params(),
        cost_estimate=cost(12),
        name="input_back",
    )(y, og, w, dlow, gd, tokens, gain, dmid, pack)


SWAP = [(i, i ^ 1) for i in range(8)]
FLIP = {0: 1, 1: 3}
XORDER = ((0, 1), (1, 0))
ORDERS = (((0, 1, 2, 3), (1, 0, 3, 2)), ((2, 3, 0, 1), (3, 2, 1, 0)))


def bit_of(seq, which):
    at = seq // 4 if which < 2 else seq % 4
    return at // 2 if which % 2 else int(at in (1, 2))


def chunk_of(order, bits):
    value = dict(zip(order, bits))
    along = [[0, 1, 3, 2][2 * value[2 * a + 1] + value[2 * a]] for a in range(2)]
    return along[0] * 4 + along[1]


def partner(seq, which):
    z, y = seq // 4, seq % 4
    return (z ^ FLIP[which]) * 4 + y if which < 2 else z * 4 + (y ^ FLIP[which - 2])


def tables():
    table = np.zeros((128, 96), np.int32)
    for device in range(128):
        core, seq = (device // 16) % 2, device % 16
        for v in range(2):
            order = ORDERS[v][core]
            chunks = [chunk_of(order, [(i >> 3) & 1, (i >> 2) & 1, (i >> 1) & 1, i & 1]) for i in range(16)]
            mine = [bit_of(seq, which) for which in order]
            table[device, v * 16 : v * 16 + 8] = chunks[mine[0] * 8 : mine[0] * 8 + 8]
            table[device, v * 16 + 8 : v * 16 + 16] = chunks[(1 - mine[0]) * 8 : (1 - mine[0]) * 8 + 8]
            table[device, 32 + v * 4 : 36 + v * 4] = mine
            for slot in range(16):
                table[device, 48 + v * 16 + chunks[slot ^ (8 * mine[0])]] = slot
        table[device, 40] = core
        table[device, 46] = seq
        x, (near, far) = device // 32, XORDER[core]
        for slab in range(4):
            away = bit_of(slab * 4, near) != bit_of(x * 4, near)
            table[device, 41 + slab] = bit_of(slab * 4, far) + 2 * away
        table[device, 45] = bit_of(x * 4, far)
        for who in range(2):
            near, far = XORDER[core ^ who]
            table[device, 80 + 4 * who : 84 + 4 * who] = [x, x ^ FLIP[far], x ^ FLIP[near], x ^ 2]
    return table


TABLE = tables()
STEPS = [
    [
        [(d, (d // 16) * 16 + partner(d % 16, ORDERS[v][(d // 16) % 2][step])) for d in range(128)]
        for step in range(4)
    ]
    for v in range(2)
]
ACROSS = [
    [(i, ((i // 2) ^ FLIP[XORDER[i % 2][step]]) * 2 + i % 2) for i in range(8)] for step in range(2)
]


def exchange(value):
    return lax.all_to_all(value, "seq", 0, 0, tiled=True)


def swap(value):
    return lax.ppermute(value, "dp", SWAP)


def halve_x_kernel(table_ref, k_ref, r_ref, send_ref):
    del table_ref
    send_ref[...] = k_ref[...] + r_ref[...]


def halve_x(table, keep, got):
    rows = keep.shape[1] // 2
    theirs = pl.BlockSpec((1, rows, 128), lambda j, t: (1 - t[45], j, 0))
    return pl.pallas_call(
        halve_x_kernel,
        grid_spec=pltpu.PrefetchScalarGridSpec(
            num_scalar_prefetch=1, grid=(2,), in_specs=[theirs, theirs],
            out_specs=pl.BlockSpec((1, rows, 128), lambda j, t: (0, j, 0)),
        ),
        out_shape=jax.ShapeDtypeStruct((1, 2 * rows, 128), F32),
        compiler_params=params(),
        cost_estimate=cost(0.1),
        name="halve_x",
    )(table, keep, got)


def halve_kernel(shapes, moves, table_ref, *refs):
    del table_ref
    ins = list(refs)
    at = 0
    values = []
    for groups, later in shapes:
        row, parts = 0, []
        rests = ins[at + 2 * groups : at + 2 * groups + later]
        for group in range(groups):
            k_ref, r_ref = ins[at + 2 * group : at + 2 * group + 2]
            parts.append((row, row + k_ref.shape[1], k_ref, r_ref))
            row += k_ref.shape[1]
        values.append((parts, rests))
        at += 2 * groups + later
    for v, first, count, out, place in moves:
        out_ref = ins[at + out]
        for low, high, k_ref, r_ref in values[v][0]:
            start, stop = max(first, low), min(first + count, high)
            if start >= stop:
                continue
            total = k_ref[:, start - low : stop - low] + r_ref[:, start - low : stop - low]
            for rest in values[v][1]:
                total = total + rest[:, start:stop]
            out_ref[:, place + start - first : place + stop - first] = total


def halve(table, step, streams, moves=None):
    size = 2 if step < 3 else 1
    turns = 2 if step == 1 else 1
    operands, specs, shapes, totals = [], [], [], []
    for v, (groups, later) in enumerate(streams):
        bit = lambda t, n, v=v: t[32 + v * 4 + n]

        def block(i, t, bit=bit):
            if step == 1:
                return (1 - bit(t, 1)) * 2 + i
            if step == 2:
                return bit(t, 1) * 2 + 1 - bit(t, 2)
            last = 1 - bit(t, 3) if step == 3 else bit(t, 3)
            return bit(t, 1) * 4 + bit(t, 2) * 2 + last

        total = 0
        for pair in groups:
            for array in pair:
                operands.append(array)
                specs.append(pl.BlockSpec((size, array.shape[1], 128), lambda i, t, f=block: (f(i, t), 0, 0)))
            total += pair[0].shape[1]
        for array in later:
            operands.append(array)
            count = array.shape[0] // size
            specs.append(
                pl.BlockSpec((size, total, 128), lambda i, t, f=block, c=count: (lax.rem(f(i, t), c), 0, 0))
            )
        shapes.append((len(groups), len(later)))
        totals.append(total)
    if moves is None:
        moves = [(v, 0, totals[v], v, 0) for v in range(2)]
        outs = [(size * turns, total) for total in totals]
    else:
        outs = [(1, sum(totals))]
    return pl.pallas_call(
        functools.partial(halve_kernel, shapes, moves),
        grid_spec=pltpu.PrefetchScalarGridSpec(
            num_scalar_prefetch=1, grid=(turns,), in_specs=specs,
            out_specs=[pl.BlockSpec((size, rows, 128), lambda i, t: (i, 0, 0)) for _, rows in outs],
        ),
        out_shape=[jax.ShapeDtypeStruct((count, rows, 128), F32) for count, rows in outs],
        compiler_params=params(),
        cost_estimate=cost(0.1),
        name="halve",
    )(table, *operands)


def hop(v, step, value):
    return lax.ppermute(value, ("dp", "seq"), STEPS[v][step])


def hops(step, sends):
    return [hop(v, step, sends[v]) for v in range(2)]


def along_x(step, value):
    return lax.ppermute(value, "dp", ACROSS[step])


def after(value, *others):
    return lax.optimization_barrier((value, *others))[0]


def unpack_kernel(
    table_ref, a_ref, a_other, b_ref, b_other,
    up_ref, down_ref, out_ref, in_ref, gd_ref, gu_ref, ng_ref, mg_ref, gb_ref, hg_ref,
):
    core = table_ref[40]

    def place(own_ref, other_ref, at, rows, slabs, target, first, second):
        for slab in range(slabs):
            own = own_ref[at : at + rows]
            other = other_ref[at : at + rows]
            low = jnp.where(core == 0, own, other)
            high = jnp.where(core == 0, other, own)
            target[:, first + slab * 128 : first + (slab + 1) * 128] = low
            target[:, second + slab * 128 : second + (slab + 1) * 128] = high
            at += rows
        return at

    for v in range(2):
        for tile in range(TILES):
            column = tile * TILE + v * 128
            place(a_ref, a_other, (v * TILES + tile) * 64, 64, 1, up_ref, column, FF + column)
    at = place(b_ref, b_other, 0, 64, 4, out_ref, 0, 512)
    at = place(b_ref, b_other, at, 64, 4, in_ref, 2048, 2560)
    at = place(b_ref, b_other, at, 64, 4, in_ref, 0, 1024)
    at = place(b_ref, b_other, at, 64, 4, in_ref, 512, 1536)
    small = b_ref[at : at + 24] + b_other[at : at + 24]
    gd_ref[...] = small[:16, :64]
    gu_ref[...] = small[:16, 64:96]
    ng_ref[...] = small[16:17, :64]
    mg_ref[...] = small[16:17, 64:128]
    gb_ref[...] = small[17:18, :32]
    hg_ref[...] = small[17:18, 32:48]
    for slab in range(4):
        first = at + 24 + slab * 176
        for ref, base, place_of in ((b_ref, core * 512, 80), (b_other, (1 - core) * 512, 84)):
            cols = pl.ds(pl.multiple_of(base + table_ref[place_of + slab] * 128, 128), 128)
            down_ref[:, cols] = ref[first : first + 176]


def unpack(table, a, a_other, b, b_other):
    shapes = [
        (64, 2 * FF), (176, D), (64, D), (64, 3072), (16, 64), (16, 32), (1, 64), (1, 64), (1, 32), (1, 16),
    ]
    return pl.pallas_call(
        unpack_kernel,
        in_specs=[pl.BlockSpec(memory_space=pltpu.SMEM)] + [pl.BlockSpec(memory_space=pltpu.VMEM)] * 4,
        out_specs=[pl.BlockSpec(memory_space=pltpu.VMEM)] * len(shapes),
        out_shape=[jax.ShapeDtypeStruct(shape, F32) for shape in shapes],
        compiler_params=params(),
        cost_estimate=cost(4),
        name="unpack",
    )(table, a, a_other, b, b_other)


def chunks(value):
    return value.reshape(SEQ, value.shape[0] // SEQ, value.shape[1])


def shards(
    tokens, lengths, cotangent, norm_gain, in_weight, gate_down, gate_up, gate_bias, head_gain,
    out_weight, mlp_gain, up_weight, down_weight,
):
    device = lax.axis_index("dp") * SEQ + lax.axis_index("seq")
    table = lax.dynamic_slice(jnp.asarray(TABLE), (device, 0), (1, 96)).reshape(96)
    tok = tokens.reshape(N, D)
    cot = cotangent.reshape(N, D)
    line = lambda vector: vector.reshape(1, -1)
    flat = lambda value: value.reshape(2, -1, 128)

    down_t, up_t = gate_down.T, gate_up.T
    k, v, normed, ld, cl, logit, low, upd, pieces = project(
        lengths, table, tok, line(norm_gain), in_weight, down_t, up_t, line(gate_bias)
    )
    gathered = exchange(pieces)
    q, og, normed_t, cot_send = project_rest(table, after(normed, pieces), in_weight, cot)
    incoming = prefix(after(gathered, q), gathered, False)
    normed_other, cot_other = swap(after(normed_t, incoming)), swap(after(cot_send, incoming))
    within = local(after(q, incoming), k, v, ld)
    d_hidden = hidden_grad(after(cot, within), down_weight)
    incoming = after(exchange(incoming), d_hidden).reshape(ROWS, HEADS, VHEAD, KHEAD)
    heads, middle, mlp_in, joint = attend(
        q, og, ld, within, cl, incoming, upd, tok, out_weight, line(head_gain), line(mlp_gain)
    )
    output, dmlp, act, act_send, hidden_t = mlp(
        table, after(mlp_in, normed_other, cot_other), d_hidden, up_weight, down_weight, middle
    )
    hidden_other, act_other, joint_other = swap(hidden_t), swap(act_send), swap(joint)
    dmid, datt, g_mlp_gain, g_head_gain, dheads, dog, sends, adj, pieces_back = back(
        table, middle, dmlp, cot, line(mlp_gain), out_weight, line(head_gain), heads, og, q, ld, cl
    )
    sends_other = swap(sends)
    owned = exchange(pieces_back)
    dn_keep, dn_send = down_grad(table, after(hidden_t, pieces_back), hidden_other, cot, cot_other)
    dn_got = along_x(0, after(flat(dn_send), owned))
    owned = prefix(after(owned, dn_keep), gathered, True)
    returned = exchange(owned)
    up_0, up_send_0, up_1, up_send_1 = up_grad(
        table, after(joint, owned, sends_other), joint_other, act, act_other
    )
    up_gots = hops(0, (after(up_send_0, returned), after(up_send_1, returned)))
    keep_o, send_o, keep_g, send_g = outer(
        after(table, up_0),
        [
            (joint, joint_other, 1, datt, sends_other, 0, (0,)),
            (normed_t, normed_other, 0, dog, sends_other, 1, (1,)),
        ],
    )
    four_got = hops(0, (send_o, send_g))
    dn_first = dn_got
    dn_send = halve_x(table, after(flat(dn_keep), keep_o), dn_first)
    dn_got = along_x(1, dn_send)
    returned = after(returned, dn_send).reshape(ROWS, HEADS, VHEAD, KHEAD)
    dproj, dproj_send, dlow, pack = inner(
        lengths, table, q, k, v, dheads, ld, cl, incoming, returned, upd, adj, logit, low, up_t, normed,
        g_head_gain, g_mlp_gain,
    )
    input_grad, pack = input_back(
        dproj, dog, in_weight, dlow, down_t, tok, line(norm_gain), dmid, pack
    )
    dproj_got = swap(after(dproj_send, dn_got, pack, *up_gots, *four_got))
    up = [([(after(up_0, pack), up_gots[0])], []), ([(up_1, up_gots[1])], [])]
    up_sends = halve(table, 1, up)
    up_gots = hops(1, up_sends)
    keep_p, send_p, keep_r, send_r = outer(
        after(table, up_sends[0]),
        [(normed_t, normed_other, 0, dproj, dproj_got, 0, (0, 1))],
        (dn_keep, dn_first.reshape(dn_keep.shape), dn_got.reshape(SEQ, 176, 128), pack),
    )
    first = hops(0, (send_p, send_r))
    add = lambda streams, gots: [(groups, later + [got]) for (groups, later), got in zip(streams, gots)]
    up = add([([(after(up_0, keep_p), up[0][0][0][1])], []), up[1]], up_gots)
    up_sends = halve(table, 2, up)
    up_gots = hops(2, up_sends)
    rest = [
        ([(after(keep_o, up_sends[0]), four_got[0]), (keep_p, first[0])], []),
        ([(keep_g, four_got[1]), (keep_r, first[1])], []),
    ]
    sends = halve(table, 1, rest)
    gots = hops(1, sends)
    up = add(up, up_gots)
    up_sends = halve(after(table, sends[0]), 3, up)
    up_gots = hops(3, up_sends)
    rest = add(rest, gots)
    sends = halve(after(table, up_sends[0]), 2, rest)
    gots = hops(2, sends)
    (early,) = halve(table, 4, add(up, up_gots), [(0, 0, 704, 0, 0), (1, 0, 704, 0, 704)])
    early = early[0]
    early = early + along_x(0, early)
    rest = add(rest, gots)
    sends = halve(after(table, early), 3, rest)
    gots = hops(3, sends)
    early = early + along_x(1, early)
    (late,) = halve(
        table, 4, add(rest, gots),
        [
            (0, 0, 256, 0, 0), (1, 0, 256, 0, 256), (0, 256, 256, 0, 512), (1, 256, 256, 0, 768),
            (1, 600, 24, 0, 1024), (0, 512, 88, 0, 1048), (1, 512, 88, 0, 1136),
        ],
    )
    late = late[0]
    got = along_x(1, late)
    early_other = swap(early)
    late = jnp.concatenate([late[:1048] + got[:1048], late[1048:], got[1048:]], 0)
    got = along_x(0, late)
    late = jnp.concatenate([late[:1048] + got[:1048], late[1048:], got[1048:]], 0)
    grad_up, grad_down, grad_out, grad_in, g_down, g_upf, g_norm, g_mlp, g_bias, g_head = unpack(
        table, early, early_other, late, swap(late)
    )
    return (
        output.reshape(ROWS, SEG, D),
        input_grad.reshape(ROWS, SEG, D),
        g_norm.reshape(64),
        grad_in,
        g_down.T,
        g_upf.T,
        g_bias.reshape(32),
        g_head.reshape(16),
        grad_out,
        g_mlp.reshape(64),
        grad_up,
        grad_down,
    )


def solution(mesh):
    rows = P("dp", "seq", None)
    return jax.shard_map(
        shards,
        mesh=mesh,
        in_specs=(rows, P("dp"), rows) + (P(),) * 10,
        out_specs=(
            rows, rows, P("seq"), P("seq", None), P("seq", None), P("seq", None), P("seq"), P("seq"),
            P("seq", None), P("seq"), P("seq", None), P("seq", None),
        ),
        check_vma=False,
    )
```

```python
import functools

import jax
import jax.numpy as jnp
import numpy as np
from jax import lax
from jax.experimental import pallas as pl
from jax.experimental.pallas import tpu as pltpu
from jax.sharding import PartitionSpec as P

F32 = jnp.float32
BF16 = jnp.bfloat16
D = 1024
FF = 2816
HEADS = 4
KHEAD = 128
VHEAD = 256
KD = 512
VALUE = 1024
ROWS = 2
SEG = 256
BLK = 128
N = ROWS * SEG
SEQ = 16
TILE = 256
EPSILON = 1e-06
VMEM_LIMIT = 64 * 1024 * 1024


def params(**kw):
    return pltpu.CompilerParams(vmem_limit_bytes=VMEM_LIMIT, **kw)


def cost(us):
    return pl.CostEstimate(flops=0, bytes_accessed=int(us * 3e6), transcendentals=0)


def dot(a, b, ca=1, cb=0):
    return lax.dot_general(a, b, (((ca,), (cb,)), ((), ())), preferred_element_type=F32)


def split(a):
    high = a.astype(BF16)
    return high, (a - high.astype(F32)).astype(BF16)


def dot3(a, b, ca=1, cb=0):
    ah, al = split(a)
    bh, bl = split(b)
    return dot(ah, bh, ca, cb) + (dot(ah, bl, ca, cb) + dot(al, bh, ca, cb))


def dot_ones(ones, b, ca=1, cb=0):
    high = b.astype(BF16)
    rest = b - high.astype(F32)
    mid = rest.astype(BF16)
    low = (rest - mid.astype(F32)).astype(BF16)
    return dot(ones, high, ca, cb) + (dot(ones, mid, ca, cb) + dot(ones, low, ca, cb))


def sigmoid(u):
    return 1.0 / (1.0 + jnp.exp(-u))


def inverse_rms(u):
    return lax.rsqrt(jnp.mean(u * u, -1, keepdims=True) + EPSILON)


def live(lengths_ref, table_ref, row, first, count, width):
    where = lax.broadcasted_iota(jnp.int32, (count, width), 0) + (first + table_ref[46] * SEG)
    return (where < lengths_ref[row]).astype(F32)


def lower(shape):
    return lax.broadcasted_iota(jnp.int32, shape, 0) >= lax.broadcasted_iota(jnp.int32, shape, 1)


def proj_kernel(
    lengths_ref, table_ref, tok_ref, gain_ref, w_ref, gd_ref, gu_ref, gb_ref,
    k_ref, v_ref, normed_ref, ld_ref, cl_ref, logit_ref, low_ref, upd_ref, out_ref,
    kc_ref,
):
    n = pl.program_id(0)

    @pl.when(n == 0)
    def _():
        inputs = tok_ref[...].astype(F32)
        normed = (inputs * inverse_rms(inputs) * gain_ref[...].astype(F32)).astype(BF16)
        normed_ref[...] = normed
        low = dot(normed, gd_ref[...], 1, 1)
        low_ref[...] = low
        low_high, low_low = split(low)
        logit = dot(low_high, gu_ref[...]) + dot(low_low, gu_ref[...])
        logit = logit + gb_ref[...].astype(F32)
        logit_ref[...] = logit
        ones = lower((BLK, BLK)).astype(BF16)
        key = dot(normed, w_ref[...])
        for row in range(ROWS):
            for part in range(SEG // BLK):
                at = row * SEG + part * BLK
                here = slice(at, at + BLK)
                alive = live(lengths_ref, table_ref, row, part * BLK, BLK, KD)
                u = logit[here]
                log_gate = (jnp.minimum(u, 0.0) - jnp.log1p(jnp.exp(-jnp.abs(u)))) * (1.0 / 16.0)
                decay = dot_ones(ones, log_gate * alive)
                ld_ref[here] = decay
                m = row * (SEG // BLK) + part
                closing = decay[BLK - 1 : BLK]
                cl_ref[m : m + 1] = closing
                k_ref[here] = key[here] * alive
                kc_ref[here] = key[here] * alive * jnp.exp(closing - decay)
        cl_ref[4:8] = jnp.zeros((4, KD), F32)

    for step in (1, 2):

        @pl.when(n == step)
        def _():
            acc = dot(normed_ref[...], w_ref[...])
            for row in range(ROWS):
                values = []
                for part in range(SEG // BLK):
                    at = row * SEG + part * BLK
                    value = acc[at : at + BLK] * live(lengths_ref, table_ref, row, part * BLK, BLK, KD)
                    v_ref[at : at + BLK] = value
                    values.append(value)
                for sub in range(2):
                    head = (step - 1) * 2 + sub
                    chan = slice(head * KHEAD, (head + 1) * KHEAD)
                    total = None
                    for part in range(SEG // BLK):
                        at = row * SEG + part * BLK
                        m = row * (SEG // BLK) + part
                        update = dot3(
                            values[part][:, sub * VHEAD : (sub + 1) * VHEAD],
                            kc_ref[at : at + BLK, chan], 0, 0,
                        )
                        upd_ref[row, part, head] = update
                        if total is None:
                            total = update
                        else:
                            total = jnp.exp(cl_ref[m : m + 1, chan]) * total + update
                    base = row * (SEG // BLK)
                    gone = cl_ref[base : base + 1, chan] + cl_ref[base + 1 : base + 2, chan]
                    for half in range(2):
                        piece = (row * HEADS + head) * 2 + half
                        out_ref[piece, 0:128] = total[half * 128 : (half + 1) * 128]
                        out_ref[piece, 128:136] = jnp.broadcast_to(gone, (8, KHEAD))


def project(lengths, table, tokens, gain, w, gd, gu, gb):
    full = lambda shape: pl.BlockSpec(shape, lambda n, s, c: (0,) * len(shape))
    return pl.pallas_call(
        proj_kernel,
        grid_spec=pltpu.PrefetchScalarGridSpec(
            num_scalar_prefetch=2,
            grid=(3,),
            in_specs=[
                full((N, D)), full((1, D)), pl.BlockSpec((D, KD), lambda n, s, c: (0, n + 1)),
                full((16, D)), full((16, KD)), full((1, KD)),
            ],
            out_specs=[
                full((N, KD)), pl.BlockSpec((N, KD), lambda n, s, c: (0, jnp.maximum(n - 1, 0))),
                full((N, D)), full((N, KD)), full((8, KD)),
                full((N, KD)), full((N, 16)), full((ROWS, 2, HEADS, VHEAD, KHEAD)),
                full((SEQ, 136, KHEAD)),
            ],
            scratch_shapes=[pltpu.VMEM((N, KD), F32)],
        ),
        out_shape=[
            jax.ShapeDtypeStruct((N, KD), F32), jax.ShapeDtypeStruct((N, VALUE), F32),
            jax.ShapeDtypeStruct((N, D), BF16),
            jax.ShapeDtypeStruct((N, KD), F32), jax.ShapeDtypeStruct((8, KD), F32),
            jax.ShapeDtypeStruct((N, KD), F32), jax.ShapeDtypeStruct((N, 16), F32),
            jax.ShapeDtypeStruct((ROWS, 2, HEADS, VHEAD, KHEAD), F32),
            jax.ShapeDtypeStruct((SEQ, 136, KHEAD), F32),
        ],
        compiler_params=params(),
        cost_estimate=cost(10),
        name="project",
    )(lengths, table, tokens, gain, w, gd, gu, gb)


def rest_kernel(table_ref, normed_ref, w_ref, cot_ref, q_ref, og_ref, normt_ref, cots_ref):
    n = pl.program_id(0)
    acc = dot(normed_ref[...], w_ref[...])

    @pl.when(n == 0)
    def _():
        q_ref[...] = acc * KHEAD ** (-0.5)
        normt_ref[...] = normed_ref[...].T.astype(F32)

    @pl.when(n > 0)
    def _():
        og_ref[...] = acc

    @pl.when(n == 2)
    def _():
        cots_ref[...] = cot_ref[:, pl.ds(pl.multiple_of((1 - table_ref[40]) * 512, 512), 512)].astype(F32)


def project_rest(table, normed, w, cot):
    full = lambda shape: pl.BlockSpec(shape, lambda n, c: (0,) * len(shape))
    return pl.pallas_call(
        rest_kernel,
        grid_spec=pltpu.PrefetchScalarGridSpec(
            num_scalar_prefetch=1,
            grid=(3,),
            in_specs=[
                full((N, D)), pl.BlockSpec((D, KD), lambda n, c: (0, jnp.where(n == 0, 0, n + 3))), full((N, D)),
            ],
            out_specs=[
                full((N, KD)), pl.BlockSpec((N, KD), lambda n, c: (0, jnp.maximum(n - 1, 0))),
                full((D, N)), full((N, KD)),
            ],
        ),
        out_shape=[
            jax.ShapeDtypeStruct((N, KD), F32), jax.ShapeDtypeStruct((N, VALUE), F32),
            jax.ShapeDtypeStruct((D, N), F32), jax.ShapeDtypeStruct((N, KD), F32),
        ],
        compiler_params=params(),
        cost_estimate=cost(0.1),
        name="project_rest",
    )(table, normed, w, cot)


def local_kernel(q_ref, k_ref, v_ref, ld_ref, out_ref):
    mask = lower((BLK, BLK))
    for head in range(HEADS):
        chan = slice(head * KHEAD, (head + 1) * KHEAD)
        vals = slice(head * VHEAD, (head + 1) * VHEAD)
        decay = ld_ref[:, chan]
        centre = decay[BLK // 2 - 1 : BLK // 2]
        scores = dot3(q_ref[:, chan] * jnp.exp(decay - centre), k_ref[:, chan] * jnp.exp(centre - decay), 1, 1)
        out_ref[:, vals] = dot3(jnp.where(mask, scores, 0.0), v_ref[:, vals])


def local(q, k, v, ld):
    rows = lambda width: pl.BlockSpec((BLK, width), lambda m: (m, 0))
    return pl.pallas_call(
        local_kernel,
        grid=(4,),
        in_specs=[rows(KD), rows(KD), rows(VALUE), rows(KD)],
        out_specs=rows(VALUE),
        out_shape=jax.ShapeDtypeStruct((N, VALUE), F32),
        compiler_params=params(),
        cost_estimate=cost(0.1),
        name="local",
    )(q, k, v, ld)


def hidden_kernel(cot_ref, wd_ref, out_ref):
    out_ref[...] = dot(cot_ref[...], wd_ref[...], 1, 1)


def hidden_grad(cot, dnw):
    return pl.pallas_call(
        hidden_kernel,
        grid=(2,),
        in_specs=[pl.BlockSpec((N, D), lambda t: (0, 0)), pl.BlockSpec((FF // 2, D), lambda t: (t, 0))],
        out_specs=pl.BlockSpec((N, FF // 2), lambda t: (0, t)),
        out_shape=jax.ShapeDtypeStruct((N, FF), F32),
        compiler_params=params(),
        cost_estimate=cost(0.1),
        name="hidden_grad",
    )(cot, dnw)


def prefix_kernel(backward, part_ref, decay_ref, out_ref):
    run = jnp.zeros((128, KHEAD), F32)
    order = range(SEQ - 1, -1, -1) if backward else range(SEQ)
    for seg in order:
        out_ref[seg] = run
        run = jnp.exp(decay_ref[seg, 0:1]) * run + part_ref[seg, 0:128]


def prefix(parts, decays, backward):
    return pl.pallas_call(
        functools.partial(prefix_kernel, backward),
        grid=(1,),
        in_specs=[
            pl.BlockSpec((SEQ, 128, KHEAD), lambda n: (0, 0, 0)),
            pl.BlockSpec((SEQ, 8, KHEAD), lambda n: (0, 16, 0)),
        ],
        out_specs=pl.BlockSpec((SEQ, 128, KHEAD), lambda n: (0, 0, 0)),
        out_shape=jax.ShapeDtypeStruct((SEQ, 128, KHEAD), F32),
        compiler_params=params(),
        cost_estimate=cost(0.1),
        name="prefix",
    )(parts, decays)


def attend_kernel(
    q_ref, og_ref, ld_ref, within_ref, cl_ref, inc_ref, upd_ref, tok_ref, ow_ref, hg_ref, mg_ref,
    heads_ref, middle_ref, mlp_ref, both_ref,
    mixed_ref,
):
    m = pl.program_id(0)
    second = lax.rem(m, 2) == 1
    previous = cl_ref[pl.ds(m - lax.rem(m, 2), 1), :]
    gain = hg_ref[...].astype(F32)
    for head in range(HEADS):
        chan = slice(head * KHEAD, (head + 1) * KHEAD)
        vals = slice(head * VHEAD, (head + 1) * VHEAD)
        start = inc_ref[0, head]
        start = jnp.where(second, jnp.exp(previous[:, chan]) * start + upd_ref[0, 0, head], start)
        out = within_ref[:, vals] + dot3(q_ref[:, chan] * jnp.exp(ld_ref[:, chan]), start, 1, 1)
        heads_ref[:, vals] = out
        gate = og_ref[:, vals]
        mixed = out * inverse_rms(out) * gain * (gate * sigmoid(gate))
        mixed_ref[:, vals] = mixed.astype(BF16)

    middle = tok_ref[...].astype(F32) + dot(mixed_ref[...], ow_ref[...])
    middle_ref[...] = middle
    mlp_in = (middle * inverse_rms(middle) * mg_ref[...].astype(F32)).astype(BF16)
    mlp_ref[...] = mlp_in
    both_ref[:D] = mlp_in.T.astype(F32)
    both_ref[D:] = mixed_ref[...].T.astype(F32)


def attend(q, og, ld, within, cl, incoming, upd, tokens, ow, hg, mg):
    full = lambda shape: pl.BlockSpec(shape, lambda m: (0,) * len(shape))
    rows = lambda width: pl.BlockSpec((BLK, width), lambda m: (m, 0))
    return pl.pallas_call(
        attend_kernel,
        grid=(4,),
        in_specs=[
            rows(KD), rows(VALUE), rows(KD), rows(VALUE), full((8, KD)),
            pl.BlockSpec((1, HEADS, VHEAD, KHEAD), lambda m: (m // 2, 0, 0, 0)),
            pl.BlockSpec((1, 1, HEADS, VHEAD, KHEAD), lambda m: (m // 2, 0, 0, 0, 0)),
            rows(D), full((VALUE, D)), full((1, VHEAD)), full((1, D)),
        ],
        out_specs=[
            rows(VALUE), rows(D), rows(D), pl.BlockSpec((D + VALUE, BLK), lambda m: (0, m)),
        ],
        out_shape=[
            jax.ShapeDtypeStruct((N, VALUE), F32), jax.ShapeDtypeStruct((N, D), F32),
            jax.ShapeDtypeStruct((N, D), BF16), jax.ShapeDtypeStruct((D + VALUE, N), F32),
        ],
        scratch_shapes=[pltpu.VMEM((BLK, VALUE), BF16)],
        compiler_params=params(),
        cost_estimate=cost(13),
        name="attend",
    )(q, og, ld, within, cl, incoming, upd, tokens, ow, hg, mg)


TILES = FF // TILE


def mlp_kernel(
    core_ref, mlp_ref, dh_ref, wg_ref, wu_ref, wd_ref, middle_ref,
    out_ref, dmlp_ref, own_ref, send_ref, hidt_ref, acc_ref,
):
    t = pl.program_id(0)

    @pl.when(t == 0)
    def _():
        acc_ref[...] = middle_ref[...]
        dmlp_ref[...] = jnp.zeros((N, D), F32)

    mlp_in = mlp_ref[...]
    gate = dot(mlp_in, wg_ref[...])
    up = dot(mlp_in, wu_ref[...])
    d_hidden = dh_ref[...]
    sig = sigmoid(gate)
    act = gate * sig
    hidden = (act * up).astype(BF16)
    d_gate = (d_hidden * up * (sig * (1.0 + gate * (1.0 - sig)))).astype(BF16)
    d_up = (d_hidden * act).astype(BF16)
    acc_ref[...] += dot(hidden, wd_ref[...])
    dmlp_ref[...] += dot(d_gate, wg_ref[...], 1, 1) + dot(d_up, wu_ref[...], 1, 1)
    first = core_ref[40] == 0
    own_ref[...] = jnp.where(first, d_gate, d_up)
    send_ref[...] = jnp.where(first, d_up, d_gate).astype(F32)
    hidt_ref[...] = hidden.T.astype(F32)

    @pl.when(t == TILES - 1)
    def _():
        out_ref[...] = acc_ref[...].astype(BF16)


def mlp(core, mlp_in, d_hidden, upw, dnw, middle):
    full = lambda shape: pl.BlockSpec(shape, lambda t, c: (0,) * len(shape))
    column = lambda rows: pl.BlockSpec((rows, TILE), lambda t, c: (0, t))
    return pl.pallas_call(
        mlp_kernel,
        grid_spec=pltpu.PrefetchScalarGridSpec(
            num_scalar_prefetch=1,
            grid=(TILES,),
            in_specs=[
                full((N, D)), column(N), column(D),
                pl.BlockSpec((D, TILE), lambda t, c: (0, TILES + t)),
                pl.BlockSpec((TILE, D), lambda t, c: (t, 0)), full((N, D)),
            ],
            out_specs=[
                full((N, D)), full((N, D)), column(N), column(N),
                pl.BlockSpec((TILE, N), lambda t, c: (t, 0)),
            ],
            scratch_shapes=[pltpu.VMEM((N, D), F32)],
        ),
        out_shape=[
            jax.ShapeDtypeStruct((N, D), BF16), jax.ShapeDtypeStruct((N, D), F32),
            jax.ShapeDtypeStruct((N, FF), BF16), jax.ShapeDtypeStruct((N, FF), F32),
            jax.ShapeDtypeStruct((FF, N), F32),
        ],
        compiler_params=params(),
        cost_estimate=cost(30),
        name="mlp",
    )(core, mlp_in, d_hidden, upw, upw, dnw, middle)


def down_grad_kernel(
    table_ref, hid_ref, hid_other, cot_ref, cot_other, keep_ref, send_ref, cotb_ref, hidb_ref
):
    @pl.when(pl.program_id(0) == 0)
    def _():
        cotb_ref[:N] = cot_ref[...]
        cotb_ref[N:] = cot_other[...].astype(BF16)

    hidb_ref[:, :N] = hid_ref[...].reshape(TILE, N).astype(BF16)
    hidb_ref[:, N:] = hid_other[...].reshape(TILE, N).astype(BF16)
    down = dot(hidb_ref[...], cotb_ref[...]).reshape(SEQ, 16, 512)
    for slab in range(4):
        slot = table_ref[41 + slab]

        @pl.when(slot < 2)
        def _():
            keep_ref[slot] = down[:, :, slab * 128 : (slab + 1) * 128]

        @pl.when(slot >= 2)
        def _():
            send_ref[slot - 2] = down[:, :, slab * 128 : (slab + 1) * 128]


def down_grad(table, hid, hid_other, cot, cot_other):
    tall = pl.BlockSpec((SEQ, 16, N), lambda t, c: (0, t, 0))
    out = pl.BlockSpec((2, SEQ, 16, 128), lambda t, c: (0, 0, t, 0))
    return pl.pallas_call(
        down_grad_kernel,
        grid_spec=pltpu.PrefetchScalarGridSpec(
            num_scalar_prefetch=1,
            grid=(TILES,),
            in_specs=[
                tall, tall, pl.BlockSpec((N, 512), lambda t, c: (0, c[40])),
                pl.BlockSpec((N, 512), lambda t, c: (0, 0)),
            ],
            out_specs=[out, out],
            scratch_shapes=[pltpu.VMEM((2 * N, 512), BF16), pltpu.VMEM((TILE, 2 * N), BF16)],
        ),
        out_shape=[jax.ShapeDtypeStruct((2, SEQ, 176, 128), F32)] * 2,
        compiler_params=params(),
        cost_estimate=cost(0.1),
        name="down_grad",
    )(table, chunks(hid), chunks(hid_other), cot, cot_other)


def up_grad_kernel(
    table_ref, mlpt_ref, mlpt_other, act_ref, act_other, keep_0, send_0, keep_1, send_1,
    left_ref, right_ref, value_ref,
):
    @pl.when(pl.program_id(0) == 0)
    def _():
        left_ref[:, :N] = mlpt_ref[...].astype(BF16)
        left_ref[:, N:] = mlpt_other[...].astype(BF16)

    right_ref[:N] = act_ref[...]
    right_ref[N:] = act_other[...].astype(BF16)
    value_ref[...] = dot(left_ref[...], right_ref[...])
    for v, (keep_ref, send_ref) in enumerate(((keep_0, send_0), (keep_1, send_1))):
        cols = slice(v * 128, v * 128 + 128)
        for index in range(8):
            keep_ref[index] = value_ref[chunk_rows(table_ref, v, index), cols]
            send_ref[index] = value_ref[chunk_rows(table_ref, v, 8 + index), cols]


def chunk_rows(table_ref, v, index):
    return pl.ds(pl.multiple_of(table_ref[v * 16 + index] * 64, 64), 64)


def up_grad(table, mlpt, mlpt_other, act, act_other):
    full = lambda shape: pl.BlockSpec(shape, lambda t, c: (0,) * len(shape))
    wide = pl.BlockSpec((N, TILE), lambda t, c: (0, t))
    return pl.pallas_call(
        up_grad_kernel,
        grid_spec=pltpu.PrefetchScalarGridSpec(
            num_scalar_prefetch=1,
            grid=(TILES,),
            in_specs=[full((D, N)), full((D, N)), wide, wide],
            out_specs=[pl.BlockSpec((8, 64, 128), lambda t, c: (0, t, 0))] * 4,
            scratch_shapes=[
                pltpu.VMEM((D, 2 * N), BF16), pltpu.VMEM((2 * N, TILE), BF16), pltpu.VMEM((D, TILE), F32),
            ],
        ),
        out_shape=[jax.ShapeDtypeStruct((8, TILES * 64, 128), F32)] * 4,
        compiler_params=params(),
        cost_estimate=cost(0.1),
        name="up_grad",
    )(table, mlpt, mlpt_other, act, act_other)


def back_kernel(
    core_ref, middle_ref, dmlp_ref, cot_ref, mg_ref, ow_ref, hg_ref, heads_ref, og_ref, q_ref, ld_ref, cl_ref,
    dmid_ref, datt_ref, mgg_ref, hgg_ref, dheads_ref, dog_ref, sends_ref, adj_ref, out_ref,
    dmix_ref,
):
    away = pl.ds(pl.multiple_of((1 - core_ref[40]) * 512, 512), 512)
    m = pl.program_id(0)

    @pl.when(m == 0)
    def _():
        mgg_ref[...] = jnp.zeros((1, D), F32)
        hgg_ref[...] = jnp.zeros((1, VHEAD), F32)

    middle = middle_ref[...]
    scale_two = inverse_rms(middle)
    unit_two = middle * scale_two
    grad = dmlp_ref[...]
    mgg_ref[...] += jnp.sum(grad * unit_two, 0, keepdims=True)
    scaled = grad * mg_ref[...].astype(F32)
    d_middle = scale_two * (scaled - unit_two * jnp.mean(scaled * unit_two, -1, keepdims=True))
    d_middle = d_middle + cot_ref[...].astype(F32)
    dmid_ref[...] = d_middle
    datt_ref[...] = d_middle.astype(BF16)
    dmix_ref[...] = dot(datt_ref[...], ow_ref[...], 1, 1)
    block = m + 1 - 2 * lax.rem(m, 2)
    first = lax.rem(m, 2) == 0
    closing = cl_ref[pl.ds(block, 1), :]
    gain = hg_ref[...].astype(F32)
    for head in range(HEADS):
        chan = slice(head * KHEAD, (head + 1) * KHEAD)
        vals = slice(head * VHEAD, (head + 1) * VHEAD)
        out = heads_ref[:, vals]
        scale = inverse_rms(out)
        unit = out * scale
        gate = og_ref[:, vals]
        sig = sigmoid(gate)
        act = gate * sig
        d_mixed = dmix_ref[:, vals]
        dog_ref[:, vals] = (d_mixed * (unit * gain) * (sig * (1.0 + gate * (1.0 - sig)))).astype(BF16)
        d_norm = d_mixed * act
        hgg_ref[...] += jnp.sum(d_norm * unit, 0, keepdims=True)
        scaled = d_norm * gain
        d_out = scale * (scaled - unit * jnp.mean(scaled * unit, -1, keepdims=True))
        dheads_ref[:, vals] = d_out
        adjoint = dot3(d_out, q_ref[:, chan] * jnp.exp(ld_ref[:, chan]), 0, 0)

        @pl.when(first)
        def _():
            adj_ref[0, head] = adjoint

        @pl.when(jnp.logical_not(first))
        def _():
            total = jnp.exp(closing[:, chan]) * adj_ref[0, head] + adjoint
            for half in range(2):
                out_ref[head * 2 + half] = total[half * 128 : (half + 1) * 128]

    sends_ref[:, :512] = datt_ref[:, away].astype(F32)
    sends_ref[:, 512:] = dog_ref[:, away].astype(F32)


def back(core, middle, dmlp, cot, mg, ow, hg, heads, og, q, ld, cl):
    full = lambda shape: pl.BlockSpec(shape, lambda m, c: (0,) * len(shape))
    block = lambda m: m + 1 - 2 * lax.rem(m, 2)
    wide = pl.BlockSpec((BLK, D), lambda m, c: (block(m), 0))
    return pl.pallas_call(
        back_kernel,
        grid_spec=pltpu.PrefetchScalarGridSpec(num_scalar_prefetch=1, grid=(4,), in_specs=[
            wide, wide, wide, full((1, D)), full((VALUE, D)), full((1, VHEAD)),
            pl.BlockSpec((BLK, VALUE), lambda m, c: (block(m), 0)),
            pl.BlockSpec((BLK, VALUE), lambda m, c: (block(m), 0)),
            pl.BlockSpec((BLK, KD), lambda m, c: (block(m), 0)),
            pl.BlockSpec((BLK, KD), lambda m, c: (block(m), 0)),
            full((8, KD)),
        ],
        out_specs=[
            wide, wide, full((1, D)), full((1, VHEAD)),
            pl.BlockSpec((BLK, VALUE), lambda m, c: (block(m), 0)),
            pl.BlockSpec((BLK, VALUE), lambda m, c: (block(m), 0)),
            pl.BlockSpec((BLK, D), lambda m, c: (block(m), 0)),
            pl.BlockSpec((1, HEADS, VHEAD, KHEAD), lambda m, c: (m // 2, 0, 0, 0)),
            pl.BlockSpec((8, 128, KHEAD), lambda m, c: (m // 2, 0, 0)),
        ],
        scratch_shapes=[pltpu.VMEM((BLK, VALUE), F32)]),
        out_shape=[
            jax.ShapeDtypeStruct((N, D), F32), jax.ShapeDtypeStruct((N, D), BF16),
            jax.ShapeDtypeStruct((1, D), F32), jax.ShapeDtypeStruct((1, VHEAD), F32),
            jax.ShapeDtypeStruct((N, VALUE), F32), jax.ShapeDtypeStruct((N, VALUE), BF16),
            jax.ShapeDtypeStruct((N, D), F32),
            jax.ShapeDtypeStruct((ROWS, HEADS, VHEAD, KHEAD), F32),
            jax.ShapeDtypeStruct((SEQ, 128, KHEAD), F32),
        ],
                compiler_params=params(),
        cost_estimate=cost(30),
        name="back",
    )(core, middle, dmlp, cot, mg, ow, hg, heads, og, q, ld, cl)


def inner_kernel(
    limit_ref, core_ref, q_ref, k_ref, v_ref, dout_ref, ld_ref, cl_ref, inc_ref, ret_ref, upd_ref, adj_ref,
    logit_ref, low_ref, gu_ref, normed_ref, hg_ref, mg_ref,
    dproj_ref, dprojs_ref, dlow_ref, pack_ref,
    dlg_ref, gb_ref, gup_ref, gdn_ref,
):
    m = pl.program_id(0)
    row = m // 2
    part = lax.rem(m, 2)
    second = part == 1

    @pl.when(m == 0)
    def _():
        gb_ref[...] = jnp.zeros((1, KD), F32)
        gup_ref[...] = jnp.zeros((16, KD), F32)
        gdn_ref[...] = jnp.zeros((16, D), F32)

    mask = lower((BLK, BLK))
    upper = lax.broadcasted_iota(jnp.int32, (BLK, BLK), 0) <= lax.broadcasted_iota(jnp.int32, (BLK, BLK), 1)
    upper = upper.astype(BF16)
    closing = cl_ref[pl.ds(m, 1), :]
    previous = cl_ref[pl.ds(row * 2, 1), :]
    following = cl_ref[pl.ds(row * 2 + 1, 1), :]
    alive = live(limit_ref, core_ref, row, part * BLK, BLK, VHEAD)
    alive_key = alive[:, :KHEAD]
    for head in range(HEADS):
        chan = slice(head * KHEAD, (head + 1) * KHEAD)
        vals = slice(head * VHEAD, (head + 1) * VHEAD)
        start = inc_ref[0, head]
        start = jnp.where(second, jnp.exp(previous[:, chan]) * start + upd_ref[0, 0, head], start)
        update = jnp.where(second, upd_ref[0, 1, head], upd_ref[0, 0, head])
        end_state = jnp.exp(closing[:, chan]) * start + update
        end_grad = ret_ref[0, head]
        end_grad = jnp.where(second, end_grad, jnp.exp(following[:, chan]) * end_grad + adj_ref[0, head])
        decay = ld_ref[:, chan]
        centre = decay[BLK // 2 - 1 : BLK // 2]
        query = q_ref[:, chan]
        key = k_ref[:, chan]
        value = v_ref[:, vals]
        d_out = dout_ref[:, vals]
        up_factor = jnp.exp(decay - centre)
        down_factor = jnp.exp(centre - decay)
        query_mid = query * up_factor
        key_mid = key * down_factor
        close_factor = jnp.exp(closing[:, chan] - decay)
        scores = jnp.where(mask, dot3(query_mid, key_mid, 1, 1), 0.0)
        d_scores = jnp.where(mask, dot3(d_out, value, 1, 1), 0.0)
        d_query = up_factor * dot3(d_scores, key_mid) + jnp.exp(decay) * dot3(d_out, start)
        d_key = down_factor * dot3(d_scores, query_mid, 0, 0) + close_factor * dot3(value, end_grad)
        d_value = dot3(scores, d_out, 0, 0) + dot3(key * close_factor, end_grad, 1, 1)
        d_decay = query * d_query - key * d_key
        dlg_ref[:, chan] = dot_ones(upper, d_decay) + jnp.sum(end_grad * end_state, 0, keepdims=True)
        dproj_ref[:, chan] = (d_query * KHEAD ** (-0.5)).astype(BF16)
        dproj_ref[:, KD + head * KHEAD : KD + (head + 1) * KHEAD] = (d_key * alive_key).astype(BF16)
        dproj_ref[:, 2 * KD + head * VHEAD : 2 * KD + (head + 1) * VHEAD] = (d_value * alive).astype(BF16)
    alive_gate = live(limit_ref, core_ref, row, part * BLK, BLK, KD)
    d_logit = dlg_ref[...] * alive_gate * (1.0 / (1.0 + jnp.exp(logit_ref[...]))) * (1.0 / 16.0)
    gb_ref[...] += jnp.sum(d_logit, 0, keepdims=True)
    gup_ref[...] += dot3(low_ref[...], d_logit, 0, 0)
    high, rest = split(d_logit)
    d_low = (dot(high, gu_ref[...], 1, 1) + dot(rest, gu_ref[...], 1, 1)).astype(BF16)
    dlow_ref[...] = d_low
    gdn_ref[...] += dot(d_low, normed_ref[...], 0, 0)
    away = pl.ds(pl.multiple_of((1 - core_ref[40]) * 1024, 1024), 1024)
    dprojs_ref[...] = dproj_ref[:, away].astype(F32)

    @pl.when(m == 3)
    def _():
        pack_ref[:, 16:24] = jnp.zeros((SEQ, 8, 128), F32)
        for chunk in range(SEQ):
            pack_ref[chunk, :16, :64] = gdn_ref[:, chunk * 64 : chunk * 64 + 64]
            pack_ref[chunk, :16, 64:96] = gup_ref[:, chunk * 32 : chunk * 32 + 32]
            pack_ref[chunk, :16, 96:] = jnp.zeros((16, 32), F32)
            pack_ref[chunk, 16:17, 64:] = mg_ref[:, chunk * 64 : chunk * 64 + 64]
            pack_ref[chunk, 17:18, :32] = gb_ref[:, chunk * 32 : chunk * 32 + 32]
            pack_ref[chunk, 17:18, 32:48] = hg_ref[:, chunk * 16 : chunk * 16 + 16]


def inner(limit, core, q, k, v, dout, ld, cl, incoming, returned, upd, adj, logit, low, gu, normed, hg, mg):
    full = lambda shape: pl.BlockSpec(shape, lambda m, s, c: (0,) * len(shape))
    by_row = pl.BlockSpec((1, HEADS, VHEAD, KHEAD), lambda m, s, c: (m // 2, 0, 0, 0))
    return pl.pallas_call(
        inner_kernel,
        grid_spec=pltpu.PrefetchScalarGridSpec(
            num_scalar_prefetch=2,
            grid=(4,),
            in_specs=[
                pl.BlockSpec((BLK, KD), lambda m, s, c: (m, 0)), pl.BlockSpec((BLK, KD), lambda m, s, c: (m, 0)),
                pl.BlockSpec((BLK, VALUE), lambda m, s, c: (m, 0)), pl.BlockSpec((BLK, VALUE), lambda m, s, c: (m, 0)),
                pl.BlockSpec((BLK, KD), lambda m, s, c: (m, 0)), full((8, KD)),
                by_row, by_row,
                pl.BlockSpec((1, 2, HEADS, VHEAD, KHEAD), lambda m, s, c: (m // 2, 0, 0, 0, 0)),
                by_row,
                pl.BlockSpec((BLK, KD), lambda m, s, c: (m, 0)), pl.BlockSpec((BLK, 16), lambda m, s, c: (m, 0)),
                full((16, KD)), pl.BlockSpec((BLK, D), lambda m, s, c: (m, 0)), full((1, VHEAD)), full((1, D)),
            ],
            out_specs=[
                pl.BlockSpec((BLK, 2048), lambda m, s, c: (m, 0)),
                pl.BlockSpec((BLK, 1024), lambda m, s, c: (m, 0)), pl.BlockSpec((BLK, 16), lambda m, s, c: (m, 0)),
                full((SEQ, 24, 128)),
            ],
            scratch_shapes=[
                pltpu.VMEM((BLK, KD), F32), pltpu.VMEM((1, KD), F32), pltpu.VMEM((16, KD), F32), pltpu.VMEM((16, D), F32),
            ],
        ),
        out_shape=[
            jax.ShapeDtypeStruct((N, 2048), BF16), jax.ShapeDtypeStruct((N, 1024), F32), jax.ShapeDtypeStruct((N, 16), BF16),
            jax.ShapeDtypeStruct((SEQ, 24, 128), F32),
        ],
        compiler_params=params(),
        cost_estimate=cost(300),
        name="inner",
    )(limit, core, q, k, v, dout, ld, cl, incoming, returned, upd, adj, logit, low, gu, normed, hg, mg)


def outer_kernel(sets, extras, table_ref, *refs):
    count = 4 * len(sets)
    more, outs = refs[count : count + extras], refs[count + extras : -3]
    left_ref, right_ref, value_ref = refs[-3:]
    at = 0
    for which, streams in enumerate(sets):
        x_ref, x_other, y_ref, y_other = refs[4 * which : 4 * which + 4]
        left_ref[:, :N] = x_ref[...].astype(BF16)
        left_ref[:, N:] = x_other[...].astype(BF16)
        for part, v in enumerate(streams):
            cols = slice(part * 512, (part + 1) * 512)
            right_ref[:N] = y_ref[:, cols]
            right_ref[N:] = y_other[:, cols].astype(BF16)
            value_ref[...] = dot(left_ref[...], right_ref[...])
            for side, target in enumerate(outs[2 * at : 2 * at + 2]):
                for index in range(8):
                    rows = chunk_rows(table_ref, v, side * 8 + index)
                    for slab in range(4):
                        target[index, slab * 64 : slab * 64 + 64] = value_ref[rows, slab * 128 : slab * 128 + 128]
                    if extras:
                        own, first, got, pack = more
                        chunk = table_ref[v * 16 + side * 8 + index]
                        cut = slice(v * 88, v * 88 + 88)
                        target[index, 256:344] = own[0, chunk, cut] + first[0, chunk, cut] + got[chunk, cut]
                        if v == 1:
                            target[index, 344:368] = pack[chunk]
            at += 1


def outer(table, sets, more=()):
    operands, specs, outs = [], [], []
    for x, x_other, rows, y, y_other, cols, streams in sets:
        width = 512 * len(streams)
        operands += [x, x_other, y, y_other]
        specs += [
            pl.BlockSpec((D, N), lambda i, t, r=rows: (r, 0)), pl.BlockSpec((D, N), lambda i, t, r=rows: (r, 0)),
            pl.BlockSpec((N, width), lambda i, t: (0, t[40])), pl.BlockSpec((N, width), lambda i, t, c=cols: (0, c)),
        ]
        for v in streams:
            total = 256 + (88 + 24 * v if more else 0)
            outs += [jax.ShapeDtypeStruct((8, total, 128), F32)] * 2
    for array in more:
        operands.append(array)
        if array.ndim == 4:
            specs.append(pl.BlockSpec((1,) + array.shape[1:], lambda i, t: (t[45], 0, 0, 0)))
        else:
            specs.append(pl.BlockSpec(array.shape, lambda i, t: (0, 0, 0)))
    return pl.pallas_call(
        functools.partial(outer_kernel, [streams for *_, streams in sets], len(more)),
        grid_spec=pltpu.PrefetchScalarGridSpec(
            num_scalar_prefetch=1, grid=(1,), in_specs=specs,
            out_specs=[pl.BlockSpec(out.shape, lambda i, t: (0, 0, 0)) for out in outs],
            scratch_shapes=[
                pltpu.VMEM((D, 2 * N), BF16), pltpu.VMEM((2 * N, 512), BF16), pltpu.VMEM((D, 512), F32),
            ],
        ),
        out_shape=outs,
        compiler_params=params(),
        cost_estimate=cost(0.1),
        name="outer",
    )(table, *operands)


def input_kernel(
    y_ref, og_ref, w_ref, dlow_ref, gd_ref, tok_ref, gain_ref, dmid_ref, pack_in,
    grad_ref, pack_ref, acc_ref,
):
    t = pl.program_id(0)

    @pl.when(t == 0)
    def _():
        acc_ref[...] = dot(dlow_ref[...], gd_ref[...])

    @pl.when(t < 4)
    def _():
        acc_ref[...] += dot(y_ref[...], w_ref[...], 1, 1)

    @pl.when(t >= 4)
    def _():
        acc_ref[...] += dot(og_ref[...], w_ref[...], 1, 1)

    @pl.when(t == 5)
    def _():
        total = jnp.zeros((1, D), F32)
        for at in range(0, N, 128):
            here = slice(at, at + 128)
            inputs = tok_ref[here].astype(F32)
            scale = inverse_rms(inputs)
            unit = inputs * scale
            grad = acc_ref[here]
            total = total + jnp.sum(grad * unit, 0, keepdims=True)
            scaled = grad * gain_ref[...].astype(F32)
            d_inputs = scale * (scaled - unit * jnp.mean(scaled * unit, -1, keepdims=True))
            grad_ref[here] = (dmid_ref[here] + d_inputs).astype(BF16)
        pack_ref[...] = pack_in[...]
        for chunk in range(SEQ):
            pack_ref[chunk, 16:17, :64] = total[:, chunk * 64 : chunk * 64 + 64]


def input_back(y, og, w, dlow, gd, tokens, gain, dmid, pack):
    full = lambda shape: pl.BlockSpec(shape, lambda t: (0,) * len(shape))
    return pl.pallas_call(
        input_kernel,
        grid=(6,),
        in_specs=[
            pl.BlockSpec((N, 512), lambda t: (0, jnp.minimum(t, 3))),
            pl.BlockSpec((N, 512), lambda t: (0, jnp.maximum(t - 4, 0))),
            pl.BlockSpec((D, 512), lambda t: (0, t)),
            full((N, 16)), full((16, D)), full((N, D)), full((1, D)), full((N, D)),
            full((SEQ, 24, 128)),
        ],
        out_specs=[full((N, D)), full((SEQ, 24, 128))],
        out_shape=[
            jax.ShapeDtypeStruct((N, D), BF16), jax.ShapeDtypeStruct((SEQ, 24, 128), F32),
        ],
        scratch_shapes=[pltpu.VMEM((N, D), F32)],
        compiler_params=params(),
        cost_estimate=cost(12),
        name="input_back",
    )(y, og, w, dlow, gd, tokens, gain, dmid, pack)


SWAP = [(i, i ^ 1) for i in range(8)]
FLIP = {0: 1, 1: 3}
XORDER = ((0, 1), (1, 0))
ORDERS = (((0, 1, 2, 3), (1, 0, 3, 2)), ((2, 3, 0, 1), (3, 2, 1, 0)))


def bit_of(seq, which):
    at = seq // 4 if which < 2 else seq % 4
    return at // 2 if which % 2 else int(at in (1, 2))


def chunk_of(order, bits):
    value = dict(zip(order, bits))
    along = [[0, 1, 3, 2][2 * value[2 * a + 1] + value[2 * a]] for a in range(2)]
    return along[0] * 4 + along[1]


def partner(seq, which):
    z, y = seq // 4, seq % 4
    return (z ^ FLIP[which]) * 4 + y if which < 2 else z * 4 + (y ^ FLIP[which - 2])


def tables():
    table = np.zeros((128, 96), np.int32)
    for device in range(128):
        core, seq = (device // 16) % 2, device % 16
        for v in range(2):
            order = ORDERS[v][core]
            chunks = [chunk_of(order, [(i >> 3) & 1, (i >> 2) & 1, (i >> 1) & 1, i & 1]) for i in range(16)]
            mine = [bit_of(seq, which) for which in order]
            table[device, v * 16 : v * 16 + 8] = chunks[mine[0] * 8 : mine[0] * 8 + 8]
            table[device, v * 16 + 8 : v * 16 + 16] = chunks[(1 - mine[0]) * 8 : (1 - mine[0]) * 8 + 8]
            table[device, 32 + v * 4 : 36 + v * 4] = mine
            for slot in range(16):
                table[device, 48 + v * 16 + chunks[slot ^ (8 * mine[0])]] = slot
        table[device, 40] = core
        table[device, 46] = seq
        x, (near, far) = device // 32, XORDER[core]
        for slab in range(4):
            away = bit_of(slab * 4, near) != bit_of(x * 4, near)
            table[device, 41 + slab] = bit_of(slab * 4, far) + 2 * away
        table[device, 45] = bit_of(x * 4, far)
        for who in range(2):
            near, far = XORDER[core ^ who]
            table[device, 80 + 4 * who : 84 + 4 * who] = [x, x ^ FLIP[far], x ^ FLIP[near], x ^ 2]
    return table


TABLE = tables()
STEPS = [
    [
        [(d, (d // 16) * 16 + partner(d % 16, ORDERS[v][(d // 16) % 2][step])) for d in range(128)]
        for step in range(4)
    ]
    for v in range(2)
]
ACROSS = [
    [(i, ((i // 2) ^ FLIP[XORDER[i % 2][step]]) * 2 + i % 2) for i in range(8)] for step in range(2)
]


def exchange(value):
    return lax.all_to_all(value, "seq", 0, 0, tiled=True)


def swap(value):
    return lax.ppermute(value, "dp", SWAP)


def halve_x_kernel(table_ref, k_ref, r_ref, send_ref):
    del table_ref
    send_ref[...] = k_ref[...] + r_ref[...]


def halve_x(table, keep, got):
    rows = keep.shape[1] // 2
    theirs = pl.BlockSpec((1, rows, 128), lambda j, t: (1 - t[45], j, 0))
    return pl.pallas_call(
        halve_x_kernel,
        grid_spec=pltpu.PrefetchScalarGridSpec(
            num_scalar_prefetch=1, grid=(2,), in_specs=[theirs, theirs],
            out_specs=pl.BlockSpec((1, rows, 128), lambda j, t: (0, j, 0)),
        ),
        out_shape=jax.ShapeDtypeStruct((1, 2 * rows, 128), F32),
        compiler_params=params(),
        cost_estimate=cost(0.1),
        name="halve_x",
    )(table, keep, got)


def halve_kernel(shapes, moves, table_ref, *refs):
    del table_ref
    ins = list(refs)
    at = 0
    values = []
    for groups, later in shapes:
        row, parts = 0, []
        rests = ins[at + 2 * groups : at + 2 * groups + later]
        for group in range(groups):
            k_ref, r_ref = ins[at + 2 * group : at + 2 * group + 2]
            parts.append((row, row + k_ref.shape[1], k_ref, r_ref))
            row += k_ref.shape[1]
        values.append((parts, rests))
        at += 2 * groups + later
    for v, first, count, out, place in moves:
        out_ref = ins[at + out]
        for low, high, k_ref, r_ref in values[v][0]:
            start, stop = max(first, low), min(first + count, high)
            if start >= stop:
                continue
            total = k_ref[:, start - low : stop - low] + r_ref[:, start - low : stop - low]
            for rest in values[v][1]:
                total = total + rest[:, start:stop]
            out_ref[:, place + start - first : place + stop - first] = total


def halve(table, step, streams, moves=None):
    size = 2 if step < 3 else 1
    turns = 2 if step == 1 else 1
    operands, specs, shapes, totals = [], [], [], []
    for v, (groups, later) in enumerate(streams):
        bit = lambda t, n, v=v: t[32 + v * 4 + n]

        def block(i, t, bit=bit):
            if step == 1:
                return (1 - bit(t, 1)) * 2 + i
            if step == 2:
                return bit(t, 1) * 2 + 1 - bit(t, 2)
            last = 1 - bit(t, 3) if step == 3 else bit(t, 3)
            return bit(t, 1) * 4 + bit(t, 2) * 2 + last

        total = 0
        for pair in groups:
            for array in pair:
                operands.append(array)
                specs.append(pl.BlockSpec((size, array.shape[1], 128), lambda i, t, f=block: (f(i, t), 0, 0)))
            total += pair[0].shape[1]
        for array in later:
            operands.append(array)
            count = array.shape[0] // size
            specs.append(
                pl.BlockSpec((size, total, 128), lambda i, t, f=block, c=count: (lax.rem(f(i, t), c), 0, 0))
            )
        shapes.append((len(groups), len(later)))
        totals.append(total)
    if moves is None:
        moves = [(v, 0, totals[v], v, 0) for v in range(2)]
        outs = [(size * turns, total) for total in totals]
    else:
        outs = [(1, sum(totals))]
    return pl.pallas_call(
        functools.partial(halve_kernel, shapes, moves),
        grid_spec=pltpu.PrefetchScalarGridSpec(
            num_scalar_prefetch=1, grid=(turns,), in_specs=specs,
            out_specs=[pl.BlockSpec((size, rows, 128), lambda i, t: (i, 0, 0)) for _, rows in outs],
        ),
        out_shape=[jax.ShapeDtypeStruct((count, rows, 128), F32) for count, rows in outs],
        compiler_params=params(),
        cost_estimate=cost(0.1),
        name="halve",
    )(table, *operands)


def hop(v, step, value):
    return lax.ppermute(value, ("dp", "seq"), STEPS[v][step])


def hops(step, sends):
    return [hop(v, step, sends[v]) for v in range(2)]


def along_x(step, value):
    return lax.ppermute(value, "dp", ACROSS[step])


def after(value, *others):
    return lax.optimization_barrier((value, *others))[0]


def unpack_kernel(
    table_ref, a_ref, a_other, b_ref, b_other,
    up_ref, down_ref, out_ref, in_ref, gd_ref, gu_ref, ng_ref, mg_ref, gb_ref, hg_ref,
):
    core = table_ref[40]

    def place(own_ref, other_ref, at, rows, slabs, target, first, second):
        for slab in range(slabs):
            own = own_ref[at : at + rows]
            other = other_ref[at : at + rows]
            low = jnp.where(core == 0, own, other)
            high = jnp.where(core == 0, other, own)
            target[:, first + slab * 128 : first + (slab + 1) * 128] = low
            target[:, second + slab * 128 : second + (slab + 1) * 128] = high
            at += rows
        return at

    for v in range(2):
        for tile in range(TILES):
            column = tile * TILE + v * 128
            place(a_ref, a_other, (v * TILES + tile) * 64, 64, 1, up_ref, column, FF + column)
    at = place(b_ref, b_other, 0, 64, 4, out_ref, 0, 512)
    at = place(b_ref, b_other, at, 64, 4, in_ref, 2048, 2560)
    at = place(b_ref, b_other, at, 64, 4, in_ref, 0, 1024)
    at = place(b_ref, b_other, at, 64, 4, in_ref, 512, 1536)
    small = b_ref[at : at + 24] + b_other[at : at + 24]
    gd_ref[...] = small[:16, :64]
    gu_ref[...] = small[:16, 64:96]
    ng_ref[...] = small[16:17, :64]
    mg_ref[...] = small[16:17, 64:128]
    gb_ref[...] = small[17:18, :32]
    hg_ref[...] = small[17:18, 32:48]
    for slab in range(4):
        first = at + 24 + slab * 176
        for ref, base, place_of in ((b_ref, core * 512, 80), (b_other, (1 - core) * 512, 84)):
            cols = pl.ds(pl.multiple_of(base + table_ref[place_of + slab] * 128, 128), 128)
            down_ref[:, cols] = ref[first : first + 176]


def unpack(table, a, a_other, b, b_other):
    shapes = [
        (64, 2 * FF), (176, D), (64, D), (64, 3072), (16, 64), (16, 32), (1, 64), (1, 64), (1, 32), (1, 16),
    ]
    return pl.pallas_call(
        unpack_kernel,
        in_specs=[pl.BlockSpec(memory_space=pltpu.SMEM)] + [pl.BlockSpec(memory_space=pltpu.VMEM)] * 4,
        out_specs=[pl.BlockSpec(memory_space=pltpu.VMEM)] * len(shapes),
        out_shape=[jax.ShapeDtypeStruct(shape, F32) for shape in shapes],
        compiler_params=params(),
        cost_estimate=cost(4),
        name="unpack",
    )(table, a, a_other, b, b_other)


def chunks(value):
    return value.reshape(SEQ, value.shape[0] // SEQ, value.shape[1])


def shards(
    tokens, lengths, cotangent, norm_gain, in_weight, gate_down, gate_up, gate_bias, head_gain,
    out_weight, mlp_gain, up_weight, down_weight,
):
    device = lax.axis_index("dp") * SEQ + lax.axis_index("seq")
    table = lax.dynamic_slice(jnp.asarray(TABLE), (device, 0), (1, 96)).reshape(96)
    tok = tokens.reshape(N, D)
    cot = cotangent.reshape(N, D)
    line = lambda vector: vector.reshape(1, -1)
    flat = lambda value: value.reshape(2, -1, 128)

    down_t, up_t = gate_down.T, gate_up.T
    k, v, normed, ld, cl, logit, low, upd, pieces = project(
        lengths, table, tok, line(norm_gain), in_weight, down_t, up_t, line(gate_bias)
    )
    gathered = exchange(pieces)
    q, og, normed_t, cot_send = project_rest(table, after(normed, pieces), in_weight, cot)
    incoming = prefix(after(gathered, q), gathered, False)
    normed_other, cot_other = swap(after(normed_t, incoming)), swap(after(cot_send, incoming))
    within = local(after(q, incoming), k, v, ld)
    d_hidden = hidden_grad(after(cot, within), down_weight)
    incoming = after(exchange(incoming), d_hidden).reshape(ROWS, HEADS, VHEAD, KHEAD)
    heads, middle, mlp_in, joint = attend(
        q, og, ld, within, cl, incoming, upd, tok, out_weight, line(head_gain), line(mlp_gain)
    )
    output, dmlp, act, act_send, hidden_t = mlp(
        table, after(mlp_in, normed_other, cot_other), d_hidden, up_weight, down_weight, middle
    )
    hidden_other, act_other, joint_other = swap(hidden_t), swap(act_send), swap(joint)
    dmid, datt, g_mlp_gain, g_head_gain, dheads, dog, sends, adj, pieces_back = back(
        table, middle, dmlp, cot, line(mlp_gain), out_weight, line(head_gain), heads, og, q, ld, cl
    )
    sends_other = swap(sends)
    owned = exchange(pieces_back)
    dn_keep, dn_send = down_grad(table, after(hidden_t, pieces_back), hidden_other, cot, cot_other)
    dn_got = along_x(0, after(flat(dn_send), owned))
    owned = prefix(after(owned, dn_keep), gathered, True)
    returned = exchange(owned)
    up_0, up_send_0, up_1, up_send_1 = up_grad(
        table, after(joint, owned, sends_other), joint_other, act, act_other
    )
    up_gots = hops(0, (after(up_send_0, returned), after(up_send_1, returned)))
    keep_o, send_o, keep_g, send_g = outer(
        after(table, up_0),
        [
            (joint, joint_other, 1, datt, sends_other, 0, (0,)),
            (normed_t, normed_other, 0, dog, sends_other, 1, (1,)),
        ],
    )
    four_got = hops(0, (send_o, send_g))
    dn_first = dn_got
    dn_send = halve_x(table, after(flat(dn_keep), keep_o), dn_first)
    dn_got = along_x(1, dn_send)
    returned = after(returned, dn_send).reshape(ROWS, HEADS, VHEAD, KHEAD)
    dproj, dproj_send, dlow, pack = inner(
        lengths, table, q, k, v, dheads, ld, cl, incoming, returned, upd, adj, logit, low, up_t, normed,
        g_head_gain, g_mlp_gain,
    )
    input_grad, pack = input_back(
        dproj, dog, in_weight, dlow, down_t, tok, line(norm_gain), dmid, pack
    )
    dproj_got = swap(after(dproj_send, dn_got, pack, *up_gots, *four_got))
    up = [([(after(up_0, pack), up_gots[0])], []), ([(up_1, up_gots[1])], [])]
    up_sends = halve(table, 1, up)
    up_gots = hops(1, up_sends)
    keep_p, send_p, keep_r, send_r = outer(
        after(table, up_sends[0]),
        [(normed_t, normed_other, 0, dproj, dproj_got, 0, (0, 1))],
        (dn_keep, dn_first.reshape(dn_keep.shape), dn_got.reshape(SEQ, 176, 128), pack),
    )
    first = hops(0, (send_p, send_r))
    add = lambda streams, gots: [(groups, later + [got]) for (groups, later), got in zip(streams, gots)]
    up = add([([(after(up_0, keep_p), up[0][0][0][1])], []), up[1]], up_gots)
    up_sends = halve(table, 2, up)
    up_gots = hops(2, up_sends)
    rest = [
        ([(after(keep_o, up_sends[0]), four_got[0]), (keep_p, first[0])], []),
        ([(keep_g, four_got[1]), (keep_r, first[1])], []),
    ]
    sends = halve(table, 1, rest)
    gots = hops(1, sends)
    up = add(up, up_gots)
    up_sends = halve(after(table, sends[0]), 3, up)
    up_gots = hops(3, up_sends)
    rest = add(rest, gots)
    sends = halve(after(table, up_sends[0]), 2, rest)
    gots = hops(2, sends)
    (early,) = halve(table, 4, add(up, up_gots), [(0, 0, 704, 0, 0), (1, 0, 704, 0, 704)])
    early = early[0]
    early = early + along_x(0, early)
    rest = add(rest, gots)
    sends = halve(after(table, early), 3, rest)
    gots = hops(3, sends)
    early = early + along_x(1, early)
    (late,) = halve(
        after(table, early), 4, add(rest, gots),
        [
            (0, 0, 256, 0, 0), (1, 0, 256, 0, 256), (0, 256, 256, 0, 512), (1, 256, 256, 0, 768),
            (1, 600, 24, 0, 1024), (0, 512, 88, 0, 1048), (1, 512, 88, 0, 1136),
        ],
    )
    late = late[0]
    got = along_x(1, late)
    early_other = swap(early)
    late = jnp.concatenate([late[:1048] + got[:1048], late[1048:], got[1048:]], 0)
    got = along_x(0, late)
    late = jnp.concatenate([late[:1048] + got[:1048], late[1048:], got[1048:]], 0)
    grad_up, grad_down, grad_out, grad_in, g_down, g_upf, g_norm, g_mlp, g_bias, g_head = unpack(
        table, early, early_other, late, swap(late)
    )
    return (
        output.reshape(ROWS, SEG, D),
        input_grad.reshape(ROWS, SEG, D),
        g_norm.reshape(64),
        grad_in,
        g_down.T,
        g_upf.T,
        g_bias.reshape(32),
        g_head.reshape(16),
        grad_out,
        g_mlp.reshape(64),
        grad_up,
        grad_down,
    )


def solution(mesh):
    rows = P("dp", "seq", None)
    return jax.shard_map(
        shards,
        mesh=mesh,
        in_specs=(rows, P("dp"), rows) + (P(),) * 10,
        out_specs=(
            rows, rows, P("seq"), P("seq", None), P("seq", None), P("seq", None), P("seq"), P("seq"),
            P("seq", None), P("seq"), P("seq", None), P("seq", None),
        ),
        check_vma=False,
    )
```

```python
import functools

import jax
import jax.numpy as jnp
import numpy as np
from jax import lax
from jax.experimental import pallas as pl
from jax.experimental.pallas import tpu as pltpu
from jax.sharding import PartitionSpec as P

F32 = jnp.float32
BF16 = jnp.bfloat16
D = 1024
FF = 2816
HEADS = 4
KHEAD = 128
VHEAD = 256
KD = 512
VALUE = 1024
ROWS = 2
SEG = 256
BLK = 128
N = ROWS * SEG
SEQ = 16
TILE = 256
EPSILON = 1e-06
VMEM_LIMIT = 64 * 1024 * 1024


def params(**kw):
    return pltpu.CompilerParams(vmem_limit_bytes=VMEM_LIMIT, **kw)


def cost(us):
    return pl.CostEstimate(flops=0, bytes_accessed=int(us * 3e6), transcendentals=0)


def dot(a, b, ca=1, cb=0):
    return lax.dot_general(a, b, (((ca,), (cb,)), ((), ())), preferred_element_type=F32)


def split(a):
    high = a.astype(BF16)
    return high, (a - high.astype(F32)).astype(BF16)


def dot3(a, b, ca=1, cb=0):
    ah, al = split(a)
    bh, bl = split(b)
    return dot(ah, bh, ca, cb) + (dot(ah, bl, ca, cb) + dot(al, bh, ca, cb))


def dot_ones(ones, b, ca=1, cb=0):
    high = b.astype(BF16)
    rest = b - high.astype(F32)
    mid = rest.astype(BF16)
    low = (rest - mid.astype(F32)).astype(BF16)
    return dot(ones, high, ca, cb) + (dot(ones, mid, ca, cb) + dot(ones, low, ca, cb))


def sigmoid(u):
    return 1.0 / (1.0 + jnp.exp(-u))


def inverse_rms(u):
    return lax.rsqrt(jnp.mean(u * u, -1, keepdims=True) + EPSILON)


def live(lengths_ref, table_ref, row, first, count, width):
    where = lax.broadcasted_iota(jnp.int32, (count, width), 0) + (first + table_ref[46] * SEG)
    return (where < lengths_ref[row]).astype(F32)


def lower(shape):
    return lax.broadcasted_iota(jnp.int32, shape, 0) >= lax.broadcasted_iota(jnp.int32, shape, 1)


def proj_kernel(
    lengths_ref, table_ref, tok_ref, gain_ref, w_ref, gd_ref, gu_ref, gb_ref,
    k_ref, v_ref, normed_ref, ld_ref, cl_ref, logit_ref, low_ref, upd_ref, out_ref,
    kc_ref,
):
    n = pl.program_id(0)

    @pl.when(n == 0)
    def _():
        inputs = tok_ref[...].astype(F32)
        normed = (inputs * inverse_rms(inputs) * gain_ref[...].astype(F32)).astype(BF16)
        normed_ref[...] = normed
        low = dot(normed, gd_ref[...], 1, 1)
        low_ref[...] = low
        low_high, low_low = split(low)
        logit = dot(low_high, gu_ref[...]) + dot(low_low, gu_ref[...])
        logit = logit + gb_ref[...].astype(F32)
        logit_ref[...] = logit
        ones = lower((BLK, BLK)).astype(BF16)
        key = dot(normed, w_ref[...])
        for row in range(ROWS):
            for part in range(SEG // BLK):
                at = row * SEG + part * BLK
                here = slice(at, at + BLK)
                alive = live(lengths_ref, table_ref, row, part * BLK, BLK, KD)
                u = logit[here]
                log_gate = (jnp.minimum(u, 0.0) - jnp.log1p(jnp.exp(-jnp.abs(u)))) * (1.0 / 16.0)
                decay = dot_ones(ones, log_gate * alive)
                ld_ref[here] = decay
                m = row * (SEG // BLK) + part
                closing = decay[BLK - 1 : BLK]
                cl_ref[m : m + 1] = closing
                k_ref[here] = key[here] * alive
                kc_ref[here] = key[here] * alive * jnp.exp(closing - decay)
        cl_ref[4:8] = jnp.zeros((4, KD), F32)

    for step in (1, 2):

        @pl.when(n == step)
        def _():
            acc = dot(normed_ref[...], w_ref[...])
            for row in range(ROWS):
                values = []
                for part in range(SEG // BLK):
                    at = row * SEG + part * BLK
                    value = acc[at : at + BLK] * live(lengths_ref, table_ref, row, part * BLK, BLK, KD)
                    v_ref[at : at + BLK] = value
                    values.append(value)
                for sub in range(2):
                    head = (step - 1) * 2 + sub
                    chan = slice(head * KHEAD, (head + 1) * KHEAD)
                    total = None
                    for part in range(SEG // BLK):
                        at = row * SEG + part * BLK
                        m = row * (SEG // BLK) + part
                        update = dot3(
                            values[part][:, sub * VHEAD : (sub + 1) * VHEAD],
                            kc_ref[at : at + BLK, chan], 0, 0,
                        )
                        upd_ref[row, part, head] = update
                        if total is None:
                            total = update
                        else:
                            total = jnp.exp(cl_ref[m : m + 1, chan]) * total + update
                    base = row * (SEG // BLK)
                    gone = cl_ref[base : base + 1, chan] + cl_ref[base + 1 : base + 2, chan]
                    for half in range(2):
                        piece = (row * HEADS + head) * 2 + half
                        out_ref[piece, 0:128] = total[half * 128 : (half + 1) * 128]
                        out_ref[piece, 128:136] = jnp.broadcast_to(gone, (8, KHEAD))


def project(lengths, table, tokens, gain, w, gd, gu, gb):
    full = lambda shape: pl.BlockSpec(shape, lambda n, s, c: (0,) * len(shape))
    return pl.pallas_call(
        proj_kernel,
        grid_spec=pltpu.PrefetchScalarGridSpec(
            num_scalar_prefetch=2,
            grid=(3,),
            in_specs=[
                full((N, D)), full((1, D)), pl.BlockSpec((D, KD), lambda n, s, c: (0, n + 1)),
                full((16, D)), full((16, KD)), pl.BlockSpec((1, KD), lambda n, s, c: (0, 4)),
            ],
            out_specs=[
                full((N, KD)), pl.BlockSpec((N, KD), lambda n, s, c: (0, jnp.maximum(n - 1, 0))),
                full((N, D)), full((N, KD)), full((8, KD)),
                full((N, KD)), full((N, 16)), full((ROWS, 2, HEADS, VHEAD, KHEAD)),
                full((SEQ, 136, KHEAD)),
            ],
            scratch_shapes=[pltpu.VMEM((N, KD), F32)],
        ),
        out_shape=[
            jax.ShapeDtypeStruct((N, KD), F32), jax.ShapeDtypeStruct((N, VALUE), F32),
            jax.ShapeDtypeStruct((N, D), BF16),
            jax.ShapeDtypeStruct((N, KD), F32), jax.ShapeDtypeStruct((8, KD), F32),
            jax.ShapeDtypeStruct((N, KD), F32), jax.ShapeDtypeStruct((N, 16), F32),
            jax.ShapeDtypeStruct((ROWS, 2, HEADS, VHEAD, KHEAD), F32),
            jax.ShapeDtypeStruct((SEQ, 136, KHEAD), F32),
        ],
        compiler_params=params(),
        cost_estimate=cost(10),
        name="project",
    )(lengths, table, tokens, gain, w, gd, gu, gb)


def rest_kernel(table_ref, normed_ref, w_ref, cot_ref, q_ref, og_ref, normt_ref, cots_ref):
    n = pl.program_id(0)
    acc = dot(normed_ref[...], w_ref[...])

    @pl.when(n == 0)
    def _():
        q_ref[...] = acc * KHEAD ** (-0.5)
        normt_ref[...] = normed_ref[...].T.astype(F32)

    @pl.when(n > 0)
    def _():
        og_ref[...] = acc

    @pl.when(n == 2)
    def _():
        cots_ref[...] = cot_ref[:, pl.ds(pl.multiple_of((1 - table_ref[40]) * 512, 512), 512)].astype(F32)


def project_rest(table, normed, w, cot):
    full = lambda shape: pl.BlockSpec(shape, lambda n, c: (0,) * len(shape))
    return pl.pallas_call(
        rest_kernel,
        grid_spec=pltpu.PrefetchScalarGridSpec(
            num_scalar_prefetch=1,
            grid=(3,),
            in_specs=[
                full((N, D)), pl.BlockSpec((D, KD), lambda n, c: (0, jnp.where(n == 0, 0, n + 3))), full((N, D)),
            ],
            out_specs=[
                full((N, KD)), pl.BlockSpec((N, KD), lambda n, c: (0, jnp.maximum(n - 1, 0))),
                full((D, N)), full((N, KD)),
            ],
        ),
        out_shape=[
            jax.ShapeDtypeStruct((N, KD), F32), jax.ShapeDtypeStruct((N, VALUE), F32),
            jax.ShapeDtypeStruct((D, N), F32), jax.ShapeDtypeStruct((N, KD), F32),
        ],
        compiler_params=params(),
        cost_estimate=cost(0.1),
        name="project_rest",
    )(table, normed, w, cot)


def local_kernel(q_ref, k_ref, v_ref, ld_ref, out_ref):
    mask = lower((BLK, BLK))
    for head in range(HEADS):
        chan = slice(head * KHEAD, (head + 1) * KHEAD)
        vals = slice(head * VHEAD, (head + 1) * VHEAD)
        decay = ld_ref[:, chan]
        centre = decay[BLK // 2 - 1 : BLK // 2]
        scores = dot3(q_ref[:, chan] * jnp.exp(decay - centre), k_ref[:, chan] * jnp.exp(centre - decay), 1, 1)
        out_ref[:, vals] = dot3(jnp.where(mask, scores, 0.0), v_ref[:, vals])


def local(q, k, v, ld):
    rows = lambda width: pl.BlockSpec((BLK, width), lambda m: (m, 0))
    return pl.pallas_call(
        local_kernel,
        grid=(4,),
        in_specs=[rows(KD), rows(KD), rows(VALUE), rows(KD)],
        out_specs=rows(VALUE),
        out_shape=jax.ShapeDtypeStruct((N, VALUE), F32),
        compiler_params=params(),
        cost_estimate=cost(0.1),
        name="local",
    )(q, k, v, ld)


def hidden_kernel(cot_ref, wd_ref, out_ref):
    out_ref[...] = dot(cot_ref[...], wd_ref[...], 1, 1)


def hidden_grad(cot, dnw):
    return pl.pallas_call(
        hidden_kernel,
        grid=(2,),
        in_specs=[pl.BlockSpec((N, D), lambda t: (0, 0)), pl.BlockSpec((FF // 2, D), lambda t: (t, 0))],
        out_specs=pl.BlockSpec((N, FF // 2), lambda t: (0, t)),
        out_shape=jax.ShapeDtypeStruct((N, FF), F32),
        compiler_params=params(),
        cost_estimate=cost(0.1),
        name="hidden_grad",
    )(cot, dnw)


def prefix_kernel(backward, part_ref, decay_ref, out_ref):
    run = jnp.zeros((128, KHEAD), F32)
    order = range(SEQ - 1, -1, -1) if backward else range(SEQ)
    for seg in order:
        out_ref[seg] = run
        run = jnp.exp(decay_ref[seg, 0:1]) * run + part_ref[seg, 0:128]


def prefix(parts, decays, backward):
    return pl.pallas_call(
        functools.partial(prefix_kernel, backward),
        grid=(1,),
        in_specs=[
            pl.BlockSpec((SEQ, 128, KHEAD), lambda n: (0, 0, 0)),
            pl.BlockSpec((SEQ, 8, KHEAD), lambda n: (0, 16, 0)),
        ],
        out_specs=pl.BlockSpec((SEQ, 128, KHEAD), lambda n: (0, 0, 0)),
        out_shape=jax.ShapeDtypeStruct((SEQ, 128, KHEAD), F32),
        compiler_params=params(),
        cost_estimate=cost(0.1),
        name="prefix",
    )(parts, decays)


def attend_kernel(
    q_ref, og_ref, ld_ref, within_ref, cl_ref, inc_ref, upd_ref, tok_ref, ow_ref, hg_ref, mg_ref,
    heads_ref, middle_ref, mlp_ref, both_ref,
    mixed_ref,
):
    m = pl.program_id(0)
    second = lax.rem(m, 2) == 1
    previous = cl_ref[pl.ds(m - lax.rem(m, 2), 1), :]
    gain = hg_ref[...].astype(F32)
    for head in range(HEADS):
        chan = slice(head * KHEAD, (head + 1) * KHEAD)
        vals = slice(head * VHEAD, (head + 1) * VHEAD)
        start = inc_ref[0, head]
        start = jnp.where(second, jnp.exp(previous[:, chan]) * start + upd_ref[0, 0, head], start)
        out = within_ref[:, vals] + dot3(q_ref[:, chan] * jnp.exp(ld_ref[:, chan]), start, 1, 1)
        heads_ref[:, vals] = out
        gate = og_ref[:, vals]
        mixed = out * inverse_rms(out) * gain * (gate * sigmoid(gate))
        mixed_ref[:, vals] = mixed.astype(BF16)

    middle = tok_ref[...].astype(F32) + dot(mixed_ref[...], ow_ref[...])
    middle_ref[...] = middle
    mlp_in = (middle * inverse_rms(middle) * mg_ref[...].astype(F32)).astype(BF16)
    mlp_ref[...] = mlp_in
    both_ref[:D] = mlp_in.T.astype(F32)
    both_ref[D:] = mixed_ref[...].T.astype(F32)


def attend(q, og, ld, within, cl, incoming, upd, tokens, ow, hg, mg):
    full = lambda shape: pl.BlockSpec(shape, lambda m: (0,) * len(shape))
    rows = lambda width: pl.BlockSpec((BLK, width), lambda m: (m, 0))
    return pl.pallas_call(
        attend_kernel,
        grid=(4,),
        in_specs=[
            rows(KD), rows(VALUE), rows(KD), rows(VALUE), full((8, KD)),
            pl.BlockSpec((1, HEADS, VHEAD, KHEAD), lambda m: (m // 2, 0, 0, 0)),
            pl.BlockSpec((1, 1, HEADS, VHEAD, KHEAD), lambda m: (m // 2, 0, 0, 0, 0)),
            rows(D), full((VALUE, D)), pl.BlockSpec((1, VHEAD), lambda m: (0, 10)),
            pl.BlockSpec((1, D), lambda m: (0, 1)),
        ],
        out_specs=[
            rows(VALUE), rows(D), rows(D), pl.BlockSpec((D + VALUE, BLK), lambda m: (0, m)),
        ],
        out_shape=[
            jax.ShapeDtypeStruct((N, VALUE), F32), jax.ShapeDtypeStruct((N, D), F32),
            jax.ShapeDtypeStruct((N, D), BF16), jax.ShapeDtypeStruct((D + VALUE, N), F32),
        ],
        scratch_shapes=[pltpu.VMEM((BLK, VALUE), BF16)],
        compiler_params=params(),
        cost_estimate=cost(13),
        name="attend",
    )(q, og, ld, within, cl, incoming, upd, tokens, ow, hg, mg)


TILES = FF // TILE


def mlp_kernel(
    core_ref, mlp_ref, dh_ref, wg_ref, wu_ref, wd_ref, middle_ref,
    out_ref, dmlp_ref, own_ref, send_ref, hidt_ref, acc_ref,
):
    t = pl.program_id(0)

    @pl.when(t == 0)
    def _():
        acc_ref[...] = middle_ref[...]
        dmlp_ref[...] = jnp.zeros((N, D), F32)

    mlp_in = mlp_ref[...]
    gate = dot(mlp_in, wg_ref[...])
    up = dot(mlp_in, wu_ref[...])
    d_hidden = dh_ref[...]
    sig = sigmoid(gate)
    act = gate * sig
    hidden = (act * up).astype(BF16)
    d_gate = (d_hidden * up * (sig * (1.0 + gate * (1.0 - sig)))).astype(BF16)
    d_up = (d_hidden * act).astype(BF16)
    acc_ref[...] += dot(hidden, wd_ref[...])
    dmlp_ref[...] += dot(d_gate, wg_ref[...], 1, 1) + dot(d_up, wu_ref[...], 1, 1)
    first = core_ref[40] == 0
    own_ref[...] = jnp.where(first, d_gate, d_up)
    send_ref[...] = jnp.where(first, d_up, d_gate).astype(F32)
    hidt_ref[...] = hidden.T.astype(F32)

    @pl.when(t == TILES - 1)
    def _():
        out_ref[...] = acc_ref[...].astype(BF16)


def mlp(core, mlp_in, d_hidden, upw, dnw, middle):
    full = lambda shape: pl.BlockSpec(shape, lambda t, c: (0,) * len(shape))
    column = lambda rows: pl.BlockSpec((rows, TILE), lambda t, c: (0, t))
    return pl.pallas_call(
        mlp_kernel,
        grid_spec=pltpu.PrefetchScalarGridSpec(
            num_scalar_prefetch=1,
            grid=(TILES,),
            in_specs=[
                full((N, D)), column(N), column(D),
                pl.BlockSpec((D, TILE), lambda t, c: (0, TILES + t)),
                pl.BlockSpec((TILE, D), lambda t, c: (t, 0)), full((N, D)),
            ],
            out_specs=[
                full((N, D)), full((N, D)), column(N), column(N),
                pl.BlockSpec((TILE, N), lambda t, c: (t, 0)),
            ],
            scratch_shapes=[pltpu.VMEM((N, D), F32)],
        ),
        out_shape=[
            jax.ShapeDtypeStruct((N, D), BF16), jax.ShapeDtypeStruct((N, D), F32),
            jax.ShapeDtypeStruct((N, FF), BF16), jax.ShapeDtypeStruct((N, FF), F32),
            jax.ShapeDtypeStruct((FF, N), F32),
        ],
        compiler_params=params(),
        cost_estimate=cost(30),
        name="mlp",
    )(core, mlp_in, d_hidden, upw, upw, dnw, middle)


def down_grad_kernel(
    table_ref, hid_ref, hid_other, cot_ref, cot_other, keep_ref, send_ref, cotb_ref, hidb_ref
):
    @pl.when(pl.program_id(0) == 0)
    def _():
        cotb_ref[:N] = cot_ref[...]
        cotb_ref[N:] = cot_other[...].astype(BF16)

    hidb_ref[:, :N] = hid_ref[...].reshape(TILE, N).astype(BF16)
    hidb_ref[:, N:] = hid_other[...].reshape(TILE, N).astype(BF16)
    down = dot(hidb_ref[...], cotb_ref[...]).reshape(SEQ, 16, 512)
    for slab in range(4):
        slot = table_ref[41 + slab]

        @pl.when(slot < 2)
        def _():
            keep_ref[slot] = down[:, :, slab * 128 : (slab + 1) * 128]

        @pl.when(slot >= 2)
        def _():
            send_ref[slot - 2] = down[:, :, slab * 128 : (slab + 1) * 128]


def down_grad(table, hid, hid_other, cot, cot_other):
    tall = pl.BlockSpec((SEQ, 16, N), lambda t, c: (0, t, 0))
    out = pl.BlockSpec((2, SEQ, 16, 128), lambda t, c: (0, 0, t, 0))
    return pl.pallas_call(
        down_grad_kernel,
        grid_spec=pltpu.PrefetchScalarGridSpec(
            num_scalar_prefetch=1,
            grid=(TILES,),
            in_specs=[
                tall, tall, pl.BlockSpec((N, 512), lambda t, c: (0, c[40])),
                pl.BlockSpec((N, 512), lambda t, c: (0, 0)),
            ],
            out_specs=[out, out],
            scratch_shapes=[pltpu.VMEM((2 * N, 512), BF16), pltpu.VMEM((TILE, 2 * N), BF16)],
        ),
        out_shape=[jax.ShapeDtypeStruct((2, SEQ, 176, 128), F32)] * 2,
        compiler_params=params(),
        cost_estimate=cost(0.1),
        name="down_grad",
    )(table, chunks(hid), chunks(hid_other), cot, cot_other)


def up_grad_kernel(
    table_ref, mlpt_ref, mlpt_other, act_ref, act_other, keep_0, send_0, keep_1, send_1,
    left_ref, right_ref, value_ref,
):
    @pl.when(pl.program_id(0) == 0)
    def _():
        left_ref[:, :N] = mlpt_ref[...].astype(BF16)
        left_ref[:, N:] = mlpt_other[...].astype(BF16)

    right_ref[:N] = act_ref[...]
    right_ref[N:] = act_other[...].astype(BF16)
    value_ref[...] = dot(left_ref[...], right_ref[...])
    for v, (keep_ref, send_ref) in enumerate(((keep_0, send_0), (keep_1, send_1))):
        cols = slice(v * 128, v * 128 + 128)
        for index in range(8):
            keep_ref[index] = value_ref[chunk_rows(table_ref, v, index), cols]
            send_ref[index] = value_ref[chunk_rows(table_ref, v, 8 + index), cols]


def chunk_rows(table_ref, v, index):
    return pl.ds(pl.multiple_of(table_ref[v * 16 + index] * 64, 64), 64)


def up_grad(table, mlpt, mlpt_other, act, act_other):
    full = lambda shape: pl.BlockSpec(shape, lambda t, c: (0,) * len(shape))
    wide = pl.BlockSpec((N, TILE), lambda t, c: (0, t))
    return pl.pallas_call(
        up_grad_kernel,
        grid_spec=pltpu.PrefetchScalarGridSpec(
            num_scalar_prefetch=1,
            grid=(TILES,),
            in_specs=[full((D, N)), full((D, N)), wide, wide],
            out_specs=[pl.BlockSpec((8, 64, 128), lambda t, c: (0, t, 0))] * 4,
            scratch_shapes=[
                pltpu.VMEM((D, 2 * N), BF16), pltpu.VMEM((2 * N, TILE), BF16), pltpu.VMEM((D, TILE), F32),
            ],
        ),
        out_shape=[jax.ShapeDtypeStruct((8, TILES * 64, 128), F32)] * 4,
        compiler_params=params(),
        cost_estimate=cost(0.1),
        name="up_grad",
    )(table, mlpt, mlpt_other, act, act_other)


def back_kernel(
    core_ref, middle_ref, dmlp_ref, cot_ref, mg_ref, ow_ref, hg_ref, heads_ref, og_ref, q_ref, ld_ref, cl_ref,
    dmid_ref, datt_ref, mgg_ref, hgg_ref, dheads_ref, dog_ref, sends_ref, adj_ref, out_ref,
    dmix_ref,
):
    away = pl.ds(pl.multiple_of((1 - core_ref[40]) * 512, 512), 512)
    m = pl.program_id(0)

    @pl.when(m == 0)
    def _():
        mgg_ref[...] = jnp.zeros((1, D), F32)
        hgg_ref[...] = jnp.zeros((1, VHEAD), F32)

    middle = middle_ref[...]
    scale_two = inverse_rms(middle)
    unit_two = middle * scale_two
    grad = dmlp_ref[...]
    mgg_ref[...] += jnp.sum(grad * unit_two, 0, keepdims=True)
    scaled = grad * mg_ref[...].astype(F32)
    d_middle = scale_two * (scaled - unit_two * jnp.mean(scaled * unit_two, -1, keepdims=True))
    d_middle = d_middle + cot_ref[...].astype(F32)
    dmid_ref[...] = d_middle
    datt_ref[...] = d_middle.astype(BF16)
    dmix_ref[...] = dot(datt_ref[...], ow_ref[...], 1, 1)
    block = m + 1 - 2 * lax.rem(m, 2)
    first = lax.rem(m, 2) == 0
    closing = cl_ref[pl.ds(block, 1), :]
    gain = hg_ref[...].astype(F32)
    for head in range(HEADS):
        chan = slice(head * KHEAD, (head + 1) * KHEAD)
        vals = slice(head * VHEAD, (head + 1) * VHEAD)
        out = heads_ref[:, vals]
        scale = inverse_rms(out)
        unit = out * scale
        gate = og_ref[:, vals]
        sig = sigmoid(gate)
        act = gate * sig
        d_mixed = dmix_ref[:, vals]
        dog_ref[:, vals] = (d_mixed * (unit * gain) * (sig * (1.0 + gate * (1.0 - sig)))).astype(BF16)
        d_norm = d_mixed * act
        hgg_ref[...] += jnp.sum(d_norm * unit, 0, keepdims=True)
        scaled = d_norm * gain
        d_out = scale * (scaled - unit * jnp.mean(scaled * unit, -1, keepdims=True))
        dheads_ref[:, vals] = d_out
        adjoint = dot3(d_out, q_ref[:, chan] * jnp.exp(ld_ref[:, chan]), 0, 0)

        @pl.when(first)
        def _():
            adj_ref[0, head] = adjoint

        @pl.when(jnp.logical_not(first))
        def _():
            total = jnp.exp(closing[:, chan]) * adj_ref[0, head] + adjoint
            for half in range(2):
                out_ref[head * 2 + half] = total[half * 128 : (half + 1) * 128]

    sends_ref[:, :512] = datt_ref[:, away].astype(F32)
    sends_ref[:, 512:] = dog_ref[:, away].astype(F32)


def back(core, middle, dmlp, cot, mg, ow, hg, heads, og, q, ld, cl):
    full = lambda shape: pl.BlockSpec(shape, lambda m, c: (0,) * len(shape))
    block = lambda m: m + 1 - 2 * lax.rem(m, 2)
    wide = pl.BlockSpec((BLK, D), lambda m, c: (block(m), 0))
    return pl.pallas_call(
        back_kernel,
        grid_spec=pltpu.PrefetchScalarGridSpec(num_scalar_prefetch=1, grid=(4,), in_specs=[
            wide, wide, wide, pl.BlockSpec((1, D), lambda m, c: (0, 1)), full((VALUE, D)),
            pl.BlockSpec((1, VHEAD), lambda m, c: (0, 10)),
            pl.BlockSpec((BLK, VALUE), lambda m, c: (block(m), 0)),
            pl.BlockSpec((BLK, VALUE), lambda m, c: (block(m), 0)),
            pl.BlockSpec((BLK, KD), lambda m, c: (block(m), 0)),
            pl.BlockSpec((BLK, KD), lambda m, c: (block(m), 0)),
            full((8, KD)),
        ],
        out_specs=[
            wide, wide, full((1, D)), full((1, VHEAD)),
            pl.BlockSpec((BLK, VALUE), lambda m, c: (block(m), 0)),
            pl.BlockSpec((BLK, VALUE), lambda m, c: (block(m), 0)),
            pl.BlockSpec((BLK, D), lambda m, c: (block(m), 0)),
            pl.BlockSpec((1, HEADS, VHEAD, KHEAD), lambda m, c: (m // 2, 0, 0, 0)),
            pl.BlockSpec((8, 128, KHEAD), lambda m, c: (m // 2, 0, 0)),
        ],
        scratch_shapes=[pltpu.VMEM((BLK, VALUE), F32)]),
        out_shape=[
            jax.ShapeDtypeStruct((N, D), F32), jax.ShapeDtypeStruct((N, D), BF16),
            jax.ShapeDtypeStruct((1, D), F32), jax.ShapeDtypeStruct((1, VHEAD), F32),
            jax.ShapeDtypeStruct((N, VALUE), F32), jax.ShapeDtypeStruct((N, VALUE), BF16),
            jax.ShapeDtypeStruct((N, D), F32),
            jax.ShapeDtypeStruct((ROWS, HEADS, VHEAD, KHEAD), F32),
            jax.ShapeDtypeStruct((SEQ, 128, KHEAD), F32),
        ],
                compiler_params=params(),
        cost_estimate=cost(30),
        name="back",
    )(core, middle, dmlp, cot, mg, ow, hg, heads, og, q, ld, cl)


def inner_kernel(
    limit_ref, core_ref, q_ref, k_ref, v_ref, dout_ref, ld_ref, cl_ref, inc_ref, ret_ref, upd_ref, adj_ref,
    logit_ref, low_ref, gu_ref, normed_ref, hg_ref, mg_ref,
    dproj_ref, dprojs_ref, dlow_ref, pack_ref,
    dlg_ref, gb_ref, gup_ref, gdn_ref,
):
    m = pl.program_id(0)
    row = m // 2
    part = lax.rem(m, 2)
    second = part == 1

    @pl.when(m == 0)
    def _():
        gb_ref[...] = jnp.zeros((1, KD), F32)
        gup_ref[...] = jnp.zeros((16, KD), F32)
        gdn_ref[...] = jnp.zeros((16, D), F32)

    mask = lower((BLK, BLK))
    upper = lax.broadcasted_iota(jnp.int32, (BLK, BLK), 0) <= lax.broadcasted_iota(jnp.int32, (BLK, BLK), 1)
    upper = upper.astype(BF16)
    closing = cl_ref[pl.ds(m, 1), :]
    previous = cl_ref[pl.ds(row * 2, 1), :]
    following = cl_ref[pl.ds(row * 2 + 1, 1), :]
    alive = live(limit_ref, core_ref, row, part * BLK, BLK, VHEAD)
    alive_key = alive[:, :KHEAD]
    for head in range(HEADS):
        chan = slice(head * KHEAD, (head + 1) * KHEAD)
        vals = slice(head * VHEAD, (head + 1) * VHEAD)
        start = inc_ref[0, head]
        start = jnp.where(second, jnp.exp(previous[:, chan]) * start + upd_ref[0, 0, head], start)
        update = jnp.where(second, upd_ref[0, 1, head], upd_ref[0, 0, head])
        end_state = jnp.exp(closing[:, chan]) * start + update
        end_grad = ret_ref[0, head]
        end_grad = jnp.where(second, end_grad, jnp.exp(following[:, chan]) * end_grad + adj_ref[0, head])
        decay = ld_ref[:, chan]
        centre = decay[BLK // 2 - 1 : BLK // 2]
        query = q_ref[:, chan]
        key = k_ref[:, chan]
        value = v_ref[:, vals]
        d_out = dout_ref[:, vals]
        up_factor = jnp.exp(decay - centre)
        down_factor = jnp.exp(centre - decay)
        query_mid = query * up_factor
        key_mid = key * down_factor
        close_factor = jnp.exp(closing[:, chan] - decay)
        scores = jnp.where(mask, dot3(query_mid, key_mid, 1, 1), 0.0)
        d_scores = jnp.where(mask, dot3(d_out, value, 1, 1), 0.0)
        d_query = up_factor * dot3(d_scores, key_mid) + jnp.exp(decay) * dot3(d_out, start)
        d_key = down_factor * dot3(d_scores, query_mid, 0, 0) + close_factor * dot3(value, end_grad)
        d_value = dot3(scores, d_out, 0, 0) + dot3(key * close_factor, end_grad, 1, 1)
        d_decay = query * d_query - key * d_key
        dlg_ref[:, chan] = dot_ones(upper, d_decay) + jnp.sum(end_grad * end_state, 0, keepdims=True)
        dproj_ref[:, chan] = (d_query * KHEAD ** (-0.5)).astype(BF16)
        dproj_ref[:, KD + head * KHEAD : KD + (head + 1) * KHEAD] = (d_key * alive_key).astype(BF16)
        dproj_ref[:, 2 * KD + head * VHEAD : 2 * KD + (head + 1) * VHEAD] = (d_value * alive).astype(BF16)
    alive_gate = live(limit_ref, core_ref, row, part * BLK, BLK, KD)
    d_logit = dlg_ref[...] * alive_gate * (1.0 / (1.0 + jnp.exp(logit_ref[...]))) * (1.0 / 16.0)
    gb_ref[...] += jnp.sum(d_logit, 0, keepdims=True)
    gup_ref[...] += dot3(low_ref[...], d_logit, 0, 0)
    high, rest = split(d_logit)
    d_low = (dot(high, gu_ref[...], 1, 1) + dot(rest, gu_ref[...], 1, 1)).astype(BF16)
    dlow_ref[...] = d_low
    gdn_ref[...] += dot(d_low, normed_ref[...], 0, 0)
    away = pl.ds(pl.multiple_of((1 - core_ref[40]) * 1024, 1024), 1024)
    dprojs_ref[...] = dproj_ref[:, away].astype(F32)

    @pl.when(m == 3)
    def _():
        pack_ref[:, 16:24] = jnp.zeros((SEQ, 8, 128), F32)
        for chunk in range(SEQ):
            pack_ref[chunk, :16, :64] = gdn_ref[:, chunk * 64 : chunk * 64 + 64]
            pack_ref[chunk, :16, 64:96] = gup_ref[:, chunk * 32 : chunk * 32 + 32]
            pack_ref[chunk, :16, 96:] = jnp.zeros((16, 32), F32)
            pack_ref[chunk, 16:17, 64:] = mg_ref[:, chunk * 64 : chunk * 64 + 64]
            pack_ref[chunk, 17:18, :32] = gb_ref[:, chunk * 32 : chunk * 32 + 32]
            pack_ref[chunk, 17:18, 32:48] = hg_ref[:, chunk * 16 : chunk * 16 + 16]


def inner(limit, core, q, k, v, dout, ld, cl, incoming, returned, upd, adj, logit, low, gu, normed, hg, mg):
    full = lambda shape: pl.BlockSpec(shape, lambda m, s, c: (0,) * len(shape))
    by_row = pl.BlockSpec((1, HEADS, VHEAD, KHEAD), lambda m, s, c: (m // 2, 0, 0, 0))
    return pl.pallas_call(
        inner_kernel,
        grid_spec=pltpu.PrefetchScalarGridSpec(
            num_scalar_prefetch=2,
            grid=(4,),
            in_specs=[
                pl.BlockSpec((BLK, KD), lambda m, s, c: (m, 0)), pl.BlockSpec((BLK, KD), lambda m, s, c: (m, 0)),
                pl.BlockSpec((BLK, VALUE), lambda m, s, c: (m, 0)), pl.BlockSpec((BLK, VALUE), lambda m, s, c: (m, 0)),
                pl.BlockSpec((BLK, KD), lambda m, s, c: (m, 0)), full((8, KD)),
                by_row, by_row,
                pl.BlockSpec((1, 2, HEADS, VHEAD, KHEAD), lambda m, s, c: (m // 2, 0, 0, 0, 0)),
                by_row,
                pl.BlockSpec((BLK, KD), lambda m, s, c: (m, 0)), pl.BlockSpec((BLK, 16), lambda m, s, c: (m, 0)),
                full((16, KD)), pl.BlockSpec((BLK, D), lambda m, s, c: (m, 0)), full((1, VHEAD)), full((1, D)),
            ],
            out_specs=[
                pl.BlockSpec((BLK, 2048), lambda m, s, c: (m, 0)),
                pl.BlockSpec((BLK, 1024), lambda m, s, c: (m, 0)), pl.BlockSpec((BLK, 16), lambda m, s, c: (m, 0)),
                full((SEQ, 24, 128)),
            ],
            scratch_shapes=[
                pltpu.VMEM((BLK, KD), F32), pltpu.VMEM((1, KD), F32), pltpu.VMEM((16, KD), F32), pltpu.VMEM((16, D), F32),
            ],
        ),
        out_shape=[
            jax.ShapeDtypeStruct((N, 2048), BF16), jax.ShapeDtypeStruct((N, 1024), F32), jax.ShapeDtypeStruct((N, 16), BF16),
            jax.ShapeDtypeStruct((SEQ, 24, 128), F32),
        ],
        compiler_params=params(),
        cost_estimate=cost(300),
        name="inner",
    )(limit, core, q, k, v, dout, ld, cl, incoming, returned, upd, adj, logit, low, gu, normed, hg, mg)


def outer_kernel(sets, extras, table_ref, *refs):
    count = 4 * len(sets)
    more, outs = refs[count : count + extras], refs[count + extras : -3]
    left_ref, right_ref, value_ref = refs[-3:]
    at = 0
    for which, streams in enumerate(sets):
        x_ref, x_other, y_ref, y_other = refs[4 * which : 4 * which + 4]
        left_ref[:, :N] = x_ref[...].astype(BF16)
        left_ref[:, N:] = x_other[...].astype(BF16)
        for part, v in enumerate(streams):
            cols = slice(part * 512, (part + 1) * 512)
            right_ref[:N] = y_ref[:, cols]
            right_ref[N:] = y_other[:, cols].astype(BF16)
            value_ref[...] = dot(left_ref[...], right_ref[...])
            for side, target in enumerate(outs[2 * at : 2 * at + 2]):
                for index in range(8):
                    rows = chunk_rows(table_ref, v, side * 8 + index)
                    for slab in range(4):
                        target[index, slab * 64 : slab * 64 + 64] = value_ref[rows, slab * 128 : slab * 128 + 128]
                    if extras:
                        own, first, got, pack = more
                        chunk = table_ref[v * 16 + side * 8 + index]
                        cut = slice(v * 88, v * 88 + 88)
                        target[index, 256:344] = own[0, chunk, cut] + first[0, chunk, cut] + got[chunk, cut]
                        if v == 1:
                            target[index, 344:368] = pack[chunk]
            at += 1


def outer(table, sets, more=()):
    operands, specs, outs = [], [], []
    for x, x_other, rows, y, y_other, cols, streams in sets:
        width = 512 * len(streams)
        operands += [x, x_other, y, y_other]
        specs += [
            pl.BlockSpec((D, N), lambda i, t, r=rows: (r, 0)), pl.BlockSpec((D, N), lambda i, t, r=rows: (r, 0)),
            pl.BlockSpec((N, width), lambda i, t: (0, t[40])), pl.BlockSpec((N, width), lambda i, t, c=cols: (0, c)),
        ]
        for v in streams:
            total = 256 + (88 + 24 * v if more else 0)
            outs += [jax.ShapeDtypeStruct((8, total, 128), F32)] * 2
    for array in more:
        operands.append(array)
        if array.ndim == 4:
            specs.append(pl.BlockSpec((1,) + array.shape[1:], lambda i, t: (t[45], 0, 0, 0)))
        else:
            specs.append(pl.BlockSpec(array.shape, lambda i, t: (0, 0, 0)))
    return pl.pallas_call(
        functools.partial(outer_kernel, [streams for *_, streams in sets], len(more)),
        grid_spec=pltpu.PrefetchScalarGridSpec(
            num_scalar_prefetch=1, grid=(1,), in_specs=specs,
            out_specs=[pl.BlockSpec(out.shape, lambda i, t: (0, 0, 0)) for out in outs],
            scratch_shapes=[
                pltpu.VMEM((D, 2 * N), BF16), pltpu.VMEM((2 * N, 512), BF16), pltpu.VMEM((D, 512), F32),
            ],
        ),
        out_shape=outs,
        compiler_params=params(),
        cost_estimate=cost(0.1),
        name="outer",
    )(table, *operands)


def input_kernel(
    y_ref, og_ref, w_ref, dlow_ref, gd_ref, tok_ref, gain_ref, dmid_ref, pack_in,
    grad_ref, pack_ref, acc_ref,
):
    t = pl.program_id(0)

    @pl.when(t == 0)
    def _():
        acc_ref[...] = dot(dlow_ref[...], gd_ref[...])

    @pl.when(t < 4)
    def _():
        acc_ref[...] += dot(y_ref[...], w_ref[...], 1, 1)

    @pl.when(t >= 4)
    def _():
        acc_ref[...] += dot(og_ref[...], w_ref[...], 1, 1)

    @pl.when(t == 5)
    def _():
        total = jnp.zeros((1, D), F32)
        for at in range(0, N, 128):
            here = slice(at, at + 128)
            inputs = tok_ref[here].astype(F32)
            scale = inverse_rms(inputs)
            unit = inputs * scale
            grad = acc_ref[here]
            total = total + jnp.sum(grad * unit, 0, keepdims=True)
            scaled = grad * gain_ref[...].astype(F32)
            d_inputs = scale * (scaled - unit * jnp.mean(scaled * unit, -1, keepdims=True))
            grad_ref[here] = (dmid_ref[here] + d_inputs).astype(BF16)
        pack_ref[...] = pack_in[...]
        for chunk in range(SEQ):
            pack_ref[chunk, 16:17, :64] = total[:, chunk * 64 : chunk * 64 + 64]


def input_back(y, og, w, dlow, gd, tokens, gain, dmid, pack):
    full = lambda shape: pl.BlockSpec(shape, lambda t: (0,) * len(shape))
    return pl.pallas_call(
        input_kernel,
        grid=(6,),
        in_specs=[
            pl.BlockSpec((N, 512), lambda t: (0, jnp.minimum(t, 3))),
            pl.BlockSpec((N, 512), lambda t: (0, jnp.maximum(t - 4, 0))),
            pl.BlockSpec((D, 512), lambda t: (0, t)),
            full((N, 16)), full((16, D)), full((N, D)), full((1, D)), full((N, D)),
            full((SEQ, 24, 128)),
        ],
        out_specs=[full((N, D)), full((SEQ, 24, 128))],
        out_shape=[
            jax.ShapeDtypeStruct((N, D), BF16), jax.ShapeDtypeStruct((SEQ, 24, 128), F32),
        ],
        scratch_shapes=[pltpu.VMEM((N, D), F32)],
        compiler_params=params(),
        cost_estimate=cost(12),
        name="input_back",
    )(y, og, w, dlow, gd, tokens, gain, dmid, pack)


SWAP = [(i, i ^ 1) for i in range(8)]
FLIP = {0: 1, 1: 3}
XORDER = ((0, 1), (1, 0))
ORDERS = (((0, 1, 2, 3), (1, 0, 3, 2)), ((2, 3, 0, 1), (3, 2, 1, 0)))


def bit_of(seq, which):
    at = seq // 4 if which < 2 else seq % 4
    return at // 2 if which % 2 else int(at in (1, 2))


def chunk_of(order, bits):
    value = dict(zip(order, bits))
    along = [[0, 1, 3, 2][2 * value[2 * a + 1] + value[2 * a]] for a in range(2)]
    return along[0] * 4 + along[1]


def partner(seq, which):
    z, y = seq // 4, seq % 4
    return (z ^ FLIP[which]) * 4 + y if which < 2 else z * 4 + (y ^ FLIP[which - 2])


def tables():
    table = np.zeros((128, 96), np.int32)
    for device in range(128):
        core, seq = (device // 16) % 2, device % 16
        for v in range(2):
            order = ORDERS[v][core]
            chunks = [chunk_of(order, [(i >> 3) & 1, (i >> 2) & 1, (i >> 1) & 1, i & 1]) for i in range(16)]
            mine = [bit_of(seq, which) for which in order]
            table[device, v * 16 : v * 16 + 8] = chunks[mine[0] * 8 : mine[0] * 8 + 8]
            table[device, v * 16 + 8 : v * 16 + 16] = chunks[(1 - mine[0]) * 8 : (1 - mine[0]) * 8 + 8]
            table[device, 32 + v * 4 : 36 + v * 4] = mine
            for slot in range(16):
                table[device, 48 + v * 16 + chunks[slot ^ (8 * mine[0])]] = slot
        table[device, 40] = core
        table[device, 46] = seq
        x, (near, far) = device // 32, XORDER[core]
        for slab in range(4):
            away = bit_of(slab * 4, near) != bit_of(x * 4, near)
            table[device, 41 + slab] = bit_of(slab * 4, far) + 2 * away
        table[device, 45] = bit_of(x * 4, far)
        for who in range(2):
            near, far = XORDER[core ^ who]
            table[device, 80 + 4 * who : 84 + 4 * who] = [x, x ^ FLIP[far], x ^ FLIP[near], x ^ 2]
    return table


TABLE = tables()
STEPS = [
    [
        [(d, (d // 16) * 16 + partner(d % 16, ORDERS[v][(d // 16) % 2][step])) for d in range(128)]
        for step in range(4)
    ]
    for v in range(2)
]
ACROSS = [
    [(i, ((i // 2) ^ FLIP[XORDER[i % 2][step]]) * 2 + i % 2) for i in range(8)] for step in range(2)
]


def exchange(value):
    return lax.all_to_all(value, "seq", 0, 0, tiled=True)


def swap(value):
    return lax.ppermute(value, "dp", SWAP)


def halve_x_kernel(table_ref, k_ref, r_ref, send_ref):
    del table_ref
    send_ref[...] = k_ref[...] + r_ref[...]


def halve_x(table, keep, got):
    rows = keep.shape[1] // 2
    theirs = pl.BlockSpec((1, rows, 128), lambda j, t: (1 - t[45], j, 0))
    return pl.pallas_call(
        halve_x_kernel,
        grid_spec=pltpu.PrefetchScalarGridSpec(
            num_scalar_prefetch=1, grid=(2,), in_specs=[theirs, theirs],
            out_specs=pl.BlockSpec((1, rows, 128), lambda j, t: (0, j, 0)),
        ),
        out_shape=jax.ShapeDtypeStruct((1, 2 * rows, 128), F32),
        compiler_params=params(),
        cost_estimate=cost(0.1),
        name="halve_x",
    )(table, keep, got)


def halve_kernel(shapes, moves, table_ref, *refs):
    del table_ref
    ins = list(refs)
    at = 0
    values = []
    for groups, later in shapes:
        row, parts = 0, []
        rests = ins[at + 2 * groups : at + 2 * groups + later]
        for group in range(groups):
            k_ref, r_ref = ins[at + 2 * group : at + 2 * group + 2]
            parts.append((row, row + k_ref.shape[1], k_ref, r_ref))
            row += k_ref.shape[1]
        values.append((parts, rests))
        at += 2 * groups + later
    for v, first, count, out, place in moves:
        out_ref = ins[at + out]
        for low, high, k_ref, r_ref in values[v][0]:
            start, stop = max(first, low), min(first + count, high)
            if start >= stop:
                continue
            total = k_ref[:, start - low : stop - low] + r_ref[:, start - low : stop - low]
            for rest in values[v][1]:
                total = total + rest[:, start:stop]
            out_ref[:, place + start - first : place + stop - first] = total


def halve(table, step, streams, moves=None):
    size = 2 if step < 3 else 1
    turns = 2 if step == 1 else 1
    operands, specs, shapes, totals = [], [], [], []
    for v, (groups, later) in enumerate(streams):
        bit = lambda t, n, v=v: t[32 + v * 4 + n]

        def block(i, t, bit=bit):
            if step == 1:
                return (1 - bit(t, 1)) * 2 + i
            if step == 2:
                return bit(t, 1) * 2 + 1 - bit(t, 2)
            last = 1 - bit(t, 3) if step == 3 else bit(t, 3)
            return bit(t, 1) * 4 + bit(t, 2) * 2 + last

        total = 0
        for pair in groups:
            for array in pair:
                operands.append(array)
                specs.append(pl.BlockSpec((size, array.shape[1], 128), lambda i, t, f=block: (f(i, t), 0, 0)))
            total += pair[0].shape[1]
        for array in later:
            operands.append(array)
            count = array.shape[0] // size
            specs.append(
                pl.BlockSpec((size, total, 128), lambda i, t, f=block, c=count: (lax.rem(f(i, t), c), 0, 0))
            )
        shapes.append((len(groups), len(later)))
        totals.append(total)
    if moves is None:
        moves = [(v, 0, totals[v], v, 0) for v in range(2)]
        outs = [(size * turns, total) for total in totals]
    else:
        outs = [(1, sum(totals))]
    return pl.pallas_call(
        functools.partial(halve_kernel, shapes, moves),
        grid_spec=pltpu.PrefetchScalarGridSpec(
            num_scalar_prefetch=1, grid=(turns,), in_specs=specs,
            out_specs=[pl.BlockSpec((size, rows, 128), lambda i, t: (i, 0, 0)) for _, rows in outs],
        ),
        out_shape=[jax.ShapeDtypeStruct((count, rows, 128), F32) for count, rows in outs],
        compiler_params=params(),
        cost_estimate=cost(0.1),
        name="halve",
    )(table, *operands)


def hop(v, step, value):
    return lax.ppermute(value, ("dp", "seq"), STEPS[v][step])


def hops(step, sends):
    return [hop(v, step, sends[v]) for v in range(2)]


def along_x(step, value):
    return lax.ppermute(value, "dp", ACROSS[step])


def after(value, *others):
    return lax.optimization_barrier((value, *others))[0]


def unpack_kernel(
    table_ref, a_ref, a_other, b_ref, b_other,
    up_ref, down_ref, out_ref, in_ref, gd_ref, gu_ref, ng_ref, mg_ref, gb_ref, hg_ref,
):
    core = table_ref[40]

    def place(own_ref, other_ref, at, rows, slabs, target, first, second):
        for slab in range(slabs):
            own = own_ref[at : at + rows]
            other = other_ref[at : at + rows]
            low = jnp.where(core == 0, own, other)
            high = jnp.where(core == 0, other, own)
            target[:, first + slab * 128 : first + (slab + 1) * 128] = low
            target[:, second + slab * 128 : second + (slab + 1) * 128] = high
            at += rows
        return at

    for v in range(2):
        for tile in range(TILES):
            column = tile * TILE + v * 128
            place(a_ref, a_other, (v * TILES + tile) * 64, 64, 1, up_ref, column, FF + column)
    at = place(b_ref, b_other, 0, 64, 4, out_ref, 0, 512)
    at = place(b_ref, b_other, at, 64, 4, in_ref, 2048, 2560)
    at = place(b_ref, b_other, at, 64, 4, in_ref, 0, 1024)
    at = place(b_ref, b_other, at, 64, 4, in_ref, 512, 1536)
    small = b_ref[at : at + 24] + b_other[at : at + 24]
    gd_ref[...] = small[:16, :64]
    gu_ref[...] = small[:16, 64:96]
    ng_ref[...] = small[16:17, :64]
    mg_ref[...] = small[16:17, 64:128]
    gb_ref[...] = small[17:18, :32]
    hg_ref[...] = small[17:18, 32:48]
    for slab in range(4):
        first = at + 24 + slab * 176
        for ref, base, place_of in ((b_ref, core * 512, 80), (b_other, (1 - core) * 512, 84)):
            cols = pl.ds(pl.multiple_of(base + table_ref[place_of + slab] * 128, 128), 128)
            down_ref[:, cols] = ref[first : first + 176]


def unpack(table, a, a_other, b, b_other):
    shapes = [
        (64, 2 * FF), (176, D), (64, D), (64, 3072), (16, 64), (16, 32), (1, 64), (1, 64), (1, 32), (1, 16),
    ]
    return pl.pallas_call(
        unpack_kernel,
        in_specs=[pl.BlockSpec(memory_space=pltpu.SMEM)] + [pl.BlockSpec(memory_space=pltpu.VMEM)] * 4,
        out_specs=[pl.BlockSpec(memory_space=pltpu.VMEM)] * len(shapes),
        out_shape=[jax.ShapeDtypeStruct(shape, F32) for shape in shapes],
        compiler_params=params(),
        cost_estimate=cost(4),
        name="unpack",
    )(table, a, a_other, b, b_other)


def chunks(value):
    return value.reshape(SEQ, value.shape[0] // SEQ, value.shape[1])


def shards(
    tokens, lengths, cotangent, norm_gain, in_weight, gate_down, gate_up, gate_bias, head_gain,
    out_weight, mlp_gain, up_weight, down_weight,
):
    device = lax.axis_index("dp") * SEQ + lax.axis_index("seq")
    table = lax.dynamic_slice(jnp.asarray(TABLE), (device, 0), (1, 96)).reshape(96)
    tok = tokens.reshape(N, D)
    cot = cotangent.reshape(N, D)
    flat = lambda value: value.reshape(2, -1, 128)

    down_t, up_t = gate_down.T, gate_up.T
    vectors = jnp.concatenate([norm_gain, mlp_gain, gate_bias, head_gain]).reshape(1, -1)
    k, v, normed, ld, cl, logit, low, upd, pieces = project(
        lengths, table, tok, vectors, in_weight, down_t, up_t, vectors
    )
    gathered = exchange(pieces)
    q, og, normed_t, cot_send = project_rest(table, after(normed, pieces), in_weight, cot)
    incoming = prefix(after(gathered, q), gathered, False)
    normed_other, cot_other = swap(after(normed_t, incoming)), swap(after(cot_send, incoming))
    within = local(after(q, incoming), k, v, ld)
    d_hidden = hidden_grad(after(cot, within), down_weight)
    incoming = after(exchange(incoming), d_hidden).reshape(ROWS, HEADS, VHEAD, KHEAD)
    heads, middle, mlp_in, joint = attend(
        q, og, ld, within, cl, incoming, upd, tok, out_weight, vectors, vectors
    )
    output, dmlp, act, act_send, hidden_t = mlp(
        table, after(mlp_in, normed_other, cot_other), d_hidden, up_weight, down_weight, middle
    )
    hidden_other, act_other, joint_other = swap(hidden_t), swap(act_send), swap(joint)
    dmid, datt, g_mlp_gain, g_head_gain, dheads, dog, sends, adj, pieces_back = back(
        table, middle, dmlp, cot, vectors, out_weight, vectors, heads, og, q, ld, cl
    )
    sends_other = swap(sends)
    owned = exchange(pieces_back)
    dn_keep, dn_send = down_grad(table, after(hidden_t, pieces_back), hidden_other, cot, cot_other)
    dn_got = along_x(0, after(flat(dn_send), owned))
    owned = prefix(after(owned, dn_keep), gathered, True)
    returned = exchange(owned)
    up_0, up_send_0, up_1, up_send_1 = up_grad(
        table, after(joint, owned, sends_other), joint_other, act, act_other
    )
    up_gots = hops(0, (after(up_send_0, returned), after(up_send_1, returned)))
    keep_o, send_o, keep_g, send_g = outer(
        after(table, up_0),
        [
            (joint, joint_other, 1, datt, sends_other, 0, (0,)),
            (normed_t, normed_other, 0, dog, sends_other, 1, (1,)),
        ],
    )
    four_got = hops(0, (send_o, send_g))
    dn_first = dn_got
    dn_send = halve_x(table, after(flat(dn_keep), keep_o), dn_first)
    dn_got = along_x(1, dn_send)
    returned = after(returned, dn_send).reshape(ROWS, HEADS, VHEAD, KHEAD)
    dproj, dproj_send, dlow, pack = inner(
        lengths, table, q, k, v, dheads, ld, cl, incoming, returned, upd, adj, logit, low, up_t, normed,
        g_head_gain, g_mlp_gain,
    )
    input_grad, pack = input_back(
        dproj, dog, in_weight, dlow, down_t, tok, vectors, dmid, pack
    )
    dproj_got = swap(after(dproj_send, dn_got, pack, *up_gots, *four_got))
    up = [([(after(up_0, pack), up_gots[0])], []), ([(up_1, up_gots[1])], [])]
    up_sends = halve(table, 1, up)
    up_gots = hops(1, up_sends)
    keep_p, send_p, keep_r, send_r = outer(
        after(table, up_sends[0]),
        [(normed_t, normed_other, 0, dproj, dproj_got, 0, (0, 1))],
        (dn_keep, dn_first.reshape(dn_keep.shape), dn_got.reshape(SEQ, 176, 128), pack),
    )
    first = hops(0, (send_p, send_r))
    add = lambda streams, gots: [(groups, later + [got]) for (groups, later), got in zip(streams, gots)]
    up = add([([(after(up_0, keep_p), up[0][0][0][1])], []), up[1]], up_gots)
    up_sends = halve(table, 2, up)
    up_gots = hops(2, up_sends)
    rest = [
        ([(after(keep_o, up_sends[0]), four_got[0]), (keep_p, first[0])], []),
        ([(keep_g, four_got[1]), (keep_r, first[1])], []),
    ]
    sends = halve(table, 1, rest)
    gots = hops(1, sends)
    up = add(up, up_gots)
    up_sends = halve(after(table, sends[0]), 3, up)
    up_gots = hops(3, up_sends)
    rest = add(rest, gots)
    sends = halve(after(table, up_sends[0]), 2, rest)
    gots = hops(2, sends)
    (early,) = halve(table, 4, add(up, up_gots), [(0, 0, 704, 0, 0), (1, 0, 704, 0, 704)])
    early = early[0]
    early = early + along_x(0, early)
    rest = add(rest, gots)
    sends = halve(after(table, early), 3, rest)
    gots = hops(3, sends)
    early = early + along_x(1, early)
    (late,) = halve(
        after(table, early), 4, add(rest, gots),
        [
            (0, 0, 256, 0, 0), (1, 0, 256, 0, 256), (0, 256, 256, 0, 512), (1, 256, 256, 0, 768),
            (1, 600, 24, 0, 1024), (0, 512, 88, 0, 1048), (1, 512, 88, 0, 1136),
        ],
    )
    late = late[0]
    got = along_x(1, late)
    early_other = swap(early)
    late = jnp.concatenate([late[:1048] + got[:1048], late[1048:], got[1048:]], 0)
    got = along_x(0, late)
    late = jnp.concatenate([late[:1048] + got[:1048], late[1048:], got[1048:]], 0)
    grad_up, grad_down, grad_out, grad_in, g_down, g_upf, g_norm, g_mlp, g_bias, g_head = unpack(
        table, early, early_other, late, swap(late)
    )
    return (
        output.reshape(ROWS, SEG, D),
        input_grad.reshape(ROWS, SEG, D),
        g_norm.reshape(64),
        grad_in,
        g_down.T,
        g_upf.T,
        g_bias.reshape(32),
        g_head.reshape(16),
        grad_out,
        g_mlp.reshape(64),
        grad_up,
        grad_down,
    )


def solution(mesh):
    rows = P("dp", "seq", None)
    return jax.shard_map(
        shards,
        mesh=mesh,
        in_specs=(rows, P("dp"), rows) + (P(),) * 10,
        out_specs=(
            rows, rows, P("seq"), P("seq", None), P("seq", None), P("seq", None), P("seq"), P("seq"),
            P("seq", None), P("seq"), P("seq", None), P("seq", None),
        ),
        check_vma=False,
    )
```
